512 devices in a mesh: wide: 64 (over z, y), narrow: 8 (over x, core).
Axes of the slice: x: 4, y: 4, z: 16, core: 2. Of those that a mesh axis runs over, the one named last changes fastest.
Arguments:
- points: float32 [3, 2097152], P(None, ('wide', 'narrow'))
- charges: float32 [2097152], P(('wide', 'narrow')), may hold values from -1.5 to 1.5
- order: int32 [2097152], P(('wide', 'narrow')), may hold values from 0 to 4095, as said below
- source_basis: float32 [32, 2097152], P(None, ('wide', 'narrow')), may hold values from -0.375 to 0.375
- target_basis: float32 [32, 2097152], P(None, ('wide', 'narrow')), may hold values from -1 to 1
- skeleton_points: float32 [3, 262144], P(None, ('wide', 'narrow'))
- transfer: float32 [32, 262144], P(None, ('wide', 'narrow')), may hold values from -3 to 3
- top_points: float32 [3, 2048], P(None, 'wide')
- near_pairs: int32 [2, 32768], P(None, ('wide', 'narrow')), may hold values from 0 to 8191, as said below
- near_count: int32 [512], P(('wide', 'narrow')), may hold values from 16 to 64
- far_pairs: int32 [3, 65536], P(None, ('wide', 'narrow')), may hold values from 0 to 8191, as said below
- far_count: int32 [512], P(('wide', 'narrow')), may hold values from 64 to 128
Outputs:
- potential: float32 [2097152], P(('wide', 'narrow'))
The draws below stay inside these ranges and needn't reach their ends.
Inputs may be any that keep to these rules, and one draw needn't show every extreme that they name: `order`: within each device's block of 4096 slots, a permutation of 0 to 4095. `near_pairs`: clusters sit on a grid of cells, 8 wide and 16 deep in each group's layer: cluster c has cell (w % 8, w // 8, c // 128) with w = c % 128. Row 0 is a cluster of the device that holds the slot; row 1 is a cluster whose cell is at Chebyshev distance exactly 1 from the target's cell (so it lies in the target's group or the group just before or after it). Only the first near_count slots of a device are used. `far_pairs`: row 0 is a cluster of the device that holds the slot; row 2 is 0 or 1; with 0, row 1 is a cluster of the target's group or of the group just before or after it whose cell is at Chebyshev distance 2 or more from the target's cell; with 1, row 1 is a group two or more groups away from the target's. Only the first far_count slots of a device are used.
All inputs are finite; a program needn't handle non-finite values.
Results may differ from the reference program's by a relative error of at most 0.0003.
Values sent between devices are 32-bit elements; how exact they have to be, the bound alone decides.
No kernel may reach another device: no remote copies, remote signals or barrier semaphores. Data moves between devices by JAX's collectives and lax.ppermute only.
A program may use at most 64 MiB of HBM per device.

```python
import jax
import jax.numpy as jnp
import numpy as np
from jax import lax

C = 256
R = 32
CL_DEV = 16
NEAR_DEV = 64
FAR_DEV = 128
NCL = 8192
NP = 2097152
GROUP = 128
GROUPS = 64


def cell_of(cluster):
    width = min(8, GROUP)
    within = cluster % GROUP
    return (within % width, within // width, cluster // GROUP)


def centre_of(cluster):
    col_x, row_y, layer_z = cell_of(cluster)
    coords = jnp.stack([col_x, row_y, layer_z], axis=0)
    return 1.5 * coords.astype(jnp.float32)


def neighbour_table():
    rows = [[step_x, step_y, step_z] for step_z in (-1, 0, 1) for step_y in (-1, 0, 1) for step_x in (-1, 0, 1) if not (step_x == 0 and step_y == 0 and (step_z == 0))]
    return np.array(rows, dtype=np.int32)


def pick_valid(key, valid):
    columns = valid.shape[1]
    scores = jax.random.randint(key, valid.shape, 0, 2 ** 20) * 1024 + jnp.arange(columns, dtype=jnp.int32)[None, :]
    scores = jnp.where(valid, scores, -1)
    return lax.top_k(scores, 1)[1][:, 0].astype(jnp.int32)


def neighbour_source(key, target):
    width = min(8, GROUP)
    depth = GROUP // width
    col_x, row_y, layer_z = cell_of(target)
    table = jnp.asarray(neighbour_table())
    next_x = col_x[:, None] + table[None, :, 0]
    next_y = row_y[:, None] + table[None, :, 1]
    next_z = layer_z[:, None] + table[None, :, 2]
    valid = (next_x >= 0) & (next_x < width) & (next_y >= 0) & (next_y < depth) & (next_z >= 0) & (next_z < GROUPS)
    chosen = table[pick_valid(key, valid)]
    source = (layer_z + chosen[:, 2]) * GROUP + (row_y + chosen[:, 1]) * width + col_x + chosen[:, 0]
    return source.astype(jnp.int32)


def distant_source(key, target):
    width = min(8, GROUP)
    col_x, row_y, layer_z = cell_of(target)
    lowest = jnp.maximum(layer_z - 1, 0)
    highest_layer = jnp.minimum(layer_z + 1, GROUPS - 1)
    layer = lowest + jax.random.randint(jax.random.fold_in(key, 1), target.shape, 0, highest_layer - lowest + 1)
    within = jnp.arange(GROUP, dtype=jnp.int32)
    cand_x = within % width
    cand_y = within // width
    apart = jnp.maximum(jnp.abs(cand_x[None, :] - col_x[:, None]), jnp.abs(cand_y[None, :] - row_y[:, None]))
    place = pick_valid(jax.random.fold_in(key, 2), apart >= 2)
    return (layer * GROUP + place).astype(jnp.int32)


def panel_order(key):
    block_size = CL_DEV * C
    blocks = NCL // CL_DEV
    scores = jax.random.randint(jax.random.fold_in(key, 11), (blocks, block_size), 0, 2 ** 31 // block_size)
    scores = scores * block_size + jnp.arange(block_size, dtype=jnp.int32)[None, :]
    local = jnp.argsort(scores, axis=1).astype(jnp.int32)
    return local.reshape(-1).astype(jnp.int32)


def forced_counts(key, counts, highest_value, lowest_value):
    devices = counts.shape[0]
    first = jax.random.randint(jax.random.fold_in(key, 21), (), 0, devices)
    second = (first + 1 + jax.random.randint(jax.random.fold_in(key, 22), (), 0, devices - 1)) % devices
    return counts.at[first].set(highest_value).at[second].set(lowest_value).astype(jnp.int32)


def draw_order(key, part):
    return panel_order(key)


def draw_points(key, part):
    block_size = CL_DEV * C
    arrival = panel_order(key) + jnp.arange(NP, dtype=jnp.int32) // block_size * block_size
    key = jax.random.fold_in(key, 2)
    cluster = jnp.arange(NP, dtype=jnp.int32) // C
    coords = centre_of(cluster) + jax.random.uniform(key, (3, NP), jnp.float32, -0.5, 0.5)
    return jnp.zeros((3, NP), jnp.float32).at[:, arrival].set(coords)


def draw_skeleton_points(key, part):
    key = jax.random.fold_in(key, 3)
    cluster = jnp.arange(NCL * R, dtype=jnp.int32) // R
    return centre_of(cluster) + jax.random.uniform(key, (3, NCL * R), jnp.float32, -0.5, 0.5)


def draw_top_points(key, part):
    key = jax.random.fold_in(key, 4)
    width = min(8, GROUP)
    depth = GROUP // width
    group_index = jnp.arange(GROUPS * R, dtype=jnp.int32) // R
    unit = jax.random.uniform(key, (3, GROUPS * R), jnp.float32, 0.0, 1.0)
    coord_x = -0.5 + (1.5 * (width - 1) + 1.0) * unit[0]
    coord_y = -0.5 + (1.5 * (depth - 1) + 1.0) * unit[1]
    coord_z = 1.5 * group_index.astype(jnp.float32) - 0.5 + unit[2]
    return jnp.stack([coord_x, coord_y, coord_z], axis=0).astype(jnp.float32)


def draw_near_pairs(key, part):
    key = jax.random.fold_in(key, 5)
    slots = NEAR_DEV * (NCL // CL_DEV)
    device = jnp.arange(slots, dtype=jnp.int32) // NEAR_DEV
    target = device * CL_DEV + jax.random.randint(jax.random.fold_in(key, 1), (slots,), 0, CL_DEV)
    source = neighbour_source(jax.random.fold_in(key, 2), target)
    return jnp.stack([target, source]).astype(jnp.int32)


def draw_near_count(key, part):
    key = jax.random.fold_in(key, 6)
    devices = NCL // CL_DEV
    heavy = jax.random.randint(jax.random.fold_in(key, 1), (devices,), 0, 4) == 0
    light_count = jax.random.randint(jax.random.fold_in(key, 2), (devices,), NEAR_DEV // 4, NEAR_DEV // 2 + 1)
    heavy_count = jax.random.randint(jax.random.fold_in(key, 3), (devices,), 3 * NEAR_DEV // 4, NEAR_DEV + 1)
    counts = jnp.where(heavy, heavy_count, light_count)
    return forced_counts(key, counts, NEAR_DEV, NEAR_DEV // 4)


def draw_far_pairs(key, part):
    key = jax.random.fold_in(key, 7)
    slots = FAR_DEV * (NCL // CL_DEV)
    device = jnp.arange(slots, dtype=jnp.int32) // FAR_DEV
    target = device * CL_DEV + jax.random.randint(jax.random.fold_in(key, 1), (slots,), 0, CL_DEV)
    level = jax.random.randint(jax.random.fold_in(key, 2), (slots,), 0, 2)
    leaf = distant_source(jax.random.fold_in(key, 3), target)
    own_group = target // GROUP
    other = (own_group + 2 + jax.random.randint(jax.random.fold_in(key, 4), (slots,), 0, GROUPS - 3)) % GROUPS
    source = jnp.where(level == 0, leaf, other)
    return jnp.stack([target, source, level]).astype(jnp.int32)


def draw_far_count(key, part):
    key = jax.random.fold_in(key, 8)
    devices = NCL // CL_DEV
    counts = jax.random.randint(jax.random.fold_in(key, 1), (devices,), FAR_DEV // 2, FAR_DEV + 1)
    return forced_counts(key, counts, FAR_DEV, FAR_DEV // 2)


def block_scale(key, shape, pieces, smallest, largest):
    def one(dim, blocks):
        heights = jax.random.uniform(jax.random.fold_in(jax.random.fold_in(key, 6), dim), (blocks,), jnp.float32, smallest / len(pieces), largest / len(pieces))
        return jnp.repeat(jnp.exp(heights), shape[dim] // blocks).reshape((-1,) + (1,) * (len(shape) - dim - 1))

    factor_of = one(*pieces[0])
    for cut in pieces[1:]:
        factor_of = factor_of * one(*cut)
    return factor_of


def gaussian(key, dims, scale, bound, pieces=(), kind=jnp.bfloat16):
    entries = scale * jax.random.normal(key, dims, jnp.float32)
    if pieces:
        entries = entries * block_scale(key, dims, pieces, -0.22, 0.18)
    return jnp.clip(entries, -bound, bound).astype(kind)


def setup_inputs(seed: int = 0) -> dict:
    key_of = jax.random.split(jax.random.key(seed), 13)
    return {
        "points": draw_points(jax.random.fold_in(key_of[12], 71), 0),
        "charges": gaussian(key_of[1], (NP,), 0.25, 1.5, ((0, 512),), jnp.float32),
        "order": draw_order(jax.random.fold_in(key_of[12], 71), 0),
        "source_basis": gaussian(key_of[3], (R, NP), C ** -0.5, 0.375, ((1, 512),), jnp.float32),
        "target_basis": gaussian(key_of[4], (R, NP), R ** -0.5, 1.0, ((1, 512),), jnp.float32),
        "skeleton_points": draw_skeleton_points(jax.random.fold_in(key_of[12], 71), 0),
        "transfer": gaussian(key_of[6], (R, NCL * R), 0.5, 3.0, ((1, 512),), jnp.float32),
        "top_points": draw_top_points(jax.random.fold_in(key_of[12], 71), 0),
        "near_pairs": draw_near_pairs(jax.random.fold_in(key_of[12], 71), 0),
        "near_count": draw_near_count(jax.random.fold_in(key_of[12], 71), 0),
        "far_pairs": draw_far_pairs(jax.random.fold_in(key_of[12], 71), 0),
        "far_count": draw_far_count(jax.random.fold_in(key_of[12], 71), 0),
    }


soft_square = 0.01
kernel_scale = 0.07957747154594767
highest = lax.Precision.HIGHEST

def kernel_tile(target_xyz, source_xyz):
    offsets = target_xyz[..., :, :, None] - source_xyz[..., :, None, :]
    dist_sq = lax.optimization_barrier(jnp.sum(offsets * offsets, axis=-3))
    return kernel_scale * lax.rsqrt(dist_sq + soft_square)

def reference(points, charges, order, source_basis, target_basis, skeleton_points, transfer, top_points, near_pairs, near_count, far_pairs, far_count):
    device_total = NCL // CL_DEV
    block_size = CL_DEV * C
    arrival = (order + jnp.arange(NP, dtype=jnp.int32) // block_size * block_size).astype(jnp.int32)
    slot_xyz = points[:, arrival].reshape(3, NCL, C).transpose(1, 0, 2)
    slot_charge = charges[arrival].reshape(NCL, C)
    skel_xyz = skeleton_points.reshape(3, NCL, R).transpose(1, 0, 2)
    skel_charge = jnp.einsum('rci,ci->cr', source_basis.reshape(R, NCL, C), slot_charge, precision=highest)
    group_charge = jnp.einsum('acb,cb->ca', transfer.reshape(R, NCL, R), skel_charge, precision=highest)
    group_charge = group_charge.reshape(GROUPS, GROUP, R).sum(axis=1)
    top_xyz = top_points.reshape(3, GROUPS, R).transpose(1, 0, 2)
    target_rows = target_basis.reshape(R, NCL, C).transpose(1, 0, 2)

    def self_part(entry):
        block_xyz, block_charge = entry
        tiles = kernel_tile(block_xyz, block_xyz)
        return jnp.einsum('nij,nj->ni', tiles, block_charge, precision=highest)
    self_potential = lax.map(self_part, (slot_xyz.reshape(device_total, CL_DEV, 3, C), slot_charge.reshape(device_total, CL_DEV, C))).reshape(NCL, C)
    near_rows = near_pairs.reshape(2, device_total, NEAR_DEV).transpose(1, 0, 2)
    near_live = (jnp.arange(NEAR_DEV)[None, :] < near_count[:, None]).astype(jnp.float32)

    def near_step(sums, entry):
        pair, weight = entry
        target = pair[0]
        source = pair[1]
        tiles = kernel_tile(slot_xyz[target], slot_xyz[source])
        to_target = jnp.einsum('nij,nj->ni', tiles, slot_charge[source], precision=highest) * weight[:, None]
        to_source = jnp.einsum('nij,ni->nj', tiles, slot_charge[target], precision=highest) * weight[:, None]
        return (sums.at[target].add(to_target).at[source].add(to_source), None)
    near_potential, unused = lax.scan(near_step, jnp.zeros((NCL, C), jnp.float32), (near_rows, near_live))
    far_rows = far_pairs.reshape(3, device_total, FAR_DEV).transpose(1, 0, 2)
    far_live = (jnp.arange(FAR_DEV)[None, :] < far_count[:, None]).astype(jnp.float32)

    def far_step(sums, entry):
        triple, weight = entry
        target = triple[0]
        source = triple[1]
        is_leaf = triple[2] == 0
        leaf_index = jnp.clip(source, 0, NCL - 1)
        top_index = jnp.clip(source, 0, GROUPS - 1)
        source_xyz = jnp.where(is_leaf[:, None, None], skel_xyz[leaf_index], top_xyz[top_index])
        source_charge = jnp.where(is_leaf[:, None], skel_charge[leaf_index], group_charge[top_index])
        coupling = kernel_tile(skel_xyz[target], source_xyz)
        middle = jnp.einsum('nab,nb->na', coupling, source_charge, precision=highest) * weight[:, None]
        spread = jnp.einsum('nac,na->nc', target_rows[target], middle, precision=highest)
        return (sums.at[target].add(spread), None)
    far_potential, unused = lax.scan(far_step, jnp.zeros((NCL, C), jnp.float32), (far_rows, far_live))
    total = self_potential + near_potential + far_potential
    return jnp.zeros((NP,), jnp.float32).at[arrival].set(total.reshape(-1))
```

```python
import functools

import jax
import jax.numpy as jnp
from jax import lax
from jax.experimental import pallas as pl
from jax.experimental.pallas import tpu as pltpu
from jax.sharding import PartitionSpec as P

C = 256
R = 32
LANES = 128
CLUSTERS = 16
ROWS = 32
NARROW = 8
GROUP = 128
WIDTH = 8
STRIP_CLUSTERS = 32
PAIR_ROW = 8 * STRIP_CLUSTERS
SKEL_ROW = PAIR_ROW + 24
STRIP_ROWS = SKEL_ROW + GROUP
SKEL_REC = 24
WINDOW = 3 * STRIP_CLUSTERS
DUMMY = WINDOW
SELF = WINDOW + 1
DEPTH = 48
UNROLL = 2
CHUNK = 64

soft_square = 0.01
kernel_scale = 0.07957747154594767
f32 = jnp.float32
bf16 = jnp.bfloat16
i32 = jnp.int32


def iota(shape, dim):
    return lax.broadcasted_iota(i32, shape, dim)


def split3(x):
    high = x.astype(bf16)
    rest = x - high.astype(f32)
    mid = rest.astype(bf16)
    low = (rest - mid.astype(f32)).astype(bf16)
    return high, mid, low


def parts_dot(x, ones, dims):
    dots = [
        lax.dot_general(part, ones, (dims, ((), ())), preferred_element_type=f32)
        for part in split3(x)
    ]
    return dots[0] + dots[1] + dots[2]


def as_bf16(mask):
    return mask.astype(f32).astype(bf16)


def slots_kernel(
    near_count,
    points,
    charges,
    order,
    source_basis,
    transfer,
    skeleton_points,
    top_points,
    near_pairs,
    own,
    to_down,
    to_up,
    skel_out,
):
    low = order[...] & (LANES - 1)
    high = order[...] >> 7
    sub = iota((8, LANES), 0)
    tables = []
    for row in range(ROWS):
        xyz = points[:, row * LANES : (row + 1) * LANES]
        charge = charges[row : row + 1, :]
        tables.append(jnp.concatenate([xyz, charge, xyz, charge], axis=0))
    tiles = []
    for tile in range(CLUSTERS):
        first = 4 * (tile // 2) + tile % 2
        low_tile = jnp.where(sub < 4, low[first : first + 1], low[first + 2 : first + 3])
        high_tile = jnp.where(sub < 4, high[first : first + 1], high[first + 2 : first + 3])
        values = jnp.zeros((8, LANES), f32)
        for row in range(ROWS):
            found = jnp.take_along_axis(tables[row], low_tile, axis=1)
            values = jnp.where(high_tile == row, found, values)
        own[8 * tile : 8 * tile + 8, :] = values
        if tile < 8:
            to_down[8 * tile : 8 * tile + 8, :] = values
        else:
            to_up[8 * tile - 64 : 8 * tile - 56, :] = values
        tiles.append(values)

    pairs = jnp.where(iota((2, 64), 1) < near_count[0], near_pairs[...] + 1, 0).astype(f32)
    for ref, start in ((own, 128), (to_down, 64), (to_up, 64)):
        ref[start : start + 8, :] = jnp.zeros((8, LANES), f32)
        ref[start : start + 2, 0:64] = pairs

    lane = iota((R, LANES), 1)
    skel = jnp.zeros((R, LANES), f32)
    for cluster in range(CLUSTERS):
        block, place = cluster // 2, 4 * (cluster % 2) + 3
        basis = source_basis[:, cluster * C : (cluster + 1) * C]
        product = (
            basis[:, :LANES] * tiles[2 * block][place : place + 1]
            + basis[:, LANES:] * tiles[2 * block + 1][place : place + 1]
        )
        skel = jnp.where(lane == cluster, jnp.sum(product, axis=1, keepdims=True), skel)
    skel_rows = skel.T[:CLUSTERS, :]
    long_lane = iota((R, CLUSTERS * R), 1)
    repeat = as_bf16(long_lane % R == iota((R, CLUSTERS * R), 0))
    tiled = parts_dot(skel_rows, repeat, ((1,), (0,)))
    mine = iota((CLUSTERS, CLUSTERS * R), 1) // R == iota((CLUSTERS, CLUSTERS * R), 0)
    flat = jnp.sum(jnp.where(mine, tiled, 0.0), axis=0, keepdims=True)
    partial = jnp.sum(transfer[...] * flat, axis=1, keepdims=True)
    skel = jnp.where(lane == CLUSTERS, partial, skel)
    to_charge = as_bf16(lane == iota((R, LANES), 0) + 3 * R)
    record = parts_dot(skel.T[:SKEL_REC, :], to_charge, ((1,), (0,)))
    fold = as_bf16(iota((CLUSTERS * R, LANES), 1) % R == iota((CLUSTERS * R, LANES), 0) % R)
    short_lane = iota((CLUSTERS, LANES), 1) // R
    geometry = jnp.zeros((CLUSTERS, LANES), f32)
    for axis in range(3):
        masked = jnp.where(mine, skeleton_points[axis : axis + 1, :], 0.0)
        folded = parts_dot(masked, fold, ((1,), (0,)))
        geometry = jnp.where(short_lane == axis, folded, geometry)
    spread = as_bf16(lane % R == iota((R, LANES), 0))
    top = parts_dot(top_points[...], spread, ((1,), (0,)))
    top_mine = iota((3, LANES), 1) // R == iota((3, LANES), 0)
    top_row = jnp.sum(jnp.where(top_mine, top, 0.0), axis=0, keepdims=True)
    last = jnp.where(iota((8, LANES), 0) == 1, top_row, 0.0)
    record = record + jnp.concatenate([geometry, last], axis=0)
    for copy in range(NARROW):
        skel_out[copy] = record


def with_norms(halves, origin):
    out = []
    for half in halves:
        sub = iota((8, LANES), 0)
        shifted = jnp.where(sub < 3, half - origin, 0.0)
        norms = jnp.sum(shifted * shifted, axis=0, keepdims=True)
        out.append((shifted, norms))
    return out


def source_features(halves, origin):
    sub = iota((8, LANES), 0)
    columns = []
    for shifted, norms in with_norms(halves, origin):
        rows = jnp.where(sub < 3, shifted, jnp.where(sub == 4, norms, 0.0))
        rows = jnp.where(sub == 5, 1.0, rows)
        high, mid, low = [part.astype(f32) for part in split3(rows)]
        columns.append(jnp.concatenate([high, mid, high, mid, low, high], axis=0).astype(bf16))
    return jnp.concatenate(columns, axis=1)


def target_features(halves, origin):
    sub = iota((8, LANES), 0)
    columns = []
    for shifted, norms in with_norms(halves, origin):
        rows = jnp.where(sub < 3, -2.0 * shifted, jnp.where(sub == 5, norms + soft_square, 0.0))
        rows = jnp.where(sub == 4, 1.0, rows)
        high, mid, low = [part.astype(f32) for part in split3(rows)]
        stacked = jnp.concatenate([high, high, mid, mid, high, low], axis=0)
        columns.append(stacked.T.astype(bf16))
    return jnp.concatenate(columns, axis=0)


def near_kernel(
    place,
    before,
    strip,
    after,
    near,
    features,
    charge,
    lhs,
    entries_vmem,
    entries,
    semaphore,
    *sums,
):
    wide_index = place[0]
    narrow_index = place[1]
    sub = iota((8, LANES), 0)

    def cluster_halves(ref, block, odd):
        halves = []
        for half in range(2):
            tile = ref[pl.ds(pl.multiple_of(16 * block + 8 * half, 8), 8), :]
            halves.append(pltpu.roll(tile, 4, 0) if odd else tile)
        return halves

    def put_source(slot, halves, origin):
        features[slot] = source_features(halves, origin)
        for half in range(2):
            row = halves[half][3:4]
            charge[slot, :, half * LANES : (half + 1) * LANES] = jnp.broadcast_to(row, (8, LANES))

    base = (wide_index * GROUP + narrow_index * CLUSTERS + 1).astype(f32)
    targets, sources = [], []
    for ref in (before, strip, after):
        for block in range(3):
            start = PAIR_ROW + 8 * block
            targets.append(ref[start : start + 1, :])
            sources.append(ref[start : start + 1 + 1, :][1:2])
    nothing = jnp.zeros((6, LANES), f32)
    own_ids = jnp.concatenate(sources + [targets[4]] + [nothing], axis=0)
    other_ids = jnp.concatenate(targets + [sources[4]] + [nothing], axis=0)
    local = own_ids - base
    used = (local >= 0.0) & (local < CLUSTERS) & (own_ids > 0.0)
    count = used.astype(f32)
    upto = as_bf16(iota((LANES, LANES), 0) <= iota((LANES, LANES), 1))
    inclusive = jnp.dot(count.astype(bf16), upto, preferred_element_type=f32)
    totals = jnp.sum(count, axis=1, keepdims=True)
    row_of = iota((16, LANES), 0)
    offset = jnp.zeros((16, LANES), f32)
    for row in range(10):
        offset = jnp.where(row_of > row, offset + totals[row : row + 1], offset)
    spot = inclusive - count + offset
    other = other_ids - 1.0
    group = jnp.floor(other * (1.0 / GROUP))
    rest = other - GROUP * group
    depth = jnp.floor(rest * (1.0 / WIDTH))
    column = rest - WIDTH * depth
    group_step = group - (wide_index - 1).astype(f32)
    depth_step = depth - (2 * narrow_index - 1).astype(f32)
    window = group_step * STRIP_CLUSTERS + depth_step * WIDTH + column
    window = jnp.where(used, window, 0.0)
    local = jnp.where(used, local, 0.0)
    spot = jnp.where(used, spot, -1.0)
    spot_high = jnp.floor(spot * (1.0 / LANES))
    spot_low = spot - LANES * spot_high
    listed = jnp.zeros((16, LANES), f32)
    eight = iota((8, LANES), 0).astype(f32)
    tall = iota((LANES, LANES), 0).astype(f32)
    for row in range(10):
        here = eight == spot_high[row : row + 1]
        values = jnp.concatenate(
            [
                jnp.where(here, local[row : row + 1], 0.0),
                jnp.where(here, window[row : row + 1], 0.0),
            ],
            axis=0,
        ).astype(bf16)
        hot = as_bf16(tall == spot_low[row : row + 1])
        listed = listed + lax.dot_general(
            values, hot, (((1,), (1,)), ((), ())), preferred_element_type=f32
        )
    coded = listed[:8] * float(GROUP) + listed[8:]
    coded = jnp.where(eight == 7.0, jnp.sum(totals), coded)
    entries_vmem[...] = coded.astype(i32)
    copy = pltpu.make_async_copy(entries_vmem, entries, semaphore)
    copy.start()

    whole = jnp.zeros((8, LANES), f32)
    for block in range(8):
        for half in range(2):
            start = 64 + 16 * block + 8 * half
            whole = whole + strip[start : start + 8, :]
    mean = jnp.sum(whole, axis=1, keepdims=True) * (1.0 / (CLUSTERS * C))
    mean = jnp.broadcast_to(mean, (8, LANES))
    origin = jnp.where(sub < 3, mean + pltpu.roll(mean, 4, 0), 0.0)

    def own_block(block, carry):
        for odd in range(2):
            cluster = 2 * block + odd
            halves = cluster_halves(strip, block + 4, odd)
            lhs[cluster] = target_features(halves, origin)
            centre = jnp.sum(halves[0] + halves[1], axis=1, keepdims=True) * (1.0 / C)
            lhs[CLUSTERS + cluster] = target_features(halves, centre)
            put_source(SELF + cluster, halves, centre)
        return carry

    lax.fori_loop(0, CLUSTERS // 2, own_block, 0)

    def window_block(block, carry):
        for part, ref in enumerate((before, strip, after)):
            for odd in range(2):
                put_source(
                    part * STRIP_CLUSTERS + 2 * block + odd, cluster_halves(ref, block, odd), origin
                )
        return carry

    lax.fori_loop(0, STRIP_CLUSTERS // 2, window_block, 0)
    features[DUMMY] = jnp.zeros((DEPTH, C), bf16)
    charge[DUMMY] = jnp.zeros((8, C), f32)

    def interact(left, slot, first):
        rhs = features[slot]
        charge_low = charge[slot, 0:1, 0:LANES]
        charge_high = charge[slot, 0:1, LANES:C]
        for start in range(0, C, CHUNK):
            square = jnp.dot(
                lhs[left, start : start + CHUNK, :], rhs, preferred_element_type=f32
            )
            inverse = lax.rsqrt(jnp.maximum(square, soft_square))
            first(start, inverse[:, :LANES] * charge_low + inverse[:, LANES:] * charge_high)

    def self_step(step, carry):
        for turn in range(UNROLL):
            cluster = step * UNROLL + turn

            def store(start, value):
                for other_turn in range(UNROLL):
                    sums[other_turn][cluster, start : start + CHUNK, :] = (
                        value if other_turn == turn else jnp.zeros_like(value)
                    )

            interact(CLUSTERS + cluster, SELF + cluster, store)
        return carry

    lax.fori_loop(0, CLUSTERS // UNROLL, self_step, 0)
    copy.wait()
    pair_total = entries[7, 0]

    def pair_step(step, carry):
        for turn in range(UNROLL):
            index = step * UNROLL + turn
            code = entries[index >> 7, index & (LANES - 1)]
            live = index < pair_total
            cluster = jnp.where(live, code >> 7, 0)
            slot = jnp.where(live, code & (LANES - 1), DUMMY)

            def add(start, value):
                sums[turn][cluster, start : start + CHUNK, :] += value

            interact(cluster, slot, add)
        return carry

    lax.fori_loop(0, (pair_total + UNROLL - 1) // UNROLL, pair_step, 0)

    for cluster in range(CLUSTERS):
        for half in range(2):
            rows = slice(half * LANES, (half + 1) * LANES)
            total = sums[0][cluster, rows, :]
            for turn in range(1, UNROLL):
                total = total + sums[turn][cluster, rows, :]
            row = 2 * cluster + half
            near[row : row + 1, :] = kernel_scale * jnp.sum(total.T, axis=0, keepdims=True)


def far_kernel(
    place,
    far_count,
    before,
    strip,
    after,
    own_skel,
    top,
    far_pairs,
    near,
    order,
    target_basis,
    potential,
    total,
):
    wide_index = place[0]
    narrow_index = place[1]
    first = wide_index * GROUP + narrow_index * CLUSTERS
    target = far_pairs[0:1, :] - first
    source = far_pairs[1:2, :]
    is_leaf = far_pairs[2:3, :] == 0
    live = iota((1, LANES), 1) < far_count[0]
    index = jnp.where(is_leaf, source - (wide_index - 1) * GROUP, source + 3 * GROUP)
    skel = slice(SKEL_ROW, SKEL_ROW + GROUP)
    table = jnp.concatenate([before[skel, :], strip[skel, :], after[skel, :], top[...]], axis=0)
    chosen = as_bf16(iota((table.shape[0], LANES), 0) == index)
    over_rows = ((0,), (0,))
    sources = parts_dot(table, chosen, over_rows)
    own_chosen = as_bf16(iota((CLUSTERS, LANES), 0) == target)
    targets = parts_dot(own_skel[0, :CLUSTERS, :], own_chosen, over_rows)
    rows = []
    for a in range(R):
        square = soft_square
        for axis in range(3):
            offset = sources[axis * R : (axis + 1) * R] - targets[axis * R + a : axis * R + a + 1]
            square = square + offset * offset
        product = lax.rsqrt(square) * sources[3 * R :]
        rows.append(jnp.sum(product, axis=0, keepdims=True))
    middle = jnp.where(live, jnp.concatenate(rows, axis=0) * kernel_scale, 0.0)
    for cluster in range(CLUSTERS):
        column = jnp.sum(jnp.where(target == cluster, middle, 0.0), axis=1, keepdims=True)
        spread = jnp.sum(
            target_basis[:, cluster * C : (cluster + 1) * C] * column, axis=0, keepdims=True
        )
        for half in range(2):
            row = 2 * cluster + half
            total[row : row + 1, :] = (
                near[row : row + 1, :] + spread[:, half * LANES : (half + 1) * LANES]
            )
    low = order[...] & (LANES - 1)
    high = order[...] >> 7
    out = jnp.zeros((ROWS, LANES), f32)
    tall = iota((LANES, LANES), 0)
    wide = iota((ROWS, LANES), 0)
    for row in range(ROWS):
        here = wide == high[row : row + 1]
        value = jnp.where(here, total[row : row + 1, :], 0.0)
        out = out + parts_dot(value, as_bf16(tall == low[row : row + 1]), ((1,), (1,)))
    potential[...] = out


def smem():
    return pl.BlockSpec(memory_space=pltpu.SMEM)


def vmem():
    return pl.BlockSpec(memory_space=pltpu.VMEM)


params = pltpu.CompilerParams(vmem_limit_bytes=50 * 1024 * 1024)


def local(
    points,
    charges,
    order,
    source_basis,
    target_basis,
    skeleton_points,
    transfer,
    top_points,
    near_pairs,
    near_count,
    far_pairs,
    far_count,
):
    wide_size = lax.axis_size("wide")
    narrow_size = lax.axis_size("narrow")
    place = jnp.stack([lax.axis_index("wide"), lax.axis_index("narrow")]).astype(i32)
    order = order.reshape(ROWS, LANES)
    shape = jax.ShapeDtypeStruct
    with jax.named_scope("slots"):
        own, to_down, to_up, skel = pl.pallas_call(
            slots_kernel,
            out_shape=(
                shape((136, LANES), f32),
                shape((72, LANES), f32),
                shape((72, LANES), f32),
                shape((NARROW, SKEL_REC, LANES), f32),
            ),
            in_specs=[smem()] + [vmem()] * 8,
            out_specs=[vmem()] * 4,
            compiler_params=params,
        )(
            near_count,
            points,
            charges.reshape(ROWS, LANES),
            order,
            source_basis,
            transfer,
            skeleton_points,
            top_points,
            near_pairs,
        )
    upward = [(i, i + 1) for i in range(narrow_size - 1)]
    downward = [(i + 1, i) for i in range(narrow_size - 1)]
    from_down = lax.ppermute(to_up, "narrow", upward)
    from_up = lax.ppermute(to_down, "narrow", downward)
    skels = lax.all_to_all(skel, "narrow", 0, 0, tiled=True)
    message = jnp.sum(skels[:, CLUSTERS, :], axis=0) + skels[0, CLUSTERS + 1, :]
    tops = lax.all_to_all(
        jnp.broadcast_to(message[None, None, :], (wide_size, 1, LANES)), "wide", 0, 0, tiled=True
    )
    strip = jnp.concatenate(
        [
            from_down[:64],
            own[:128],
            from_up[:64],
            from_down[64:],
            own[128:],
            from_up[64:],
            skels[:, :CLUSTERS, :].reshape(GROUP, LANES),
        ],
        axis=0,
    )
    before = lax.ppermute(strip, "wide", [(i, i + 1) for i in range(wide_size - 1)])
    after = lax.ppermute(strip, "wide", [(i + 1, i) for i in range(wide_size - 1)])
    with jax.named_scope("near"):
        near = pl.pallas_call(
            near_kernel,
            out_shape=shape((ROWS, LANES), f32),
            in_specs=[smem()] + [vmem()] * 3,
            out_specs=vmem(),
            scratch_shapes=[
                pltpu.VMEM((SELF + CLUSTERS, DEPTH, C), bf16),
                pltpu.VMEM((SELF + CLUSTERS, 8, C), f32),
                pltpu.VMEM((2 * CLUSTERS, C, DEPTH), bf16),
                pltpu.VMEM((8, LANES), i32),
                pltpu.SMEM((8, LANES), i32),
                pltpu.SemaphoreType.DMA(()),
            ]
            + [pltpu.VMEM((CLUSTERS, C, LANES), f32)] * UNROLL,
            compiler_params=params,
        )(place, before, strip, after)
    with jax.named_scope("far"):
        potential = pl.pallas_call(
            far_kernel,
            out_shape=shape((ROWS, LANES), f32),
            in_specs=[smem(), smem()] + [vmem()] * 9,
            out_specs=vmem(),
            scratch_shapes=[pltpu.VMEM((ROWS, LANES), f32)],
            compiler_params=params,
        )(
            place,
            far_count,
            before,
            strip,
            after,
            skel,
            tops.reshape(wide_size, LANES),
            far_pairs,
            near,
            order,
            target_basis,
        )
    return potential.reshape(-1)


def solution(mesh):
    both = ("wide", "narrow")
    split = P(None, both)
    return jax.shard_map(
        local,
        mesh=mesh,
        in_specs=(
            split,
            P(both),
            P(both),
            split,
            split,
            split,
            split,
            P(None, "wide"),
            split,
            P(both),
            split,
            P(both),
        ),
        out_specs=P(both),
        check_vma=False,
    )
```

```python
import jax
import jax.numpy as jnp
from jax import lax
from jax.experimental import pallas as pl
from jax.experimental.pallas import tpu as pltpu
from jax.sharding import PartitionSpec as P

C = 256
R = 32
LANES = 128
CLUSTERS = 16
ROWS = 32
NARROW = 8
GROUP = 128
WIDTH = 8
STRIP_CLUSTERS = 32
PAIR_ROW = 8 * STRIP_CLUSTERS
SKEL_ROW = PAIR_ROW + 24
STRIP_ROWS = SKEL_ROW + GROUP
SKEL_REC = 24
MESSAGE_ROWS = 72 + SKEL_REC
WINDOW = 3 * STRIP_CLUSTERS
DUMMY = WINDOW
DEPTH = 48
UNROLL = 8
SUMS = 4
CHUNK = 64

soft_square = 0.01
kernel_scale = 0.07957747154594767
f32 = jnp.float32
bf16 = jnp.bfloat16
i32 = jnp.int32


def iota(shape, dim):
    return lax.broadcasted_iota(i32, shape, dim)


def split3(x):
    high = x.astype(bf16)
    rest = x - high.astype(f32)
    mid = rest.astype(bf16)
    low = (rest - mid.astype(f32)).astype(bf16)
    return high, mid, low


def parts_dot(x, ones, dims):
    dots = [
        lax.dot_general(part, ones, (dims, ((), ())), preferred_element_type=f32)
        for part in split3(x)
    ]
    return dots[0] + dots[1] + dots[2]


def as_bf16(mask):
    return mask.astype(f32).astype(bf16)


def slots_kernel(near_count, place, *refs):
    count = 8
    held = refs[count + 2 : 2 * count + 2]
    semaphores = refs[2 * count + 2]
    own, message = refs[count : count + 2]
    copies = [
        pltpu.make_async_copy(refs[i], held[i], semaphores.at[i]) for i in range(count)
    ]
    for copy in copies:
        copy.start()
    order, points, charges, near_pairs, source_basis, transfer, skeleton_points, top_points = held
    narrow_index = place[1]
    for copy in copies[:4]:
        copy.wait()
    low = order[...] & (LANES - 1)
    high = order[...] >> 7
    sub = iota((8, LANES), 0)
    tables = []
    for row in range(ROWS):
        xyz = points[:, row * LANES : (row + 1) * LANES]
        charge = charges[row : row + 1, :]
        tables.append(jnp.concatenate([xyz, charge, xyz, charge], axis=0))
    tiles = []
    for tile in range(CLUSTERS):
        first = 4 * (tile // 2) + tile % 2
        low_tile = jnp.where(sub < 4, low[first : first + 1], low[first + 2 : first + 3])
        high_tile = jnp.where(sub < 4, high[first : first + 1], high[first + 2 : first + 3])
        values = jnp.zeros((8, LANES), f32)
        for row in range(ROWS):
            found = jnp.take_along_axis(tables[row], low_tile, axis=1)
            values = jnp.where(high_tile == row, found, values)
        own[8 * tile : 8 * tile + 8, :] = values
        tiles.append(values)

    pairs = jnp.where(iota((2, 64), 1) < near_count[0], near_pairs[...] + 1, 0).astype(f32)
    own[128:136, :] = jnp.zeros((8, LANES), f32)
    own[128:130, 0:64] = pairs
    for copy in copies[4:]:
        copy.wait()

    lane = iota((R, LANES), 1)
    skel = jnp.zeros((R, LANES), f32)
    for cluster in range(CLUSTERS):
        block, place = cluster // 2, 4 * (cluster % 2) + 3
        basis = source_basis[:, cluster * C : (cluster + 1) * C]
        product = (
            basis[:, :LANES] * tiles[2 * block][place : place + 1]
            + basis[:, LANES:] * tiles[2 * block + 1][place : place + 1]
        )
        skel = jnp.where(lane == cluster, jnp.sum(product, axis=1, keepdims=True), skel)
    skel_rows = skel.T[:CLUSTERS, :]
    long_lane = iota((R, CLUSTERS * R), 1)
    repeat = as_bf16(long_lane % R == iota((R, CLUSTERS * R), 0))
    tiled = parts_dot(skel_rows, repeat, ((1,), (0,)))
    mine = iota((CLUSTERS, CLUSTERS * R), 1) // R == iota((CLUSTERS, CLUSTERS * R), 0)
    flat = jnp.sum(jnp.where(mine, tiled, 0.0), axis=0, keepdims=True)
    partial = jnp.sum(transfer[...] * flat, axis=1, keepdims=True)
    skel = jnp.where(lane == CLUSTERS, partial, skel)
    to_charge = as_bf16(lane == iota((R, LANES), 0) + 3 * R)
    record = parts_dot(skel.T[:SKEL_REC, :], to_charge, ((1,), (0,)))
    fold = as_bf16(iota((CLUSTERS * R, LANES), 1) % R == iota((CLUSTERS * R, LANES), 0) % R)
    short_lane = iota((CLUSTERS, LANES), 1) // R
    geometry = jnp.zeros((CLUSTERS, LANES), f32)
    for axis in range(3):
        masked = jnp.where(mine, skeleton_points[axis : axis + 1, :], 0.0)
        folded = parts_dot(masked, fold, ((1,), (0,)))
        geometry = jnp.where(short_lane == axis, folded, geometry)
    spread = as_bf16(lane % R == iota((R, LANES), 0))
    top = parts_dot(top_points[...], spread, ((1,), (0,)))
    top_mine = iota((3, LANES), 1) // R == iota((3, LANES), 0)
    top_row = jnp.sum(jnp.where(top_mine, top, 0.0), axis=0, keepdims=True)
    last = jnp.where(iota((8, LANES), 0) == 1, top_row, 0.0)
    record = record + jnp.concatenate([geometry, last], axis=0)
    pair_block = own[128:136, :]
    for device in range(NARROW):
        for tile in range(8):
            message[device, 8 * tile : 8 * tile + 8, :] = jnp.where(
                narrow_index < device, tiles[8 + tile], tiles[tile]
            )
        message[device, 64:72, :] = jnp.where(narrow_index == device, 0.0, pair_block)
        message[device, 72:, :] = record


def strip_kernel(place, received, own, strip, top_message):
    narrow_index = place[1]
    down = jnp.maximum(narrow_index - 1, 0)
    up = jnp.minimum(narrow_index + 1, NARROW - 1)
    strip[0:64, :] = received[down, 0:64, :]
    strip[64:192, :] = own[0:128, :]
    strip[192:256, :] = received[up, 0:64, :]
    strip[PAIR_ROW : PAIR_ROW + 8, :] = received[down, 64:72, :]
    strip[PAIR_ROW + 8 : PAIR_ROW + 16, :] = own[128:136, :]
    strip[PAIR_ROW + 16 : PAIR_ROW + 24, :] = received[up, 64:72, :]
    last = received[0, 88:96, :]
    row = last[0:1] + last[1:2]
    for device in range(NARROW):
        start = SKEL_ROW + device * CLUSTERS
        strip[start : start + CLUSTERS, :] = received[device, 72:88, :]
        if device > 0:
            row = row + received[device, 88:96, :][0:1]
    top_message[...] = jnp.broadcast_to(row, top_message.shape)


def with_norms(halves, origin):
    out = []
    for half in halves:
        sub = iota((8, LANES), 0)
        shifted = jnp.where(sub < 3, half - origin, 0.0)
        norms = jnp.sum(shifted * shifted, axis=0, keepdims=True)
        out.append((shifted, norms))
    return out


def source_features(halves, origin):
    sub = iota((8, LANES), 0)
    columns = []
    for shifted, norms in with_norms(halves, origin):
        rows = jnp.where(sub < 3, shifted, jnp.where(sub == 4, norms, 0.0))
        rows = jnp.where(sub == 5, 1.0, rows)
        high, mid, low = [part.astype(f32) for part in split3(rows)]
        columns.append(jnp.concatenate([high, mid, high, mid, low, high], axis=0).astype(bf16))
    return jnp.concatenate(columns, axis=1)


def target_features(halves, origin):
    sub = iota((8, LANES), 0)
    columns = []
    for shifted, norms in with_norms(halves, origin):
        rows = jnp.where(sub < 3, -2.0 * shifted, jnp.where(sub == 5, norms + soft_square, 0.0))
        rows = jnp.where(sub == 4, 1.0, rows)
        high, mid, low = [part.astype(f32) for part in split3(rows)]
        stacked = jnp.concatenate([high, high, mid, mid, high, low], axis=0)
        columns.append(stacked.T.astype(bf16))
    return jnp.concatenate(columns, axis=0)


def cluster_halves(ref, block, odd):
    halves = []
    for half in range(2):
        tile = ref[pl.ds(pl.multiple_of(16 * block + 8 * half, 8), 8), :]
        halves.append(pltpu.roll(tile, 4, 0) if odd else tile)
    return halves


def own_origin(ref, start):
    whole = jnp.zeros((8, LANES), f32)
    for tile in range(CLUSTERS):
        whole = whole + ref[start + 8 * tile : start + 8 * tile + 8, :]
    mean = jnp.sum(whole, axis=1, keepdims=True) * (1.0 / (CLUSTERS * C))
    mean = jnp.broadcast_to(mean, (8, LANES))
    return jnp.where(iota((8, LANES), 0) < 3, mean + pltpu.roll(mean, 4, 0), 0.0)


def weighted(left, right, charge_low, charge_high, store):
    for start in range(0, C, CHUNK):
        square = jnp.dot(left(start), right, preferred_element_type=f32)
        inverse = lax.rsqrt(jnp.maximum(square, soft_square))
        store(start, inverse[:, :LANES] * charge_low + inverse[:, LANES:] * charge_high)


def self_kernel(own, lhs, near, held):
    origin = own_origin(own, 0)

    def block_step(block, carry):
        for odd in range(2):
            halves = cluster_halves(own, block, odd)
            lhs[2 * block + odd] = target_features(halves, origin)
            centre = jnp.sum(halves[0] + halves[1], axis=1, keepdims=True) * (1.0 / C)
            left = target_features(halves, centre)

            def store(start, value):
                held[odd, start : start + CHUNK, :] = value

            weighted(
                lambda start: left[start : start + CHUNK],
                source_features(halves, centre),
                halves[0][3:4],
                halves[1][3:4],
                store,
            )
            for half in range(2):
                part = held[odd, half * LANES : (half + 1) * LANES, :]
                near[pl.ds(2 * (2 * block + odd) + half, 1), :] = kernel_scale * jnp.sum(
                    part.T, axis=0, keepdims=True
                )
        return carry

    lax.fori_loop(0, CLUSTERS // 2, block_step, 0)


def near_kernel(
    place,
    before,
    strip,
    after,
    lhs,
    self_rows,
    near,
    features,
    charge,
    entries_vmem,
    entries,
    semaphore,
    *sums,
):
    wide_index = place[0]
    narrow_index = place[1]

    def put_source(slot, halves, origin):
        features[slot] = source_features(halves, origin)
        for half in range(2):
            row = halves[half][3:4]
            charge[slot, :, half * LANES : (half + 1) * LANES] = jnp.broadcast_to(row, (8, LANES))

    base = (wide_index * GROUP + narrow_index * CLUSTERS + 1).astype(f32)
    targets, sources = [], []
    for ref in (before, strip, after):
        for block in range(3):
            start = PAIR_ROW + 8 * block
            targets.append(ref[start : start + 1, :])
            sources.append(ref[start : start + 1 + 1, :][1:2])
    nothing = jnp.zeros((6, LANES), f32)
    own_ids = jnp.concatenate(sources + [targets[4]] + [nothing], axis=0)
    other_ids = jnp.concatenate(targets + [sources[4]] + [nothing], axis=0)
    local = own_ids - base
    used = (local >= 0.0) & (local < CLUSTERS) & (own_ids > 0.0)
    count = used.astype(f32)
    upto = as_bf16(iota((LANES, LANES), 0) <= iota((LANES, LANES), 1))
    inclusive = jnp.dot(count.astype(bf16), upto, preferred_element_type=f32)
    totals = jnp.sum(count, axis=1, keepdims=True)
    row_of = iota((16, LANES), 0)
    offset = jnp.zeros((16, LANES), f32)
    for row in range(10):
        offset = jnp.where(row_of > row, offset + totals[row : row + 1], offset)
    spot = inclusive - count + offset
    other = other_ids - 1.0
    group = jnp.floor(other * (1.0 / GROUP))
    rest = other - GROUP * group
    depth = jnp.floor(rest * (1.0 / WIDTH))
    column = rest - WIDTH * depth
    group_step = group - (wide_index - 1).astype(f32)
    depth_step = depth - (2 * narrow_index - 1).astype(f32)
    window = group_step * STRIP_CLUSTERS + depth_step * WIDTH + column
    window = jnp.where(used, window, 0.0)
    local = jnp.where(used, local, 0.0)
    spot = jnp.where(used, spot, -1.0)
    spot_high = jnp.floor(spot * (1.0 / LANES))
    spot_low = spot - LANES * spot_high
    listed = jnp.zeros((16, LANES), f32)
    eight = iota((8, LANES), 0).astype(f32)
    tall = iota((LANES, LANES), 0).astype(f32)
    for row in range(10):
        here = eight == spot_high[row : row + 1]
        values = jnp.concatenate(
            [
                jnp.where(here, local[row : row + 1], 0.0),
                jnp.where(here, window[row : row + 1], 0.0),
            ],
            axis=0,
        ).astype(bf16)
        hot = as_bf16(tall == spot_low[row : row + 1])
        listed = listed + lax.dot_general(
            values, hot, (((1,), (1,)), ((), ())), preferred_element_type=f32
        )
    coded = listed[:8] * float(GROUP) + listed[8:]
    coded = jnp.where(eight == 7.0, jnp.sum(totals), coded)
    entries_vmem[...] = coded.astype(i32)
    copy = pltpu.make_async_copy(entries_vmem, entries, semaphore)
    copy.start()

    for total in sums:
        total[...] = jnp.zeros(total.shape, f32)
    origin = own_origin(strip, 64)

    def window_block(block, carry):
        for part, ref in enumerate((before, strip, after)):
            for odd in range(2):
                put_source(
                    part * STRIP_CLUSTERS + 2 * block + odd, cluster_halves(ref, block, odd), origin
                )
        return carry

    lax.fori_loop(0, STRIP_CLUSTERS // 2, window_block, 0)
    features[DUMMY] = jnp.zeros((DEPTH, C), bf16)
    charge[DUMMY] = jnp.zeros((8, C), f32)

    copy.wait()
    pair_total = entries[7, 0]

    def pair_step(step, carry):
        for turn in range(UNROLL):
            index = step * UNROLL + turn
            code = entries[index >> 7, index & (LANES - 1)]
            live = index < pair_total
            cluster = jnp.where(live, code >> 7, 0)
            slot = jnp.where(live, code & (LANES - 1), DUMMY)

            def add(start, value):
                sums[turn % SUMS][cluster, start : start + CHUNK, :] += value

            weighted(
                lambda start: lhs[cluster, start : start + CHUNK, :],
                features[slot],
                charge[slot, 0:1, 0:LANES],
                charge[slot, 0:1, LANES:C],
                add,
            )
        return carry

    lax.fori_loop(0, (pair_total + UNROLL - 1) // UNROLL, pair_step, 0)

    for cluster in range(CLUSTERS):
        for half in range(2):
            rows = slice(half * LANES, (half + 1) * LANES)
            total = sums[0][cluster, rows, :]
            for turn in range(1, SUMS):
                total = total + sums[turn][cluster, rows, :]
            row = 2 * cluster + half
            near[row : row + 1, :] = self_rows[row : row + 1, :] + kernel_scale * jnp.sum(
                total.T, axis=0, keepdims=True
            )


def far_kernel(
    place,
    far_count,
    before,
    strip,
    after,
    top,
    far_pairs,
    near,
    order_in,
    target_basis_in,
    potential,
    total,
    order,
    target_basis,
    semaphores,
):
    order_copy = pltpu.make_async_copy(order_in, order, semaphores.at[0])
    basis_copy = pltpu.make_async_copy(target_basis_in, target_basis, semaphores.at[1])
    order_copy.start()
    basis_copy.start()
    wide_index = place[0]
    narrow_index = place[1]
    first = wide_index * GROUP + narrow_index * CLUSTERS
    target = far_pairs[0:1, :] - first
    source = far_pairs[1:2, :]
    is_leaf = far_pairs[2:3, :] == 0
    live = iota((1, LANES), 1) < far_count[0]
    index = jnp.where(is_leaf, source - (wide_index - 1) * GROUP, source + 3 * GROUP)
    skel = slice(SKEL_ROW, SKEL_ROW + GROUP)
    table = jnp.concatenate([before[skel, :], strip[skel, :], after[skel, :], top[...]], axis=0)
    chosen = as_bf16(iota((table.shape[0], LANES), 0) == index)
    over_rows = ((0,), (0,))
    sources = parts_dot(table, chosen, over_rows)
    own_start = pl.multiple_of(SKEL_ROW + narrow_index * CLUSTERS, 8)
    own_skel = strip[pl.ds(own_start, CLUSTERS), :]
    own_chosen = as_bf16(iota((CLUSTERS, LANES), 0) == target)
    targets = parts_dot(own_skel, own_chosen, over_rows)
    rows = []
    for a in range(R):
        square = soft_square
        for axis in range(3):
            offset = sources[axis * R : (axis + 1) * R] - targets[axis * R + a : axis * R + a + 1]
            square = square + offset * offset
        product = lax.rsqrt(square) * sources[3 * R :]
        rows.append(jnp.sum(product, axis=0, keepdims=True))
    middle = jnp.where(live, jnp.concatenate(rows, axis=0) * kernel_scale, 0.0)
    basis_copy.wait()
    for cluster in range(CLUSTERS):
        column = jnp.sum(jnp.where(target == cluster, middle, 0.0), axis=1, keepdims=True)
        spread = jnp.sum(
            target_basis[:, cluster * C : (cluster + 1) * C] * column, axis=0, keepdims=True
        )
        for half in range(2):
            row = 2 * cluster + half
            total[row : row + 1, :] = (
                near[row : row + 1, :] + spread[:, half * LANES : (half + 1) * LANES]
            )
    order_copy.wait()
    low = order[...] & (LANES - 1)
    high = order[...] >> 7
    out = jnp.zeros((ROWS, LANES), f32)
    tall = iota((LANES, LANES), 0)
    wide = iota((ROWS, LANES), 0)
    for row in range(ROWS):
        here = wide == high[row : row + 1]
        value = jnp.where(here, total[row : row + 1, :], 0.0)
        out = out + parts_dot(value, as_bf16(tall == low[row : row + 1]), ((1,), (1,)))
    potential[...] = out


def smem():
    return pl.BlockSpec(memory_space=pltpu.SMEM)


def anywhere():
    return pl.BlockSpec(memory_space=pl.ANY)


def vmem():
    return pl.BlockSpec(memory_space=pltpu.VMEM)


params = pltpu.CompilerParams(vmem_limit_bytes=50 * 1024 * 1024)


def local(
    points,
    charges,
    order,
    source_basis,
    target_basis,
    skeleton_points,
    transfer,
    top_points,
    near_pairs,
    near_count,
    far_pairs,
    far_count,
):
    wide_size = lax.axis_size("wide")
    place = jnp.stack([lax.axis_index("wide"), lax.axis_index("narrow")]).astype(i32)
    order = order.reshape(ROWS, LANES)
    shape = jax.ShapeDtypeStruct
    inputs = (
        order,
        points,
        charges.reshape(ROWS, LANES),
        near_pairs,
        source_basis,
        transfer,
        skeleton_points,
        top_points,
    )
    with jax.named_scope("slots"):
        own, message = pl.pallas_call(
            slots_kernel,
            out_shape=(
                shape((136, LANES), f32),
                shape((NARROW, MESSAGE_ROWS, LANES), f32),
            ),
            in_specs=[smem(), smem()] + [anywhere()] * len(inputs),
            out_specs=[vmem()] * 2,
            scratch_shapes=[pltpu.VMEM(x.shape, x.dtype) for x in inputs]
            + [pltpu.SemaphoreType.DMA((len(inputs),))],
            compiler_params=params,
        )(near_count, place, *inputs)
    received = lax.all_to_all(message, "narrow", 0, 0, tiled=True)
    with jax.named_scope("self"):
        lhs, self_rows = pl.pallas_call(
            self_kernel,
            out_shape=(shape((CLUSTERS, C, DEPTH), bf16), shape((ROWS, LANES), f32)),
            in_specs=[vmem()],
            out_specs=[vmem()] * 2,
            scratch_shapes=[pltpu.VMEM((2, C, LANES), f32)],
            compiler_params=params,
        )(own)
    with jax.named_scope("strip"):
        strip, top_message = pl.pallas_call(
            strip_kernel,
            out_shape=(shape((STRIP_ROWS, LANES), f32), shape((wide_size, LANES), f32)),
            in_specs=[smem()] + [vmem()] * 2,
            out_specs=[vmem()] * 2,
            compiler_params=params,
        )(place, received, own)
    before = lax.ppermute(strip, "wide", [(i, i + 1) for i in range(wide_size - 1)])
    after = lax.ppermute(strip, "wide", [(i + 1, i) for i in range(wide_size - 1)])
    tops = lax.all_to_all(top_message, "wide", 0, 0, tiled=True)
    with jax.named_scope("near"):
        near = pl.pallas_call(
            near_kernel,
            out_shape=shape((ROWS, LANES), f32),
            in_specs=[smem()] + [vmem()] * 5,
            out_specs=vmem(),
            scratch_shapes=[
                pltpu.VMEM((WINDOW + 1, DEPTH, C), bf16),
                pltpu.VMEM((WINDOW + 1, 8, C), f32),
                pltpu.VMEM((8, LANES), i32),
                pltpu.SMEM((8, LANES), i32),
                pltpu.SemaphoreType.DMA(()),
            ]
            + [pltpu.VMEM((CLUSTERS, C, LANES), f32)] * SUMS,
            compiler_params=params,
        )(place, before, strip, after, lhs, self_rows)
    with jax.named_scope("far"):
        potential = pl.pallas_call(
            far_kernel,
            out_shape=shape((ROWS, LANES), f32),
            in_specs=[smem(), smem()] + [vmem()] * 6 + [anywhere()] * 2,
            out_specs=vmem(),
            scratch_shapes=[
                pltpu.VMEM((ROWS, LANES), f32),
                pltpu.VMEM((ROWS, LANES), i32),
                pltpu.VMEM(target_basis.shape, f32),
                pltpu.SemaphoreType.DMA((2,)),
            ],
            compiler_params=params,
        )(place, far_count, before, strip, after, tops, far_pairs, near, order, target_basis)
    return potential.reshape(-1)


def solution(mesh):
    both = ("wide", "narrow")
    split = P(None, both)
    return jax.shard_map(
        local,
        mesh=mesh,
        in_specs=(
            split,
            P(both),
            P(both),
            split,
            split,
            split,
            split,
            P(None, "wide"),
            split,
            P(both),
            split,
            P(both),
        ),
        out_specs=P(both),
        check_vma=False,
    )
```

```python
import jax
import jax.numpy as jnp
from jax import lax
from jax.experimental import pallas as pl
from jax.experimental.pallas import tpu as pltpu
from jax.sharding import PartitionSpec as P

C = 256
R = 32
LANES = 128
CLUSTERS = 16
ROWS = 32
NARROW = 8
GROUP = 128
WIDTH = 8
STRIP_CLUSTERS = 32
PAIR_ROW = 8 * STRIP_CLUSTERS
SKEL_ROW = PAIR_ROW + 24
STRIP_ROWS = SKEL_ROW + GROUP
SKEL_REC = 24
MESSAGE_ROWS = 72 + SKEL_REC
WINDOW = 3 * STRIP_CLUSTERS
DUMMY = WINDOW
DEPTH = 48
UNROLL = 8
SUMS = 4
CHUNK = 64

soft_square = 0.01
kernel_scale = 0.07957747154594767
f32 = jnp.float32
bf16 = jnp.bfloat16
i32 = jnp.int32


def iota(shape, dim):
    return lax.broadcasted_iota(i32, shape, dim)


def split3(x):
    high = x.astype(bf16)
    rest = x - high.astype(f32)
    mid = rest.astype(bf16)
    low = (rest - mid.astype(f32)).astype(bf16)
    return high, mid, low


def parts_dot(x, ones, dims):
    dots = [
        lax.dot_general(part, ones, (dims, ((), ())), preferred_element_type=f32)
        for part in split3(x)
    ]
    return dots[0] + dots[1] + dots[2]


def as_bf16(mask):
    return mask.astype(f32).astype(bf16)


def slots_kernel(near_count, place, *refs):
    count = 8
    held = refs[count + 2 : 2 * count + 2]
    semaphores = refs[2 * count + 2]
    own, message = refs[count : count + 2]
    copies = [
        pltpu.make_async_copy(refs[i], held[i], semaphores.at[i]) for i in range(count)
    ]
    for copy in copies:
        copy.start()
    order, points, charges, near_pairs, source_basis, transfer, skeleton_points, top_points = held
    narrow_index = place[1]
    for copy in copies[:4]:
        copy.wait()
    low = order[...] & (LANES - 1)
    high = order[...] >> 7
    sub = iota((8, LANES), 0)
    tables = []
    for row in range(ROWS):
        xyz = points[:, row * LANES : (row + 1) * LANES]
        charge = charges[row : row + 1, :]
        tables.append(jnp.concatenate([xyz, charge, xyz, charge], axis=0))
    tiles = []
    for tile in range(CLUSTERS):
        first = 4 * (tile // 2) + tile % 2
        low_tile = jnp.where(sub < 4, low[first : first + 1], low[first + 2 : first + 3])
        high_tile = jnp.where(sub < 4, high[first : first + 1], high[first + 2 : first + 3])
        values = jnp.zeros((8, LANES), f32)
        for row in range(ROWS):
            found = jnp.take_along_axis(tables[row], low_tile, axis=1)
            values = jnp.where(high_tile == row, found, values)
        own[8 * tile : 8 * tile + 8, :] = values
        tiles.append(values)

    pairs = jnp.where(iota((2, 64), 1) < near_count[0], near_pairs[...] + 1, 0).astype(f32)
    own[128:136, :] = jnp.zeros((8, LANES), f32)
    own[128:130, 0:64] = pairs
    for copy in copies[4:]:
        copy.wait()

    lane = iota((R, LANES), 1)
    skel = jnp.zeros((R, LANES), f32)
    for cluster in range(CLUSTERS):
        block, place = cluster // 2, 4 * (cluster % 2) + 3
        basis = source_basis[:, cluster * C : (cluster + 1) * C]
        product = (
            basis[:, :LANES] * tiles[2 * block][place : place + 1]
            + basis[:, LANES:] * tiles[2 * block + 1][place : place + 1]
        )
        skel = jnp.where(lane == cluster, jnp.sum(product, axis=1, keepdims=True), skel)
    skel_rows = skel.T[:CLUSTERS, :]
    long_lane = iota((R, CLUSTERS * R), 1)
    repeat = as_bf16(long_lane % R == iota((R, CLUSTERS * R), 0))
    tiled = parts_dot(skel_rows, repeat, ((1,), (0,)))
    mine = iota((CLUSTERS, CLUSTERS * R), 1) // R == iota((CLUSTERS, CLUSTERS * R), 0)
    flat = jnp.sum(jnp.where(mine, tiled, 0.0), axis=0, keepdims=True)
    partial = jnp.sum(transfer[...] * flat, axis=1, keepdims=True)
    skel = jnp.where(lane == CLUSTERS, partial, skel)
    to_charge = as_bf16(lane == iota((R, LANES), 0) + 3 * R)
    record = parts_dot(skel.T[:SKEL_REC, :], to_charge, ((1,), (0,)))
    fold = as_bf16(iota((CLUSTERS * R, LANES), 1) % R == iota((CLUSTERS * R, LANES), 0) % R)
    short_lane = iota((CLUSTERS, LANES), 1) // R
    geometry = jnp.zeros((CLUSTERS, LANES), f32)
    for axis in range(3):
        masked = jnp.where(mine, skeleton_points[axis : axis + 1, :], 0.0)
        folded = parts_dot(masked, fold, ((1,), (0,)))
        geometry = jnp.where(short_lane == axis, folded, geometry)
    spread = as_bf16(lane % R == iota((R, LANES), 0))
    top = parts_dot(top_points[...], spread, ((1,), (0,)))
    top_mine = iota((3, LANES), 1) // R == iota((3, LANES), 0)
    top_row = jnp.sum(jnp.where(top_mine, top, 0.0), axis=0, keepdims=True)
    last = jnp.where(iota((8, LANES), 0) == 1, top_row, 0.0)
    record = record + jnp.concatenate([geometry, last], axis=0)
    pair_block = own[128:136, :]
    for device in range(NARROW):
        for tile in range(8):
            message[device, 8 * tile : 8 * tile + 8, :] = jnp.where(
                narrow_index < device, tiles[8 + tile], tiles[tile]
            )
        message[device, 64:72, :] = jnp.where(narrow_index == device, 0.0, pair_block)
        message[device, 72:, :] = record


def strip_kernel(place, received, own, self_rows, strip, top_message):
    del self_rows
    narrow_index = place[1]
    down = jnp.maximum(narrow_index - 1, 0)
    up = jnp.minimum(narrow_index + 1, NARROW - 1)
    strip[0:64, :] = received[down, 0:64, :]
    strip[64:192, :] = own[0:128, :]
    strip[192:256, :] = received[up, 0:64, :]
    strip[PAIR_ROW : PAIR_ROW + 8, :] = received[down, 64:72, :]
    strip[PAIR_ROW + 8 : PAIR_ROW + 16, :] = own[128:136, :]
    strip[PAIR_ROW + 16 : PAIR_ROW + 24, :] = received[up, 64:72, :]
    last = received[0, 88:96, :]
    row = last[0:1] + last[1:2]
    for device in range(NARROW):
        start = SKEL_ROW + device * CLUSTERS
        strip[start : start + CLUSTERS, :] = received[device, 72:88, :]
        if device > 0:
            row = row + received[device, 88:96, :][0:1]
    top_message[...] = jnp.broadcast_to(row, top_message.shape)


def with_norms(halves, origin):
    out = []
    for half in halves:
        sub = iota((8, LANES), 0)
        shifted = jnp.where(sub < 3, half - origin, 0.0)
        norms = jnp.sum(shifted * shifted, axis=0, keepdims=True)
        out.append((shifted, norms))
    return out


def source_features(halves, origin):
    sub = iota((8, LANES), 0)
    columns = []
    for shifted, norms in with_norms(halves, origin):
        rows = jnp.where(sub < 3, shifted, jnp.where(sub == 4, norms, 0.0))
        rows = jnp.where(sub == 5, 1.0, rows)
        high, mid, low = [part.astype(f32) for part in split3(rows)]
        columns.append(jnp.concatenate([high, mid, high, mid, low, high], axis=0).astype(bf16))
    return jnp.concatenate(columns, axis=1)


def target_features(halves, origin):
    sub = iota((8, LANES), 0)
    columns = []
    for shifted, norms in with_norms(halves, origin):
        rows = jnp.where(sub < 3, -2.0 * shifted, jnp.where(sub == 5, norms + soft_square, 0.0))
        rows = jnp.where(sub == 4, 1.0, rows)
        high, mid, low = [part.astype(f32) for part in split3(rows)]
        stacked = jnp.concatenate([high, high, mid, mid, high, low], axis=0)
        columns.append(stacked.T.astype(bf16))
    return jnp.concatenate(columns, axis=0)


def cluster_halves(ref, block, odd):
    halves = []
    for half in range(2):
        tile = ref[pl.ds(pl.multiple_of(16 * block + 8 * half, 8), 8), :]
        halves.append(pltpu.roll(tile, 4, 0) if odd else tile)
    return halves


def own_origin(ref, start):
    whole = jnp.zeros((8, LANES), f32)
    for tile in range(CLUSTERS):
        whole = whole + ref[start + 8 * tile : start + 8 * tile + 8, :]
    mean = jnp.sum(whole, axis=1, keepdims=True) * (1.0 / (CLUSTERS * C))
    mean = jnp.broadcast_to(mean, (8, LANES))
    return jnp.where(iota((8, LANES), 0) < 3, mean + pltpu.roll(mean, 4, 0), 0.0)


def weighted(left, right, charge_low, charge_high, store):
    for start in range(0, C, CHUNK):
        square = jnp.dot(left(start), right, preferred_element_type=f32)
        inverse = lax.rsqrt(jnp.maximum(square, soft_square))
        store(start, inverse[:, :LANES] * charge_low + inverse[:, LANES:] * charge_high)


def self_kernel(own, lhs, near, held):
    origin = own_origin(own, 0)

    def block_step(block, carry):
        for odd in range(2):
            halves = cluster_halves(own, block, odd)
            lhs[2 * block + odd] = target_features(halves, origin)
            centre = jnp.sum(halves[0] + halves[1], axis=1, keepdims=True) * (1.0 / C)
            left = target_features(halves, centre)

            def store(start, value):
                held[odd, start : start + CHUNK, :] = value

            weighted(
                lambda start: left[start : start + CHUNK],
                source_features(halves, centre),
                halves[0][3:4],
                halves[1][3:4],
                store,
            )
            for half in range(2):
                part = held[odd, half * LANES : (half + 1) * LANES, :]
                near[pl.ds(2 * (2 * block + odd) + half, 1), :] = kernel_scale * jnp.sum(
                    part.T, axis=0, keepdims=True
                )
        return carry

    lax.fori_loop(0, CLUSTERS // 2, block_step, 0)


def near_kernel(
    place,
    before,
    strip,
    after,
    lhs,
    self_rows,
    near,
    features,
    charge,
    entries_vmem,
    entries,
    semaphore,
    *sums,
):
    wide_index = place[0]
    narrow_index = place[1]

    def put_source(slot, halves, origin):
        features[slot] = source_features(halves, origin)
        for half in range(2):
            row = halves[half][3:4]
            charge[slot, :, half * LANES : (half + 1) * LANES] = jnp.broadcast_to(row, (8, LANES))

    base = (wide_index * GROUP + narrow_index * CLUSTERS + 1).astype(f32)
    targets, sources = [], []
    for ref in (before, strip, after):
        for block in range(3):
            start = PAIR_ROW + 8 * block
            targets.append(ref[start : start + 1, :])
            sources.append(ref[start : start + 1 + 1, :][1:2])
    nothing = jnp.zeros((6, LANES), f32)
    own_ids = jnp.concatenate(sources + [targets[4]] + [nothing], axis=0)
    other_ids = jnp.concatenate(targets + [sources[4]] + [nothing], axis=0)
    local = own_ids - base
    used = (local >= 0.0) & (local < CLUSTERS) & (own_ids > 0.0)
    count = used.astype(f32)
    upto = as_bf16(iota((LANES, LANES), 0) <= iota((LANES, LANES), 1))
    inclusive = jnp.dot(count.astype(bf16), upto, preferred_element_type=f32)
    totals = jnp.sum(count, axis=1, keepdims=True)
    row_of = iota((16, LANES), 0)
    offset = jnp.zeros((16, LANES), f32)
    for row in range(10):
        offset = jnp.where(row_of > row, offset + totals[row : row + 1], offset)
    spot = inclusive - count + offset
    other = other_ids - 1.0
    group = jnp.floor(other * (1.0 / GROUP))
    rest = other - GROUP * group
    depth = jnp.floor(rest * (1.0 / WIDTH))
    column = rest - WIDTH * depth
    group_step = group - (wide_index - 1).astype(f32)
    depth_step = depth - (2 * narrow_index - 1).astype(f32)
    window = group_step * STRIP_CLUSTERS + depth_step * WIDTH + column
    window = jnp.where(used, window, 0.0)
    local = jnp.where(used, local, 0.0)
    spot = jnp.where(used, spot, -1.0)
    spot_high = jnp.floor(spot * (1.0 / LANES))
    spot_low = spot - LANES * spot_high
    listed = jnp.zeros((16, LANES), f32)
    eight = iota((8, LANES), 0).astype(f32)
    tall = iota((LANES, LANES), 0).astype(f32)
    for row in range(10):
        here = eight == spot_high[row : row + 1]
        values = jnp.concatenate(
            [
                jnp.where(here, local[row : row + 1], 0.0),
                jnp.where(here, window[row : row + 1], 0.0),
            ],
            axis=0,
        ).astype(bf16)
        hot = as_bf16(tall == spot_low[row : row + 1])
        listed = listed + lax.dot_general(
            values, hot, (((1,), (1,)), ((), ())), preferred_element_type=f32
        )
    coded = listed[:8] * float(GROUP) + listed[8:]
    coded = jnp.where(eight == 7.0, jnp.sum(totals), coded)
    entries_vmem[...] = coded.astype(i32)
    copy = pltpu.make_async_copy(entries_vmem, entries, semaphore)
    copy.start()

    for total in sums:
        total[...] = jnp.zeros(total.shape, f32)
    origin = own_origin(strip, 64)

    def window_block(block, carry):
        for part, ref in enumerate((before, strip, after)):
            for odd in range(2):
                put_source(
                    part * STRIP_CLUSTERS + 2 * block + odd, cluster_halves(ref, block, odd), origin
                )
        return carry

    lax.fori_loop(0, STRIP_CLUSTERS // 2, window_block, 0)
    features[DUMMY] = jnp.zeros((DEPTH, C), bf16)
    charge[DUMMY] = jnp.zeros((8, C), f32)

    copy.wait()
    pair_total = entries[7, 0]

    def pair_step(step, carry):
        for turn in range(UNROLL):
            index = step * UNROLL + turn
            code = entries[index >> 7, index & (LANES - 1)]
            live = index < pair_total
            cluster = jnp.where(live, code >> 7, 0)
            slot = jnp.where(live, code & (LANES - 1), DUMMY)

            def add(start, value):
                sums[turn % SUMS][cluster, start : start + CHUNK, :] += value

            weighted(
                lambda start: lhs[cluster, start : start + CHUNK, :],
                features[slot],
                charge[slot, 0:1, 0:LANES],
                charge[slot, 0:1, LANES:C],
                add,
            )
        return carry

    lax.fori_loop(0, (pair_total + UNROLL - 1) // UNROLL, pair_step, 0)

    for cluster in range(CLUSTERS):
        for half in range(2):
            rows = slice(half * LANES, (half + 1) * LANES)
            total = sums[0][cluster, rows, :]
            for turn in range(1, SUMS):
                total = total + sums[turn][cluster, rows, :]
            row = 2 * cluster + half
            near[row : row + 1, :] = self_rows[row : row + 1, :] + kernel_scale * jnp.sum(
                total.T, axis=0, keepdims=True
            )


def far_kernel(
    place,
    far_count,
    before,
    strip,
    after,
    top,
    far_pairs,
    near,
    order,
    target_basis,
    potential,
    total,
):
    wide_index = place[0]
    narrow_index = place[1]
    first = wide_index * GROUP + narrow_index * CLUSTERS
    target = far_pairs[0:1, :] - first
    source = far_pairs[1:2, :]
    is_leaf = far_pairs[2:3, :] == 0
    live = iota((1, LANES), 1) < far_count[0]
    index = jnp.where(is_leaf, source - (wide_index - 1) * GROUP, source + 3 * GROUP)
    skel = slice(SKEL_ROW, SKEL_ROW + GROUP)
    table = jnp.concatenate([before[skel, :], strip[skel, :], after[skel, :], top[...]], axis=0)
    chosen = as_bf16(iota((table.shape[0], LANES), 0) == index)
    over_rows = ((0,), (0,))
    sources = parts_dot(table, chosen, over_rows)
    own_start = pl.multiple_of(SKEL_ROW + narrow_index * CLUSTERS, 8)
    own_skel = strip[pl.ds(own_start, CLUSTERS), :]
    own_chosen = as_bf16(iota((CLUSTERS, LANES), 0) == target)
    targets = parts_dot(own_skel, own_chosen, over_rows)
    rows = []
    for a in range(R):
        square = soft_square
        for axis in range(3):
            offset = sources[axis * R : (axis + 1) * R] - targets[axis * R + a : axis * R + a + 1]
            square = square + offset * offset
        product = lax.rsqrt(square) * sources[3 * R :]
        rows.append(jnp.sum(product, axis=0, keepdims=True))
    middle = jnp.where(live, jnp.concatenate(rows, axis=0) * kernel_scale, 0.0)
    for cluster in range(CLUSTERS):
        column = jnp.sum(jnp.where(target == cluster, middle, 0.0), axis=1, keepdims=True)
        spread = jnp.sum(
            target_basis[:, cluster * C : (cluster + 1) * C] * column, axis=0, keepdims=True
        )
        for half in range(2):
            row = 2 * cluster + half
            total[row : row + 1, :] = (
                near[row : row + 1, :] + spread[:, half * LANES : (half + 1) * LANES]
            )
    low = order[...] & (LANES - 1)
    high = order[...] >> 7
    tall = iota((LANES, LANES), 0)
    wide = iota((ROWS, LANES), 0)
    whole = [part.astype(f32) for part in split3(total[...])]
    values, places = [], []
    for row in range(ROWS):
        here = wide == high[row : row + 1]
        parts = [jnp.where(here, part[row : row + 1, :], 0.0) for part in whole]
        values.append(jnp.concatenate(parts, axis=0).astype(bf16))
        places.append(as_bf16(tall == low[row : row + 1]))
    placed = lax.dot_general(
        jnp.concatenate(values, axis=1),
        jnp.concatenate(places, axis=1),
        (((1,), (1,)), ((), ())),
        preferred_element_type=f32,
    )
    out = placed[:ROWS] + placed[ROWS : 2 * ROWS] + placed[2 * ROWS :]
    potential[...] = out


def smem():
    return pl.BlockSpec(memory_space=pltpu.SMEM)


def in_hbm():
    return pl.BlockSpec(memory_space=pltpu.HBM)


def vmem():
    return pl.BlockSpec(memory_space=pltpu.VMEM)


params = pltpu.CompilerParams(vmem_limit_bytes=50 * 1024 * 1024)
first_params = pltpu.CompilerParams(vmem_limit_bytes=127 * 512 * 1024)


def local(
    points,
    charges,
    order,
    source_basis,
    target_basis,
    skeleton_points,
    transfer,
    top_points,
    near_pairs,
    near_count,
    far_pairs,
    far_count,
):
    wide_size = lax.axis_size("wide")
    place = jnp.stack([lax.axis_index("wide"), lax.axis_index("narrow")]).astype(i32)
    order = order.reshape(ROWS, LANES)
    shape = jax.ShapeDtypeStruct
    inputs = (
        order,
        points,
        charges.reshape(ROWS, LANES),
        near_pairs,
        source_basis,
        transfer,
        skeleton_points,
        top_points,
    )
    with jax.named_scope("slots"):
        own, message = pl.pallas_call(
            slots_kernel,
            out_shape=(
                shape((136, LANES), f32),
                shape((NARROW, MESSAGE_ROWS, LANES), f32),
            ),
            in_specs=[smem(), smem()] + [in_hbm()] * len(inputs),
            out_specs=[vmem()] * 2,
            scratch_shapes=[pltpu.VMEM(x.shape, x.dtype) for x in inputs]
            + [pltpu.SemaphoreType.DMA((len(inputs),))],
            compiler_params=first_params,
        )(near_count, place, *inputs)
    received = lax.all_to_all(message, "narrow", 0, 0, tiled=True)
    with jax.named_scope("self"):
        lhs, self_rows = pl.pallas_call(
            self_kernel,
            out_shape=(shape((CLUSTERS, C, DEPTH), bf16), shape((ROWS, LANES), f32)),
            in_specs=[vmem()],
            out_specs=[vmem()] * 2,
            scratch_shapes=[pltpu.VMEM((2, C, LANES), f32)],
            compiler_params=params,
        )(own)
    with jax.named_scope("strip"):
        strip, top_message = pl.pallas_call(
            strip_kernel,
            out_shape=(shape((STRIP_ROWS, LANES), f32), shape((wide_size, LANES), f32)),
            in_specs=[smem()] + [vmem()] * 3,
            out_specs=[vmem()] * 2,
            compiler_params=params,
        )(place, received, own, self_rows)
    before = lax.ppermute(strip, "wide", [(i, i + 1) for i in range(wide_size - 1)])
    after = lax.ppermute(strip, "wide", [(i + 1, i) for i in range(wide_size - 1)])
    tops = lax.all_to_all(top_message, "wide", 0, 0, tiled=True)
    with jax.named_scope("near"):
        near = pl.pallas_call(
            near_kernel,
            out_shape=shape((ROWS, LANES), f32),
            in_specs=[smem()] + [vmem()] * 5,
            out_specs=vmem(),
            scratch_shapes=[
                pltpu.VMEM((WINDOW + 1, DEPTH, C), bf16),
                pltpu.VMEM((WINDOW + 1, 8, C), f32),
                pltpu.VMEM((8, LANES), i32),
                pltpu.SMEM((8, LANES), i32),
                pltpu.SemaphoreType.DMA(()),
            ]
            + [pltpu.VMEM((CLUSTERS, C, LANES), f32)] * SUMS,
            compiler_params=params,
        )(place, before, strip, after, lhs, self_rows)
    with jax.named_scope("far"):
        potential = pl.pallas_call(
            far_kernel,
            out_shape=shape((ROWS, LANES), f32),
            in_specs=[smem(), smem()] + [vmem()] * 8,
            out_specs=vmem(),
            scratch_shapes=[pltpu.VMEM((ROWS, LANES), f32)],
            compiler_params=params,
        )(place, far_count, before, strip, after, tops, far_pairs, near, order, target_basis)
    return potential.reshape(-1)


def solution(mesh):
    both = ("wide", "narrow")
    split = P(None, both)
    return jax.shard_map(
        local,
        mesh=mesh,
        in_specs=(
            split,
            P(both),
            P(both),
            split,
            split,
            split,
            split,
            P(None, "wide"),
            split,
            P(both),
            split,
            P(both),
        ),
        out_specs=P(both),
        check_vma=False,
    )
```

```python
import jax
import jax.numpy as jnp
from jax import lax
from jax.experimental import pallas as pl
from jax.experimental.pallas import tpu as pltpu
from jax.sharding import PartitionSpec as P

C = 256
R = 32
LANES = 128
CLUSTERS = 16
ROWS = 32
NARROW = 8
GROUP = 128
WIDTH = 8
STRIP_CLUSTERS = 32
PAIR_ROW = 8 * STRIP_CLUSTERS
SKEL_ROW = PAIR_ROW + 24
STRIP_ROWS = SKEL_ROW + GROUP
SKEL_REC = 24
MESSAGE_ROWS = 72 + SKEL_REC
TOP_ROWS = 2
WINDOW = 3 * STRIP_CLUSTERS
DUMMY = WINDOW
DEPTH = 48
UNROLL = 8
SUMS = 4
CHUNK = 64

soft_square = 0.01
kernel_scale = 0.07957747154594767
f32 = jnp.float32
bf16 = jnp.bfloat16
i32 = jnp.int32


def iota(shape, dim):
    return lax.broadcasted_iota(i32, shape, dim)


def split3(x):
    high = x.astype(bf16)
    rest = x - high.astype(f32)
    mid = rest.astype(bf16)
    low = (rest - mid.astype(f32)).astype(bf16)
    return high, mid, low


def parts_dot(x, ones, dims):
    dots = [
        lax.dot_general(part, ones, (dims, ((), ())), preferred_element_type=f32)
        for part in split3(x)
    ]
    return dots[0] + dots[1] + dots[2]


def as_bf16(mask):
    return mask.astype(f32).astype(bf16)


def slots_kernel(near_count, place, *refs):
    count = 8
    held = refs[count + 2 : 2 * count + 2]
    semaphores = refs[2 * count + 2]
    own, message = refs[count : count + 2]
    copies = [
        pltpu.make_async_copy(refs[i], held[i], semaphores.at[i]) for i in range(count)
    ]
    for copy in copies:
        copy.start()
    order, points, charges, near_pairs, source_basis, transfer, skeleton_points, top_points = held
    narrow_index = place[1]
    for copy in copies[:4]:
        copy.wait()
    low = order[...] & (LANES - 1)
    high = order[...] >> 7
    sub = iota((8, LANES), 0)
    tables = []
    for row in range(ROWS):
        xyz = points[:, row * LANES : (row + 1) * LANES]
        charge = charges[row : row + 1, :]
        tables.append(jnp.concatenate([xyz, charge, xyz, charge], axis=0))
    tiles = []
    for tile in range(CLUSTERS):
        first = 4 * (tile // 2) + tile % 2
        low_tile = jnp.where(sub < 4, low[first : first + 1], low[first + 2 : first + 3])
        high_tile = jnp.where(sub < 4, high[first : first + 1], high[first + 2 : first + 3])
        values = jnp.zeros((8, LANES), f32)
        for row in range(ROWS):
            found = jnp.take_along_axis(tables[row], low_tile, axis=1)
            values = jnp.where(high_tile == row, found, values)
        own[8 * tile : 8 * tile + 8, :] = values
        tiles.append(values)

    pairs = jnp.where(iota((2, 64), 1) < near_count[0], near_pairs[...] + 1, 0).astype(f32)
    own[128:136, :] = jnp.zeros((8, LANES), f32)
    own[128:130, 0:64] = pairs
    for copy in copies[4:]:
        copy.wait()

    lane = iota((R, LANES), 1)
    skel = jnp.zeros((R, LANES), f32)
    for cluster in range(CLUSTERS):
        block, place = cluster // 2, 4 * (cluster % 2) + 3
        basis = source_basis[:, cluster * C : (cluster + 1) * C]
        product = (
            basis[:, :LANES] * tiles[2 * block][place : place + 1]
            + basis[:, LANES:] * tiles[2 * block + 1][place : place + 1]
        )
        skel = jnp.where(lane == cluster, jnp.sum(product, axis=1, keepdims=True), skel)
    skel_rows = skel.T[:CLUSTERS, :]
    long_lane = iota((R, CLUSTERS * R), 1)
    repeat = as_bf16(long_lane % R == iota((R, CLUSTERS * R), 0))
    tiled = parts_dot(skel_rows, repeat, ((1,), (0,)))
    mine = iota((CLUSTERS, CLUSTERS * R), 1) // R == iota((CLUSTERS, CLUSTERS * R), 0)
    flat = jnp.sum(jnp.where(mine, tiled, 0.0), axis=0, keepdims=True)
    partial = jnp.sum(transfer[...] * flat, axis=1, keepdims=True)
    skel = jnp.where(lane == CLUSTERS, partial, skel)
    to_charge = as_bf16(lane == iota((R, LANES), 0) + 3 * R)
    record = parts_dot(skel.T[:SKEL_REC, :], to_charge, ((1,), (0,)))
    fold = as_bf16(iota((CLUSTERS * R, LANES), 1) % R == iota((CLUSTERS * R, LANES), 0) % R)
    short_lane = iota((CLUSTERS, LANES), 1) // R
    geometry = jnp.zeros((CLUSTERS, LANES), f32)
    for axis in range(3):
        masked = jnp.where(mine, skeleton_points[axis : axis + 1, :], 0.0)
        folded = parts_dot(masked, fold, ((1,), (0,)))
        geometry = jnp.where(short_lane == axis, folded, geometry)
    spread = as_bf16(lane % R == iota((R, LANES), 0))
    top = parts_dot(top_points[...], spread, ((1,), (0,)))
    top_mine = iota((3, LANES), 1) // R == iota((3, LANES), 0)
    top_row = jnp.sum(jnp.where(top_mine, top, 0.0), axis=0, keepdims=True)
    last = jnp.where(iota((8, LANES), 0) == 1, top_row, 0.0)
    record = record + jnp.concatenate([geometry, last], axis=0)
    pair_block = own[128:136, :]
    for device in range(NARROW):
        for tile in range(8):
            message[device, 8 * tile : 8 * tile + 8, :] = jnp.where(
                narrow_index < device, tiles[8 + tile], tiles[tile]
            )
        message[device, 64:72, :] = jnp.where(narrow_index == device, 0.0, pair_block)
        message[device, 72:, :] = record


def top_kernel(received, self_rows, top_message):
    del self_rows
    last = received[0, 88:96, :]
    row = last[0:1] + last[1:2]
    for device in range(1, NARROW):
        row = row + received[device, 88:96, :][0:1]
    top_message[...] = jnp.broadcast_to(row, top_message.shape)


def strip_kernel(place, received, own, top_message, strip):
    del top_message
    narrow_index = place[1]
    down = jnp.maximum(narrow_index - 1, 0)
    up = jnp.minimum(narrow_index + 1, NARROW - 1)
    strip[0:64, :] = received[down, 0:64, :]
    strip[64:192, :] = own[0:128, :]
    strip[192:256, :] = received[up, 0:64, :]
    strip[PAIR_ROW : PAIR_ROW + 8, :] = received[down, 64:72, :]
    strip[PAIR_ROW + 8 : PAIR_ROW + 16, :] = own[128:136, :]
    strip[PAIR_ROW + 16 : PAIR_ROW + 24, :] = received[up, 64:72, :]
    for device in range(NARROW):
        start = SKEL_ROW + device * CLUSTERS
        strip[start : start + CLUSTERS, :] = received[device, 72:88, :]


def with_norms(halves, origin):
    out = []
    for half in halves:
        sub = iota((8, LANES), 0)
        shifted = jnp.where(sub < 3, half - origin, 0.0)
        norms = jnp.sum(shifted * shifted, axis=0, keepdims=True)
        out.append((shifted, norms))
    return out


def source_features(halves, origin):
    sub = iota((8, LANES), 0)
    columns = []
    for shifted, norms in with_norms(halves, origin):
        rows = jnp.where(sub < 3, shifted, jnp.where(sub == 4, norms, 0.0))
        rows = jnp.where(sub == 5, 1.0, rows)
        high, mid, low = [part.astype(f32) for part in split3(rows)]
        columns.append(jnp.concatenate([high, mid, high, mid, low, high], axis=0).astype(bf16))
    return jnp.concatenate(columns, axis=1)


def target_features(halves, origin):
    sub = iota((8, LANES), 0)
    columns = []
    for shifted, norms in with_norms(halves, origin):
        rows = jnp.where(sub < 3, -2.0 * shifted, jnp.where(sub == 5, norms + soft_square, 0.0))
        rows = jnp.where(sub == 4, 1.0, rows)
        high, mid, low = [part.astype(f32) for part in split3(rows)]
        stacked = jnp.concatenate([high, high, mid, mid, high, low], axis=0)
        columns.append(stacked.T.astype(bf16))
    return jnp.concatenate(columns, axis=0)


def cluster_halves(ref, block, odd):
    halves = []
    for half in range(2):
        tile = ref[pl.ds(pl.multiple_of(16 * block + 8 * half, 8), 8), :]
        halves.append(pltpu.roll(tile, 4, 0) if odd else tile)
    return halves


def own_origin(ref, start):
    whole = jnp.zeros((8, LANES), f32)
    for tile in range(CLUSTERS):
        whole = whole + ref[start + 8 * tile : start + 8 * tile + 8, :]
    mean = jnp.sum(whole, axis=1, keepdims=True) * (1.0 / (CLUSTERS * C))
    mean = jnp.broadcast_to(mean, (8, LANES))
    return jnp.where(iota((8, LANES), 0) < 3, mean + pltpu.roll(mean, 4, 0), 0.0)


def weighted(left, right, charge_low, charge_high, store):
    for start in range(0, C, CHUNK):
        square = jnp.dot(left(start), right, preferred_element_type=f32)
        inverse = lax.rsqrt(jnp.maximum(square, soft_square))
        store(start, inverse[:, :LANES] * charge_low + inverse[:, LANES:] * charge_high)


def self_kernel(own, lhs, near, held):
    origin = own_origin(own, 0)

    def block_step(block, carry):
        for odd in range(2):
            halves = cluster_halves(own, block, odd)
            lhs[2 * block + odd] = target_features(halves, origin)
            centre = jnp.sum(halves[0] + halves[1], axis=1, keepdims=True) * (1.0 / C)
            left = target_features(halves, centre)

            def store(start, value):
                held[odd, start : start + CHUNK, :] = value

            weighted(
                lambda start: left[start : start + CHUNK],
                source_features(halves, centre),
                halves[0][3:4],
                halves[1][3:4],
                store,
            )
            for half in range(2):
                part = held[odd, half * LANES : (half + 1) * LANES, :]
                near[pl.ds(2 * (2 * block + odd) + half, 1), :] = kernel_scale * jnp.sum(
                    part.T, axis=0, keepdims=True
                )
        return carry

    lax.fori_loop(0, CLUSTERS // 2, block_step, 0)


def near_kernel(
    place,
    before,
    strip,
    after,
    lhs,
    self_rows,
    near,
    features,
    charge,
    entries_vmem,
    entries,
    semaphore,
    *sums,
):
    wide_index = place[0]
    narrow_index = place[1]

    def put_source(slot, halves, origin):
        features[slot] = source_features(halves, origin)
        for half in range(2):
            row = halves[half][3:4]
            charge[slot, :, half * LANES : (half + 1) * LANES] = jnp.broadcast_to(row, (8, LANES))

    base = (wide_index * GROUP + narrow_index * CLUSTERS + 1).astype(f32)
    targets, sources = [], []
    for ref in (before, strip, after):
        for block in range(3):
            start = PAIR_ROW + 8 * block
            targets.append(ref[start : start + 1, :])
            sources.append(ref[start : start + 1 + 1, :][1:2])
    nothing = jnp.zeros((6, LANES), f32)
    own_ids = jnp.concatenate(sources + [targets[4]] + [nothing], axis=0)
    other_ids = jnp.concatenate(targets + [sources[4]] + [nothing], axis=0)
    local = own_ids - base
    used = (local >= 0.0) & (local < CLUSTERS) & (own_ids > 0.0)
    count = used.astype(f32)
    upto = as_bf16(iota((LANES, LANES), 0) <= iota((LANES, LANES), 1))
    inclusive = jnp.dot(count.astype(bf16), upto, preferred_element_type=f32)
    totals = jnp.sum(count, axis=1, keepdims=True)
    row_of = iota((16, LANES), 0)
    offset = jnp.zeros((16, LANES), f32)
    for row in range(10):
        offset = jnp.where(row_of > row, offset + totals[row : row + 1], offset)
    spot = inclusive - count + offset
    other = other_ids - 1.0
    group = jnp.floor(other * (1.0 / GROUP))
    rest = other - GROUP * group
    depth = jnp.floor(rest * (1.0 / WIDTH))
    column = rest - WIDTH * depth
    group_step = group - (wide_index - 1).astype(f32)
    depth_step = depth - (2 * narrow_index - 1).astype(f32)
    window = group_step * STRIP_CLUSTERS + depth_step * WIDTH + column
    window = jnp.where(used, window, 0.0)
    local = jnp.where(used, local, 0.0)
    spot = jnp.where(used, spot, -1.0)
    spot_high = jnp.floor(spot * (1.0 / LANES))
    spot_low = spot - LANES * spot_high
    listed = jnp.zeros((16, LANES), f32)
    eight = iota((8, LANES), 0).astype(f32)
    tall = iota((LANES, LANES), 0).astype(f32)
    for row in range(10):
        here = eight == spot_high[row : row + 1]
        values = jnp.concatenate(
            [
                jnp.where(here, local[row : row + 1], 0.0),
                jnp.where(here, window[row : row + 1], 0.0),
            ],
            axis=0,
        ).astype(bf16)
        hot = as_bf16(tall == spot_low[row : row + 1])
        listed = listed + lax.dot_general(
            values, hot, (((1,), (1,)), ((), ())), preferred_element_type=f32
        )
    coded = listed[:8] * float(GROUP) + listed[8:]
    coded = jnp.where(eight == 7.0, jnp.sum(totals), coded)
    entries_vmem[...] = coded.astype(i32)
    copy = pltpu.make_async_copy(entries_vmem, entries, semaphore)
    copy.start()

    for total in sums:
        total[...] = jnp.zeros(total.shape, f32)
    origin = own_origin(strip, 64)

    def window_block(block, carry):
        for part, ref in enumerate((before, strip, after)):
            for odd in range(2):
                put_source(
                    part * STRIP_CLUSTERS + 2 * block + odd, cluster_halves(ref, block, odd), origin
                )
        return carry

    lax.fori_loop(0, STRIP_CLUSTERS // 2, window_block, 0)
    features[DUMMY] = jnp.zeros((DEPTH, C), bf16)
    charge[DUMMY] = jnp.zeros((8, C), f32)

    copy.wait()
    pair_total = entries[7, 0]

    def pair_step(step, carry):
        for turn in range(UNROLL):
            index = step * UNROLL + turn
            code = entries[index >> 7, index & (LANES - 1)]
            live = index < pair_total
            cluster = jnp.where(live, code >> 7, 0)
            slot = jnp.where(live, code & (LANES - 1), DUMMY)

            def add(start, value):
                sums[turn % SUMS][cluster, start : start + CHUNK, :] += value

            weighted(
                lambda start: lhs[cluster, start : start + CHUNK, :],
                features[slot],
                charge[slot, 0:1, 0:LANES],
                charge[slot, 0:1, LANES:C],
                add,
            )
        return carry

    lax.fori_loop(0, (pair_total + UNROLL - 1) // UNROLL, pair_step, 0)

    for cluster in range(CLUSTERS):
        for half in range(2):
            rows = slice(half * LANES, (half + 1) * LANES)
            total = sums[0][cluster, rows, :]
            for turn in range(1, SUMS):
                total = total + sums[turn][cluster, rows, :]
            row = 2 * cluster + half
            near[row : row + 1, :] = self_rows[row : row + 1, :] + kernel_scale * jnp.sum(
                total.T, axis=0, keepdims=True
            )


def far_kernel(
    place,
    far_count,
    before,
    strip,
    after,
    top,
    far_pairs,
    near,
    order,
    target_basis,
    potential,
    total,
):
    wide_index = place[0]
    narrow_index = place[1]
    first = wide_index * GROUP + narrow_index * CLUSTERS
    target = far_pairs[0:1, :] - first
    source = far_pairs[1:2, :]
    is_leaf = far_pairs[2:3, :] == 0
    live = iota((1, LANES), 1) < far_count[0]
    index = jnp.where(is_leaf, source - (wide_index - 1) * GROUP, source + 3 * GROUP)
    skel = slice(SKEL_ROW, SKEL_ROW + GROUP)
    tops = top[pl.ds(0, top.shape[0] // TOP_ROWS, stride=TOP_ROWS), :]
    table = jnp.concatenate([before[skel, :], strip[skel, :], after[skel, :], tops], axis=0)
    chosen = as_bf16(iota((table.shape[0], LANES), 0) == index)
    over_rows = ((0,), (0,))
    sources = parts_dot(table, chosen, over_rows)
    own_start = pl.multiple_of(SKEL_ROW + narrow_index * CLUSTERS, 8)
    own_skel = strip[pl.ds(own_start, CLUSTERS), :]
    own_chosen = as_bf16(iota((CLUSTERS, LANES), 0) == target)
    targets = parts_dot(own_skel, own_chosen, over_rows)
    rows = []
    for a in range(R):
        square = soft_square
        for axis in range(3):
            offset = sources[axis * R : (axis + 1) * R] - targets[axis * R + a : axis * R + a + 1]
            square = square + offset * offset
        product = lax.rsqrt(square) * sources[3 * R :]
        rows.append(jnp.sum(product, axis=0, keepdims=True))
    middle = jnp.where(live, jnp.concatenate(rows, axis=0) * kernel_scale, 0.0)
    for cluster in range(CLUSTERS):
        column = jnp.sum(jnp.where(target == cluster, middle, 0.0), axis=1, keepdims=True)
        spread = jnp.sum(
            target_basis[:, cluster * C : (cluster + 1) * C] * column, axis=0, keepdims=True
        )
        for half in range(2):
            row = 2 * cluster + half
            total[row : row + 1, :] = (
                near[row : row + 1, :] + spread[:, half * LANES : (half + 1) * LANES]
            )
    low = order[...] & (LANES - 1)
    high = order[...] >> 7
    tall = iota((LANES, LANES), 0)
    wide = iota((ROWS, LANES), 0)
    whole = [part.astype(f32) for part in split3(total[...])]
    values, places = [], []
    for row in range(ROWS):
        here = wide == high[row : row + 1]
        parts = [jnp.where(here, part[row : row + 1, :], 0.0) for part in whole]
        values.append(jnp.concatenate(parts, axis=0).astype(bf16))
        places.append(as_bf16(tall == low[row : row + 1]))
    placed = lax.dot_general(
        jnp.concatenate(values, axis=1),
        jnp.concatenate(places, axis=1),
        (((1,), (1,)), ((), ())),
        preferred_element_type=f32,
    )
    out = placed[:ROWS] + placed[ROWS : 2 * ROWS] + placed[2 * ROWS :]
    potential[...] = out


def smem():
    return pl.BlockSpec(memory_space=pltpu.SMEM)


def in_hbm():
    return pl.BlockSpec(memory_space=pltpu.HBM)


def vmem():
    return pl.BlockSpec(memory_space=pltpu.VMEM)


params = pltpu.CompilerParams(vmem_limit_bytes=50 * 1024 * 1024)
first_params = pltpu.CompilerParams(vmem_limit_bytes=127 * 512 * 1024)


def local(
    points,
    charges,
    order,
    source_basis,
    target_basis,
    skeleton_points,
    transfer,
    top_points,
    near_pairs,
    near_count,
    far_pairs,
    far_count,
):
    wide_size = lax.axis_size("wide")
    place = jnp.stack([lax.axis_index("wide"), lax.axis_index("narrow")]).astype(i32)
    order = order.reshape(ROWS, LANES)
    shape = jax.ShapeDtypeStruct
    inputs = (
        order,
        points,
        charges.reshape(ROWS, LANES),
        near_pairs,
        source_basis,
        transfer,
        skeleton_points,
        top_points,
    )
    with jax.named_scope("slots"):
        own, message = pl.pallas_call(
            slots_kernel,
            out_shape=(
                shape((136, LANES), f32),
                shape((NARROW, MESSAGE_ROWS, LANES), f32),
            ),
            in_specs=[smem(), smem()] + [in_hbm()] * len(inputs),
            out_specs=[vmem()] * 2,
            scratch_shapes=[pltpu.VMEM(x.shape, x.dtype) for x in inputs]
            + [pltpu.SemaphoreType.DMA((len(inputs),))],
            compiler_params=first_params,
        )(near_count, place, *inputs)
    received = lax.all_to_all(message, "narrow", 0, 0, tiled=True)
    with jax.named_scope("self"):
        lhs, self_rows = pl.pallas_call(
            self_kernel,
            out_shape=(shape((CLUSTERS, C, DEPTH), bf16), shape((ROWS, LANES), f32)),
            in_specs=[vmem()],
            out_specs=[vmem()] * 2,
            scratch_shapes=[pltpu.VMEM((2, C, LANES), f32)],
            compiler_params=params,
        )(own)
    with jax.named_scope("top"):
        top_message = pl.pallas_call(
            top_kernel,
            out_shape=shape((TOP_ROWS * wide_size, LANES), f32),
            in_specs=[vmem()] * 2,
            out_specs=vmem(),
            compiler_params=params,
        )(received, self_rows)
    tops = lax.all_to_all(top_message, "wide", 0, 0, tiled=True)
    with jax.named_scope("strip"):
        strip = pl.pallas_call(
            strip_kernel,
            out_shape=shape((STRIP_ROWS, LANES), f32),
            in_specs=[smem()] + [vmem()] * 3,
            out_specs=vmem(),
            compiler_params=params,
        )(place, received, own, top_message)
    before = lax.ppermute(strip, "wide", [(i, i + 1) for i in range(wide_size - 1)])
    after = lax.ppermute(strip, "wide", [(i + 1, i) for i in range(wide_size - 1)])
    with jax.named_scope("near"):
        near = pl.pallas_call(
            near_kernel,
            out_shape=shape((ROWS, LANES), f32),
            in_specs=[smem()] + [vmem()] * 5,
            out_specs=vmem(),
            scratch_shapes=[
                pltpu.VMEM((WINDOW + 1, DEPTH, C), bf16),
                pltpu.VMEM((WINDOW + 1, 8, C), f32),
                pltpu.VMEM((8, LANES), i32),
                pltpu.SMEM((8, LANES), i32),
                pltpu.SemaphoreType.DMA(()),
            ]
            + [pltpu.VMEM((CLUSTERS, C, LANES), f32)] * SUMS,
            compiler_params=params,
        )(place, before, strip, after, lhs, self_rows)
    with jax.named_scope("far"):
        potential = pl.pallas_call(
            far_kernel,
            out_shape=shape((ROWS, LANES), f32),
            in_specs=[smem(), smem()] + [vmem()] * 8,
            out_specs=vmem(),
            scratch_shapes=[pltpu.VMEM((ROWS, LANES), f32)],
            compiler_params=params,
        )(place, far_count, before, strip, after, tops, far_pairs, near, order, target_basis)
    return potential.reshape(-1)


def solution(mesh):
    both = ("wide", "narrow")
    split = P(None, both)
    return jax.shard_map(
        local,
        mesh=mesh,
        in_specs=(
            split,
            P(both),
            P(both),
            split,
            split,
            split,
            split,
            P(None, "wide"),
            split,
            P(both),
            split,
            P(both),
        ),
        out_specs=P(both),
        check_vma=False,
    )
```

```python
import jax
import jax.numpy as jnp
from jax import lax
from jax.experimental import pallas as pl
from jax.experimental.pallas import tpu as pltpu
from jax.sharding import PartitionSpec as P

C = 256
R = 32
LANES = 128
CLUSTERS = 16
ROWS = 32
NARROW = 8
GROUP = 128
WIDTH = 8
STRIP_CLUSTERS = 32
PAIR_ROW = 8 * STRIP_CLUSTERS
SKEL_ROW = PAIR_ROW + 24
STRIP_ROWS = SKEL_ROW + GROUP
SKEL_REC = 24
TOP_ROWS = 2
WINDOW = 3 * STRIP_CLUSTERS
DUMMY = WINDOW
DEPTH = 48
UNROLL = 8
SUMS = 2
CHUNK = 64

soft_square = 0.01
kernel_scale = 0.07957747154594767
f32 = jnp.float32
bf16 = jnp.bfloat16
i32 = jnp.int32


def iota(shape, dim):
    return lax.broadcasted_iota(i32, shape, dim)


def split3(x):
    high = x.astype(bf16)
    rest = x - high.astype(f32)
    mid = rest.astype(bf16)
    low = (rest - mid.astype(f32)).astype(bf16)
    return high, mid, low


def parts_dot(x, ones, dims):
    dots = [
        lax.dot_general(part, ones, (dims, ((), ())), preferred_element_type=f32)
        for part in split3(x)
    ]
    return dots[0] + dots[1] + dots[2]


def as_bf16(mask):
    return mask.astype(f32).astype(bf16)


def slots_kernel(near_count, *refs):
    count = 8
    own, skel_out = refs[count : count + 2]
    held = refs[count + 2 : 2 * count + 2]
    semaphores = refs[2 * count + 2]
    copies = [
        pltpu.make_async_copy(refs[i], held[i], semaphores.at[i]) for i in range(count)
    ]
    for copy in copies:
        copy.start()
    order, points, charges, near_pairs, source_basis, transfer, skeleton_points, top_points = held
    for copy in copies[:4]:
        copy.wait()
    low = order[...] & (LANES - 1)
    high = order[...] >> 7
    sub = iota((8, LANES), 0)
    tables = []
    for row in range(ROWS):
        xyz = points[:, row * LANES : (row + 1) * LANES]
        charge = charges[row : row + 1, :]
        tables.append(jnp.concatenate([xyz, charge, xyz, charge], axis=0))
    tiles = []
    for tile in range(CLUSTERS):
        first = 4 * (tile // 2) + tile % 2
        low_tile = jnp.where(sub < 4, low[first : first + 1], low[first + 2 : first + 3])
        high_tile = jnp.where(sub < 4, high[first : first + 1], high[first + 2 : first + 3])
        values = jnp.zeros((8, LANES), f32)
        for row in range(ROWS):
            found = jnp.take_along_axis(tables[row], low_tile, axis=1)
            values = jnp.where(high_tile == row, found, values)
        own[8 * tile : 8 * tile + 8, :] = values
        tiles.append(values)

    pairs = jnp.where(iota((2, 64), 1) < near_count[0], near_pairs[...] + 1, 0).astype(f32)
    own[128:136, :] = jnp.zeros((8, LANES), f32)
    own[128:130, 0:64] = pairs
    for copy in copies[4:]:
        copy.wait()

    lane = iota((R, LANES), 1)
    skel = jnp.zeros((R, LANES), f32)
    for cluster in range(CLUSTERS):
        block, place = cluster // 2, 4 * (cluster % 2) + 3
        basis = source_basis[:, cluster * C : (cluster + 1) * C]
        product = (
            basis[:, :LANES] * tiles[2 * block][place : place + 1]
            + basis[:, LANES:] * tiles[2 * block + 1][place : place + 1]
        )
        skel = jnp.where(lane == cluster, jnp.sum(product, axis=1, keepdims=True), skel)
    skel_rows = skel.T[:CLUSTERS, :]
    long_lane = iota((R, CLUSTERS * R), 1)
    repeat = as_bf16(long_lane % R == iota((R, CLUSTERS * R), 0))
    tiled = parts_dot(skel_rows, repeat, ((1,), (0,)))
    mine = iota((CLUSTERS, CLUSTERS * R), 1) // R == iota((CLUSTERS, CLUSTERS * R), 0)
    flat = jnp.sum(jnp.where(mine, tiled, 0.0), axis=0, keepdims=True)
    partial = jnp.sum(transfer[...] * flat, axis=1, keepdims=True)
    skel = jnp.where(lane == CLUSTERS, partial, skel)
    to_charge = as_bf16(lane == iota((R, LANES), 0) + 3 * R)
    record = parts_dot(skel.T[:SKEL_REC, :], to_charge, ((1,), (0,)))
    fold = as_bf16(iota((CLUSTERS * R, LANES), 1) % R == iota((CLUSTERS * R, LANES), 0) % R)
    short_lane = iota((CLUSTERS, LANES), 1) // R
    geometry = jnp.zeros((CLUSTERS, LANES), f32)
    for axis in range(3):
        masked = jnp.where(mine, skeleton_points[axis : axis + 1, :], 0.0)
        folded = parts_dot(masked, fold, ((1,), (0,)))
        geometry = jnp.where(short_lane == axis, folded, geometry)
    spread = as_bf16(lane % R == iota((R, LANES), 0))
    top = parts_dot(top_points[...], spread, ((1,), (0,)))
    top_mine = iota((3, LANES), 1) // R == iota((3, LANES), 0)
    top_row = jnp.sum(jnp.where(top_mine, top, 0.0), axis=0, keepdims=True)
    last = jnp.where(iota((8, LANES), 0) == 1, top_row, 0.0)
    record = record + jnp.concatenate([geometry, last], axis=0)
    for device in range(NARROW):
        skel_out[device] = record


def top_kernel(skels, top_message):
    last = skels[0, CLUSTERS:SKEL_REC, :]
    row = last[0:1] + last[1:2]
    for device in range(1, NARROW):
        row = row + skels[device, CLUSTERS:SKEL_REC, :][0:1]
    top_message[...] = jnp.broadcast_to(row, top_message.shape)


def strip_kernel(skels, from_down, own, from_up, top_message, strip):
    del top_message
    strip[0:64, :] = from_down[64:128, :]
    strip[64:192, :] = own[0:128, :]
    strip[192:256, :] = from_up[0:64, :]
    strip[PAIR_ROW : PAIR_ROW + 8, :] = from_down[128:136, :]
    strip[PAIR_ROW + 8 : PAIR_ROW + 16, :] = own[128:136, :]
    strip[PAIR_ROW + 16 : PAIR_ROW + 24, :] = from_up[128:136, :]
    for device in range(NARROW):
        start = SKEL_ROW + device * CLUSTERS
        strip[start : start + CLUSTERS, :] = skels[device, :CLUSTERS, :]


def with_norms(halves, origin):
    out = []
    for half in halves:
        sub = iota((8, LANES), 0)
        shifted = jnp.where(sub < 3, half - origin, 0.0)
        norms = jnp.sum(shifted * shifted, axis=0, keepdims=True)
        out.append((shifted, norms))
    return out


def source_features(halves, origin):
    sub = iota((8, LANES), 0)
    columns = []
    for shifted, norms in with_norms(halves, origin):
        rows = jnp.where(sub < 3, shifted, jnp.where(sub == 4, norms, 0.0))
        rows = jnp.where(sub == 5, 1.0, rows)
        high, mid, low = [part.astype(f32) for part in split3(rows)]
        columns.append(jnp.concatenate([high, mid, high, mid, low, high], axis=0).astype(bf16))
    return jnp.concatenate(columns, axis=1)


def target_features(halves, origin):
    sub = iota((8, LANES), 0)
    columns = []
    for shifted, norms in with_norms(halves, origin):
        rows = jnp.where(sub < 3, -2.0 * shifted, jnp.where(sub == 5, norms + soft_square, 0.0))
        rows = jnp.where(sub == 4, 1.0, rows)
        high, mid, low = [part.astype(f32) for part in split3(rows)]
        stacked = jnp.concatenate([high, high, mid, mid, high, low], axis=0)
        columns.append(stacked.T.astype(bf16))
    return jnp.concatenate(columns, axis=0)


def cluster_halves(ref, block, odd):
    halves = []
    for half in range(2):
        tile = ref[pl.ds(pl.multiple_of(16 * block + 8 * half, 8), 8), :]
        halves.append(pltpu.roll(tile, 4, 0) if odd else tile)
    return halves


def own_origin(ref, start):
    whole = jnp.zeros((8, LANES), f32)
    for tile in range(CLUSTERS):
        whole = whole + ref[start + 8 * tile : start + 8 * tile + 8, :]
    mean = jnp.sum(whole, axis=1, keepdims=True) * (1.0 / (CLUSTERS * C))
    mean = jnp.broadcast_to(mean, (8, LANES))
    return jnp.where(iota((8, LANES), 0) < 3, mean + pltpu.roll(mean, 4, 0), 0.0)


def weighted(left, right, charge_low, charge_high, store):
    for start in range(0, C, CHUNK):
        square = jnp.dot(left(start), right, preferred_element_type=f32)
        inverse = lax.rsqrt(jnp.maximum(square, soft_square))
        store(start, inverse[:, :LANES] * charge_low + inverse[:, LANES:] * charge_high)


def self_kernel(strip, lhs, near, held):
    origin = own_origin(strip, 64)

    def block_step(block, carry):
        for odd in range(2):
            halves = cluster_halves(strip, block + 4, odd)
            lhs[2 * block + odd] = target_features(halves, origin)
            centre = jnp.sum(halves[0] + halves[1], axis=1, keepdims=True) * (1.0 / C)
            left = target_features(halves, centre)

            def store(start, value):
                held[odd, start : start + CHUNK, :] = value

            weighted(
                lambda start: left[start : start + CHUNK],
                source_features(halves, centre),
                halves[0][3:4],
                halves[1][3:4],
                store,
            )
            for half in range(2):
                part = held[odd, half * LANES : (half + 1) * LANES, :]
                near[pl.ds(2 * (2 * block + odd) + half, 1), :] = kernel_scale * jnp.sum(
                    part.T, axis=0, keepdims=True
                )
        return carry

    lax.fori_loop(0, CLUSTERS // 2, block_step, 0)


def near_kernel(
    place,
    before,
    strip,
    after,
    lhs,
    self_rows,
    near,
    features,
    charge,
    entries_vmem,
    entries,
    semaphore,
    *sums,
):
    wide_index = place[0]
    narrow_index = place[1]

    def put_source(slot, halves, origin):
        features[slot] = source_features(halves, origin)
        for half in range(2):
            row = halves[half][3:4]
            charge[slot, :, half * LANES : (half + 1) * LANES] = jnp.broadcast_to(row, (8, LANES))

    base = (wide_index * GROUP + narrow_index * CLUSTERS + 1).astype(f32)
    targets, sources = [], []
    for ref in (before, strip, after):
        for block in range(3):
            start = PAIR_ROW + 8 * block
            targets.append(ref[start : start + 1, :])
            sources.append(ref[start : start + 1 + 1, :][1:2])
    nothing = jnp.zeros((6, LANES), f32)
    own_ids = jnp.concatenate(sources + [targets[4]] + [nothing], axis=0)
    other_ids = jnp.concatenate(targets + [sources[4]] + [nothing], axis=0)
    local = own_ids - base
    used = (local >= 0.0) & (local < CLUSTERS) & (own_ids > 0.0)
    count = used.astype(f32)
    upto = as_bf16(iota((LANES, LANES), 0) <= iota((LANES, LANES), 1))
    inclusive = jnp.dot(count.astype(bf16), upto, preferred_element_type=f32)
    totals = jnp.sum(count, axis=1, keepdims=True)
    row_of = iota((16, LANES), 0)
    offset = jnp.zeros((16, LANES), f32)
    for row in range(10):
        offset = jnp.where(row_of > row, offset + totals[row : row + 1], offset)
    spot = inclusive - count + offset
    other = other_ids - 1.0
    group = jnp.floor(other * (1.0 / GROUP))
    rest = other - GROUP * group
    depth = jnp.floor(rest * (1.0 / WIDTH))
    column = rest - WIDTH * depth
    group_step = group - (wide_index - 1).astype(f32)
    depth_step = depth - (2 * narrow_index - 1).astype(f32)
    window = group_step * STRIP_CLUSTERS + depth_step * WIDTH + column
    window = jnp.where(used, window, 0.0)
    local = jnp.where(used, local, 0.0)
    spot = jnp.where(used, spot, -1.0)
    spot_high = jnp.floor(spot * (1.0 / LANES))
    spot_low = spot - LANES * spot_high
    listed = jnp.zeros((16, LANES), f32)
    eight = iota((8, LANES), 0).astype(f32)
    tall = iota((LANES, LANES), 0).astype(f32)
    for row in range(10):
        here = eight == spot_high[row : row + 1]
        values = jnp.concatenate(
            [
                jnp.where(here, local[row : row + 1], 0.0),
                jnp.where(here, window[row : row + 1], 0.0),
            ],
            axis=0,
        ).astype(bf16)
        hot = as_bf16(tall == spot_low[row : row + 1])
        listed = listed + lax.dot_general(
            values, hot, (((1,), (1,)), ((), ())), preferred_element_type=f32
        )
    coded = listed[:8] * float(GROUP) + listed[8:]
    coded = jnp.where(eight == 7.0, jnp.sum(totals), coded)
    entries_vmem[...] = coded.astype(i32)
    copy = pltpu.make_async_copy(entries_vmem, entries, semaphore)
    copy.start()

    for total in sums:
        total[...] = jnp.zeros(total.shape, f32)
    origin = own_origin(strip, 64)

    def window_block(block, carry):
        for part, ref in enumerate((before, strip, after)):
            for odd in range(2):
                put_source(
                    part * STRIP_CLUSTERS + 2 * block + odd, cluster_halves(ref, block, odd), origin
                )
        return carry

    lax.fori_loop(0, STRIP_CLUSTERS // 2, window_block, 0)
    features[DUMMY] = jnp.zeros((DEPTH, C), bf16)
    charge[DUMMY] = jnp.zeros((8, C), f32)

    copy.wait()
    pair_total = entries[7, 0]

    def pair_steps(first, turns, carry):
        for turn in range(turns):
            index = first + turn
            code = entries[index >> 7, index & (LANES - 1)]
            live = index < pair_total
            cluster = jnp.where(live, code >> 7, 0)
            slot = jnp.where(live, code & (LANES - 1), DUMMY)

            def add(start, value):
                sums[turn % SUMS][cluster, start : start + CHUNK, :] += value

            weighted(
                lambda start: lhs[cluster, start : start + CHUNK, :],
                features[slot],
                charge[slot, 0:1, 0:LANES],
                charge[slot, 0:1, LANES:C],
                add,
            )
        return carry

    steps = (pair_total + UNROLL - 1) // UNROLL
    lax.fori_loop(
        0, steps // 2, lambda step, carry: pair_steps(2 * UNROLL * step, 2 * UNROLL, carry), 0
    )
    lax.fori_loop(
        2 * (steps // 2), steps, lambda step, carry: pair_steps(UNROLL * step, UNROLL, carry), 0
    )

    for cluster in range(CLUSTERS):
        for half in range(2):
            rows = slice(half * LANES, (half + 1) * LANES)
            total = sums[0][cluster, rows, :]
            for turn in range(1, SUMS):
                total = total + sums[turn][cluster, rows, :]
            row = 2 * cluster + half
            near[row : row + 1, :] = self_rows[row : row + 1, :] + kernel_scale * jnp.sum(
                total.T, axis=0, keepdims=True
            )


def far_kernel(
    place,
    far_count,
    before,
    strip,
    after,
    top,
    far_pairs,
    near,
    order,
    target_basis,
    potential,
    total,
):
    wide_index = place[0]
    narrow_index = place[1]
    first = wide_index * GROUP + narrow_index * CLUSTERS
    target = far_pairs[0:1, :] - first
    source = far_pairs[1:2, :]
    is_leaf = far_pairs[2:3, :] == 0
    live = iota((1, LANES), 1) < far_count[0]
    index = jnp.where(is_leaf, source - (wide_index - 1) * GROUP, source + 3 * GROUP)
    skel = slice(SKEL_ROW, SKEL_ROW + GROUP)
    tops = top[pl.ds(0, top.shape[0] // TOP_ROWS, stride=TOP_ROWS), :]
    table = jnp.concatenate([before[skel, :], strip[skel, :], after[skel, :], tops], axis=0)
    chosen = as_bf16(iota((table.shape[0], LANES), 0) == index)
    over_rows = ((0,), (0,))
    sources = parts_dot(table, chosen, over_rows)
    own_start = pl.multiple_of(SKEL_ROW + narrow_index * CLUSTERS, 8)
    own_skel = strip[pl.ds(own_start, CLUSTERS), :]
    own_chosen = as_bf16(iota((CLUSTERS, LANES), 0) == target)
    targets = parts_dot(own_skel, own_chosen, over_rows)
    rows = []
    for a in range(R):
        square = soft_square
        for axis in range(3):
            offset = sources[axis * R : (axis + 1) * R] - targets[axis * R + a : axis * R + a + 1]
            square = square + offset * offset
        product = lax.rsqrt(square) * sources[3 * R :]
        rows.append(jnp.sum(product, axis=0, keepdims=True))
    middle = jnp.where(live, jnp.concatenate(rows, axis=0) * kernel_scale, 0.0)
    for cluster in range(CLUSTERS):
        column = jnp.sum(jnp.where(target == cluster, middle, 0.0), axis=1, keepdims=True)
        spread = jnp.sum(
            target_basis[:, cluster * C : (cluster + 1) * C] * column, axis=0, keepdims=True
        )
        for half in range(2):
            row = 2 * cluster + half
            total[row : row + 1, :] = (
                near[row : row + 1, :] + spread[:, half * LANES : (half + 1) * LANES]
            )
    low = order[...] & (LANES - 1)
    high = order[...] >> 7
    tall = iota((LANES, LANES), 0)
    wide = iota((ROWS, LANES), 0)
    whole = [part.astype(f32) for part in split3(total[...])]
    values, places = [], []
    for row in range(ROWS):
        here = wide == high[row : row + 1]
        parts = [jnp.where(here, part[row : row + 1, :], 0.0) for part in whole]
        values.append(jnp.concatenate(parts, axis=0).astype(bf16))
        places.append(as_bf16(tall == low[row : row + 1]))
    placed = lax.dot_general(
        jnp.concatenate(values, axis=1),
        jnp.concatenate(places, axis=1),
        (((1,), (1,)), ((), ())),
        preferred_element_type=f32,
    )
    out = placed[:ROWS] + placed[ROWS : 2 * ROWS] + placed[2 * ROWS :]
    potential[...] = out


def smem():
    return pl.BlockSpec(memory_space=pltpu.SMEM)


def in_hbm():
    return pl.BlockSpec(memory_space=pltpu.HBM)


def vmem():
    return pl.BlockSpec(memory_space=pltpu.VMEM)


params = pltpu.CompilerParams(vmem_limit_bytes=50 * 1024 * 1024)
first_params = pltpu.CompilerParams(vmem_limit_bytes=127 * 512 * 1024)


def local(
    points,
    charges,
    order,
    source_basis,
    target_basis,
    skeleton_points,
    transfer,
    top_points,
    near_pairs,
    near_count,
    far_pairs,
    far_count,
):
    wide_size = lax.axis_size("wide")
    narrow_size = lax.axis_size("narrow")
    place = jnp.stack([lax.axis_index("wide"), lax.axis_index("narrow")]).astype(i32)
    order = order.reshape(ROWS, LANES)
    shape = jax.ShapeDtypeStruct
    inputs = (
        order,
        points,
        charges.reshape(ROWS, LANES),
        near_pairs,
        source_basis,
        transfer,
        skeleton_points,
        top_points,
    )
    with jax.named_scope("slots"):
        own, skel = pl.pallas_call(
            slots_kernel,
            out_shape=(
                shape((136, LANES), f32),
                shape((NARROW, SKEL_REC, LANES), f32),
            ),
            in_specs=[smem()] + [in_hbm()] * len(inputs),
            out_specs=[vmem()] * 2,
            scratch_shapes=[pltpu.VMEM(x.shape, x.dtype) for x in inputs]
            + [pltpu.SemaphoreType.DMA((len(inputs),))],
            compiler_params=first_params,
        )(near_count, *inputs)
    skels = lax.all_to_all(skel, "narrow", 0, 0, tiled=True)
    from_down = lax.ppermute(own, "narrow", [(i, i + 1) for i in range(narrow_size - 1)])
    from_up = lax.ppermute(own, "narrow", [(i + 1, i) for i in range(narrow_size - 1)])
    with jax.named_scope("top"):
        top_message = pl.pallas_call(
            top_kernel,
            out_shape=shape((TOP_ROWS * wide_size, LANES), f32),
            in_specs=[vmem()],
            out_specs=vmem(),
            compiler_params=params,
        )(skels)
    tops = lax.all_to_all(top_message, "wide", 0, 0, tiled=True)
    with jax.named_scope("strip"):
        strip = pl.pallas_call(
            strip_kernel,
            out_shape=shape((STRIP_ROWS, LANES), f32),
            in_specs=[vmem()] * 5,
            out_specs=vmem(),
            compiler_params=params,
        )(skels, from_down, own, from_up, top_message)
    before = lax.ppermute(strip, "wide", [(i, i + 1) for i in range(wide_size - 1)])
    after = lax.ppermute(strip, "wide", [(i + 1, i) for i in range(wide_size - 1)])
    with jax.named_scope("self"):
        lhs, self_rows = pl.pallas_call(
            self_kernel,
            out_shape=(shape((CLUSTERS, C, DEPTH), bf16), shape((ROWS, LANES), f32)),
            in_specs=[vmem()],
            out_specs=[vmem()] * 2,
            scratch_shapes=[pltpu.VMEM((2, C, LANES), f32)],
            compiler_params=params,
        )(strip)
    with jax.named_scope("near"):
        near = pl.pallas_call(
            near_kernel,
            out_shape=shape((ROWS, LANES), f32),
            in_specs=[smem()] + [vmem()] * 5,
            out_specs=vmem(),
            scratch_shapes=[
                pltpu.VMEM((WINDOW + 1, DEPTH, C), bf16),
                pltpu.VMEM((WINDOW + 1, 8, C), f32),
                pltpu.VMEM((8, LANES), i32),
                pltpu.SMEM((8, LANES), i32),
                pltpu.SemaphoreType.DMA(()),
            ]
            + [pltpu.VMEM((CLUSTERS, C, LANES), f32)] * SUMS,
            compiler_params=params,
        )(place, before, strip, after, lhs, self_rows)
    with jax.named_scope("far"):
        potential = pl.pallas_call(
            far_kernel,
            out_shape=shape((ROWS, LANES), f32),
            in_specs=[smem(), smem()] + [vmem()] * 8,
            out_specs=vmem(),
            scratch_shapes=[pltpu.VMEM((ROWS, LANES), f32)],
            compiler_params=params,
        )(place, far_count, before, strip, after, tops, far_pairs, near, order, target_basis)
    return potential.reshape(-1)


def solution(mesh):
    both = ("wide", "narrow")
    split = P(None, both)
    return jax.shard_map(
        local,
        mesh=mesh,
        in_specs=(
            split,
            P(both),
            P(both),
            split,
            split,
            split,
            split,
            P(None, "wide"),
            split,
            P(both),
            split,
            P(both),
        ),
        out_specs=P(both),
        check_vma=False,
    )
```

```python
import jax
import jax.numpy as jnp
from jax import lax
from jax.experimental import pallas as pl
from jax.experimental.pallas import tpu as pltpu
from jax.sharding import PartitionSpec as P

C = 256
R = 32
LANES = 128
CLUSTERS = 16
ROWS = 32
NARROW = 8
GROUP = 128
WIDTH = 8
STRIP_CLUSTERS = 32
PAIR_ROW = 8 * STRIP_CLUSTERS
SKEL_ROW = PAIR_ROW + 24
STRIP_ROWS = SKEL_ROW + GROUP
SKEL_REC = 24
TOP_ROWS = 2
OUTER = 2 * STRIP_CLUSTERS
SELF = STRIP_CLUSTERS + 1
DEPTH = 48
UNROLL = 8
SUMS = 2
CHUNK = 64

soft_square = 0.01
kernel_scale = 0.07957747154594767
f32 = jnp.float32
bf16 = jnp.bfloat16
i32 = jnp.int32


def iota(shape, dim):
    return lax.broadcasted_iota(i32, shape, dim)


def split3(x):
    high = x.astype(bf16)
    rest = x - high.astype(f32)
    mid = rest.astype(bf16)
    low = (rest - mid.astype(f32)).astype(bf16)
    return high, mid, low


def parts_dot(x, ones, dims):
    dots = [
        lax.dot_general(part, ones, (dims, ((), ())), preferred_element_type=f32)
        for part in split3(x)
    ]
    return dots[0] + dots[1] + dots[2]


def as_bf16(mask):
    return mask.astype(f32).astype(bf16)


def slots_kernel(near_count, *refs):
    count = 8
    own, skel_out = refs[count : count + 2]
    held = refs[count + 2 : 2 * count + 2]
    semaphores = refs[2 * count + 2]
    copies = [
        pltpu.make_async_copy(refs[i], held[i], semaphores.at[i]) for i in range(count)
    ]
    for copy in copies:
        copy.start()
    order, points, charges, near_pairs, source_basis, transfer, skeleton_points, top_points = held
    for copy in copies[:4]:
        copy.wait()
    low = order[...] & (LANES - 1)
    high = order[...] >> 7
    sub = iota((8, LANES), 0)
    tables = []
    for row in range(ROWS):
        xyz = points[:, row * LANES : (row + 1) * LANES]
        charge = charges[row : row + 1, :]
        tables.append(jnp.concatenate([xyz, charge, xyz, charge], axis=0))
    tiles = []
    for tile in range(CLUSTERS):
        first = 4 * (tile // 2) + tile % 2
        low_tile = jnp.where(sub < 4, low[first : first + 1], low[first + 2 : first + 3])
        high_tile = jnp.where(sub < 4, high[first : first + 1], high[first + 2 : first + 3])
        values = jnp.zeros((8, LANES), f32)
        for row in range(ROWS):
            found = jnp.take_along_axis(tables[row], low_tile, axis=1)
            values = jnp.where(high_tile == row, found, values)
        own[8 * tile : 8 * tile + 8, :] = values
        tiles.append(values)

    pairs = jnp.where(iota((2, 64), 1) < near_count[0], near_pairs[...] + 1, 0).astype(f32)
    own[128:136, :] = jnp.zeros((8, LANES), f32)
    own[128:130, 0:64] = pairs
    for copy in copies[4:]:
        copy.wait()

    lane = iota((R, LANES), 1)
    skel = jnp.zeros((R, LANES), f32)
    for cluster in range(CLUSTERS):
        block, place = cluster // 2, 4 * (cluster % 2) + 3
        basis = source_basis[:, cluster * C : (cluster + 1) * C]
        product = (
            basis[:, :LANES] * tiles[2 * block][place : place + 1]
            + basis[:, LANES:] * tiles[2 * block + 1][place : place + 1]
        )
        skel = jnp.where(lane == cluster, jnp.sum(product, axis=1, keepdims=True), skel)
    skel_rows = skel.T[:CLUSTERS, :]
    long_lane = iota((R, CLUSTERS * R), 1)
    repeat = as_bf16(long_lane % R == iota((R, CLUSTERS * R), 0))
    tiled = parts_dot(skel_rows, repeat, ((1,), (0,)))
    mine = iota((CLUSTERS, CLUSTERS * R), 1) // R == iota((CLUSTERS, CLUSTERS * R), 0)
    flat = jnp.sum(jnp.where(mine, tiled, 0.0), axis=0, keepdims=True)
    partial = jnp.sum(transfer[...] * flat, axis=1, keepdims=True)
    skel = jnp.where(lane == CLUSTERS, partial, skel)
    to_charge = as_bf16(lane == iota((R, LANES), 0) + 3 * R)
    record = parts_dot(skel.T[:SKEL_REC, :], to_charge, ((1,), (0,)))
    fold = as_bf16(iota((CLUSTERS * R, LANES), 1) % R == iota((CLUSTERS * R, LANES), 0) % R)
    short_lane = iota((CLUSTERS, LANES), 1) // R
    geometry = jnp.zeros((CLUSTERS, LANES), f32)
    for axis in range(3):
        masked = jnp.where(mine, skeleton_points[axis : axis + 1, :], 0.0)
        folded = parts_dot(masked, fold, ((1,), (0,)))
        geometry = jnp.where(short_lane == axis, folded, geometry)
    spread = as_bf16(lane % R == iota((R, LANES), 0))
    top = parts_dot(top_points[...], spread, ((1,), (0,)))
    top_mine = iota((3, LANES), 1) // R == iota((3, LANES), 0)
    top_row = jnp.sum(jnp.where(top_mine, top, 0.0), axis=0, keepdims=True)
    last = jnp.where(iota((8, LANES), 0) == 1, top_row, 0.0)
    record = record + jnp.concatenate([geometry, last], axis=0)
    for device in range(NARROW):
        skel_out[device] = record


def top_kernel(skels, top_message):
    last = skels[0, CLUSTERS:SKEL_REC, :]
    row = last[0:1] + last[1:2]
    for device in range(1, NARROW):
        row = row + skels[device, CLUSTERS:SKEL_REC, :][0:1]
    top_message[...] = jnp.broadcast_to(row, top_message.shape)


def strip_kernel(skels, from_down, own, from_up, top_message, strip):
    del top_message
    strip[0:64, :] = from_down[64:128, :]
    strip[64:192, :] = own[0:128, :]
    strip[192:256, :] = from_up[0:64, :]
    strip[PAIR_ROW : PAIR_ROW + 8, :] = from_down[128:136, :]
    strip[PAIR_ROW + 8 : PAIR_ROW + 16, :] = own[128:136, :]
    strip[PAIR_ROW + 16 : PAIR_ROW + 24, :] = from_up[128:136, :]
    for device in range(NARROW):
        start = SKEL_ROW + device * CLUSTERS
        strip[start : start + CLUSTERS, :] = skels[device, :CLUSTERS, :]


def with_norms(halves, origin):
    out = []
    for half in halves:
        sub = iota((8, LANES), 0)
        shifted = jnp.where(sub < 3, half - origin, 0.0)
        norms = jnp.sum(shifted * shifted, axis=0, keepdims=True)
        out.append((shifted, norms))
    return out


def source_features(halves, origin):
    sub = iota((8, LANES), 0)
    columns = []
    for shifted, norms in with_norms(halves, origin):
        rows = jnp.where(sub < 3, shifted, jnp.where(sub == 4, norms, 0.0))
        rows = jnp.where(sub == 5, 1.0, rows)
        high, mid, low = [part.astype(f32) for part in split3(rows)]
        columns.append(jnp.concatenate([high, mid, high, mid, low, high], axis=0).astype(bf16))
    return jnp.concatenate(columns, axis=1)


def target_features(halves, origin):
    sub = iota((8, LANES), 0)
    columns = []
    for shifted, norms in with_norms(halves, origin):
        rows = jnp.where(sub < 3, -2.0 * shifted, jnp.where(sub == 5, norms + soft_square, 0.0))
        rows = jnp.where(sub == 4, 1.0, rows)
        high, mid, low = [part.astype(f32) for part in split3(rows)]
        columns.append(jnp.concatenate([high, high, mid, mid, high, low], axis=0))
    return columns


def cluster_halves(ref, block, odd):
    halves = []
    for half in range(2):
        tile = ref[pl.ds(pl.multiple_of(16 * block + 8 * half, 8), 8), :]
        halves.append(pltpu.roll(tile, 4, 0) if odd else tile)
    return halves


def own_origin(ref, start):
    whole = jnp.zeros((8, LANES), f32)
    for tile in range(CLUSTERS):
        whole = whole + ref[start + 8 * tile : start + 8 * tile + 8, :]
    mean = jnp.sum(whole, axis=1, keepdims=True) * (1.0 / (CLUSTERS * C))
    mean = jnp.broadcast_to(mean, (8, LANES))
    return jnp.where(iota((8, LANES), 0) < 3, mean + pltpu.roll(mean, 4, 0), 0.0)


def kernel_sums(square, charge_low, charge_high):
    inverse = lax.rsqrt(jnp.maximum(square, soft_square))
    return inverse[:, :LANES] * charge_low + inverse[:, LANES:] * charge_high


def put_source(features, charge, slot, halves, origin):
    features[slot] = source_features(halves, origin)
    for half in range(2):
        row = halves[half][3:4]
        charge[slot, :, half * LANES : (half + 1) * LANES] = jnp.broadcast_to(row, (8, LANES))


def pair_rows(refs):
    targets, sources = [], []
    for ref in refs:
        for block in range(3):
            start = PAIR_ROW + 8 * block
            targets.append(ref[start : start + 1, :])
            sources.append(ref[start + 1 : start + 2, :])
    return targets, sources


def list_entries(place, own_rows, other_rows, inner, out):
    wide_index = place[0]
    narrow_index = place[1]
    count_rows = len(own_rows)
    base = (wide_index * GROUP + narrow_index * CLUSTERS + 1).astype(f32)
    nothing = [jnp.zeros((16 - count_rows, LANES), f32)]
    own_ids = jnp.concatenate(own_rows + nothing, axis=0)
    other_ids = jnp.concatenate(other_rows + nothing, axis=0)
    local = own_ids - base
    other = other_ids - 1.0
    group = jnp.floor(other * (1.0 / GROUP))
    rest = other - GROUP * group
    depth = jnp.floor(rest * (1.0 / WIDTH))
    column = rest - WIDTH * depth
    group_step = group - (wide_index - 1).astype(f32)
    depth_step = depth - (2 * narrow_index - 1).astype(f32)
    slot = depth_step * WIDTH + column
    if inner:
        wanted = group_step == 1.0
    else:
        wanted = group_step != 1.0
        slot = jnp.where(group_step > 1.0, slot + STRIP_CLUSTERS, slot)
    used = wanted & (local >= 0.0) & (local < CLUSTERS) & (own_ids > 0.0)
    count = used.astype(f32)
    upto = as_bf16(iota((LANES, LANES), 0) <= iota((LANES, LANES), 1))
    inclusive = jnp.dot(count.astype(bf16), upto, preferred_element_type=f32)
    totals = jnp.sum(count, axis=1, keepdims=True)
    row_of = iota((16, LANES), 0)
    offset = jnp.zeros((16, LANES), f32)
    for row in range(count_rows):
        offset = jnp.where(row_of > row, offset + totals[row : row + 1], offset)
    spot = jnp.where(used, inclusive - count + offset, -1.0)
    slot = jnp.where(used, slot, 0.0)
    local = jnp.where(used, local, 0.0)
    spot_high = jnp.floor(spot * (1.0 / LANES))
    spot_low = spot - LANES * spot_high
    listed = jnp.zeros((16, LANES), f32)
    eight = iota((8, LANES), 0).astype(f32)
    tall = iota((LANES, LANES), 0).astype(f32)
    for row in range(count_rows):
        here = eight == spot_high[row : row + 1]
        values = jnp.concatenate(
            [
                jnp.where(here, local[row : row + 1], 0.0),
                jnp.where(here, slot[row : row + 1], 0.0),
            ],
            axis=0,
        ).astype(bf16)
        hot = as_bf16(tall == spot_low[row : row + 1])
        listed = listed + lax.dot_general(
            values, hot, (((1,), (1,)), ((), ())), preferred_element_type=f32
        )
    coded = listed[:8] * float(GROUP) + listed[8:]
    out[...] = jnp.where(eight == 7.0, jnp.sum(totals), coded).astype(i32)


def add_pairs(entries, lhs, features, charge, dummy, sums):
    pair_total = entries[7, 0]

    def pair_steps(first, turns, carry):
        for turn in range(turns):
            index = first + turn
            code = entries[index >> 7, index & (LANES - 1)]
            live = index < pair_total
            cluster = jnp.where(live, code >> 7, 0)
            slot = jnp.where(live, code & (LANES - 1), dummy)
            right = features[slot]
            charge_low = charge[slot, 0:1, 0:LANES]
            charge_high = charge[slot, 0:1, LANES:C]
            for start in range(0, C, CHUNK):
                square = jnp.dot(
                    lhs[cluster, start : start + CHUNK, :], right, preferred_element_type=f32
                )
                sums[turn % SUMS][cluster, start : start + CHUNK, :] += kernel_sums(
                    square, charge_low, charge_high
                )
        return carry

    steps = (pair_total + UNROLL - 1) // UNROLL
    lax.fori_loop(
        0, steps // 2, lambda step, carry: pair_steps(2 * UNROLL * step, 2 * UNROLL, carry), 0
    )
    lax.fori_loop(
        2 * (steps // 2), steps, lambda step, carry: pair_steps(UNROLL * step, UNROLL, carry), 0
    )


def summed_row(sums, cluster, half):
    rows = slice(half * LANES, (half + 1) * LANES)
    total = sums[0][cluster, rows, :] + sums[1][cluster, rows, :]
    return kernel_scale * jnp.sum(total.T, axis=0, keepdims=True)


def inner_kernel(
    place, strip, lhs, near, features, charge, listed, entries, semaphore, *rest
):
    first_sum, second_sum, own_lhs = rest
    targets, sources = pair_rows((strip,))
    list_entries(place, sources + [targets[1]], targets + [sources[1]], True, listed)
    copy = pltpu.make_async_copy(listed, entries, semaphore)
    copy.start()
    origin = own_origin(strip, 64)

    def own_step(block, carry):
        for odd in range(2):
            cluster = 2 * block + odd
            halves = cluster_halves(strip, block + 4, odd)
            for half, column in enumerate(target_features(halves, origin)):
                lhs[cluster, half * LANES : (half + 1) * LANES, :] = column.T.astype(bf16)
            centre = jnp.sum(halves[0] + halves[1], axis=1, keepdims=True) * (1.0 / C)
            for half, column in enumerate(target_features(halves, centre)):
                own_lhs[cluster, :, half * LANES : (half + 1) * LANES] = column.astype(bf16)
            put_source(features, charge, SELF + cluster, halves, centre)
        return carry

    lax.fori_loop(0, CLUSTERS // 2, own_step, 0, unroll=4)

    def strip_step(block, carry):
        for odd in range(2):
            put_source(features, charge, 2 * block + odd, cluster_halves(strip, block, odd), origin)
        return carry

    lax.fori_loop(0, STRIP_CLUSTERS // 2, strip_step, 0, unroll=2)
    features[STRIP_CLUSTERS] = jnp.zeros((DEPTH, C), bf16)
    charge[STRIP_CLUSTERS] = jnp.zeros((8, C), f32)

    def self_step(step, carry):
        for turn in range(UNROLL):
            cluster = step * UNROLL + turn
            square = lax.dot_general(
                own_lhs[cluster],
                features[SELF + cluster],
                (((0,), (0,)), ((), ())),
                preferred_element_type=f32,
            )
            first_sum[cluster] = kernel_sums(
                square,
                charge[SELF + cluster, 0:1, 0:LANES],
                charge[SELF + cluster, 0:1, LANES:C],
            )
            second_sum[cluster] = jnp.zeros((C, LANES), f32)
        return carry

    lax.fori_loop(0, CLUSTERS // UNROLL, self_step, 0)
    copy.wait()
    add_pairs(entries, lhs, features, charge, STRIP_CLUSTERS, (first_sum, second_sum))
    for cluster in range(CLUSTERS):
        for half in range(2):
            row = 2 * cluster + half
            near[row : row + 1, :] = summed_row((first_sum, second_sum), cluster, half)


def outer_kernel(
    place,
    before,
    strip,
    after,
    lhs,
    inner,
    near,
    features,
    charge,
    listed,
    entries,
    semaphore,
    *sums,
):
    targets, sources = pair_rows((before, after))
    own_targets, own_sources = pair_rows((strip,))
    list_entries(
        place, sources + [own_targets[1]], targets + [own_sources[1]], False, listed
    )
    copy = pltpu.make_async_copy(listed, entries, semaphore)
    copy.start()
    for total in sums:
        total[...] = jnp.zeros(total.shape, f32)
    origin = own_origin(strip, 64)

    def window_step(block, carry):
        for part, ref in enumerate((before, after)):
            for odd in range(2):
                slot = part * STRIP_CLUSTERS + 2 * block + odd
                put_source(features, charge, slot, cluster_halves(ref, block, odd), origin)
        return carry

    lax.fori_loop(0, STRIP_CLUSTERS // 2, window_step, 0, unroll=2)
    features[OUTER] = jnp.zeros((DEPTH, C), bf16)
    charge[OUTER] = jnp.zeros((8, C), f32)
    copy.wait()
    add_pairs(entries, lhs, features, charge, OUTER, sums)
    for cluster in range(CLUSTERS):
        for half in range(2):
            row = 2 * cluster + half
            near[row : row + 1, :] = inner[row : row + 1, :] + summed_row(sums, cluster, half)


def far_kernel(
    place,
    far_count,
    before,
    strip,
    after,
    top,
    far_pairs,
    near,
    order,
    target_basis,
    potential,
    total,
):
    wide_index = place[0]
    narrow_index = place[1]
    first = wide_index * GROUP + narrow_index * CLUSTERS
    target = far_pairs[0:1, :] - first
    source = far_pairs[1:2, :]
    is_leaf = far_pairs[2:3, :] == 0
    live = iota((1, LANES), 1) < far_count[0]
    index = jnp.where(is_leaf, source - (wide_index - 1) * GROUP, source + 3 * GROUP)
    skel = slice(SKEL_ROW, SKEL_ROW + GROUP)
    tops = top[pl.ds(0, top.shape[0] // TOP_ROWS, stride=TOP_ROWS), :]
    table = jnp.concatenate([before[skel, :], strip[skel, :], after[skel, :], tops], axis=0)
    chosen = as_bf16(iota((table.shape[0], LANES), 0) == index)
    over_rows = ((0,), (0,))
    sources = parts_dot(table, chosen, over_rows)
    own_start = pl.multiple_of(SKEL_ROW + narrow_index * CLUSTERS, 8)
    own_skel = strip[pl.ds(own_start, CLUSTERS), :]
    own_chosen = as_bf16(iota((CLUSTERS, LANES), 0) == target)
    targets = parts_dot(own_skel, own_chosen, over_rows)
    rows = []
    for a in range(R):
        square = soft_square
        for axis in range(3):
            offset = sources[axis * R : (axis + 1) * R] - targets[axis * R + a : axis * R + a + 1]
            square = square + offset * offset
        product = lax.rsqrt(square) * sources[3 * R :]
        rows.append(jnp.sum(product, axis=0, keepdims=True))
    middle = jnp.where(live, jnp.concatenate(rows, axis=0) * kernel_scale, 0.0)
    for cluster in range(CLUSTERS):
        column = jnp.sum(jnp.where(target == cluster, middle, 0.0), axis=1, keepdims=True)
        spread = jnp.sum(
            target_basis[:, cluster * C : (cluster + 1) * C] * column, axis=0, keepdims=True
        )
        for half in range(2):
            row = 2 * cluster + half
            total[row : row + 1, :] = (
                near[row : row + 1, :] + spread[:, half * LANES : (half + 1) * LANES]
            )
    low = order[...] & (LANES - 1)
    high = order[...] >> 7
    tall = iota((LANES, LANES), 0)
    wide = iota((ROWS, LANES), 0)
    whole = [part.astype(f32) for part in split3(total[...])]
    values, places = [], []
    for row in range(ROWS):
        here = wide == high[row : row + 1]
        parts = [jnp.where(here, part[row : row + 1, :], 0.0) for part in whole]
        values.append(jnp.concatenate(parts, axis=0).astype(bf16))
        places.append(as_bf16(tall == low[row : row + 1]))
    placed = lax.dot_general(
        jnp.concatenate(values, axis=1),
        jnp.concatenate(places, axis=1),
        (((1,), (1,)), ((), ())),
        preferred_element_type=f32,
    )
    out = placed[:ROWS] + placed[ROWS : 2 * ROWS] + placed[2 * ROWS :]
    potential[...] = out


def smem():
    return pl.BlockSpec(memory_space=pltpu.SMEM)


def in_hbm():
    return pl.BlockSpec(memory_space=pltpu.HBM)


def vmem():
    return pl.BlockSpec(memory_space=pltpu.VMEM)


params = pltpu.CompilerParams(vmem_limit_bytes=50 * 1024 * 1024)
first_params = pltpu.CompilerParams(vmem_limit_bytes=127 * 512 * 1024)


def local(
    points,
    charges,
    order,
    source_basis,
    target_basis,
    skeleton_points,
    transfer,
    top_points,
    near_pairs,
    near_count,
    far_pairs,
    far_count,
):
    wide_size = lax.axis_size("wide")
    narrow_size = lax.axis_size("narrow")
    place = jnp.stack([lax.axis_index("wide"), lax.axis_index("narrow")]).astype(i32)
    order = order.reshape(ROWS, LANES)
    shape = jax.ShapeDtypeStruct
    inputs = (
        order,
        points,
        charges.reshape(ROWS, LANES),
        near_pairs,
        source_basis,
        transfer,
        skeleton_points,
        top_points,
    )
    with jax.named_scope("slots"):
        own, skel = pl.pallas_call(
            slots_kernel,
            out_shape=(
                shape((136, LANES), f32),
                shape((NARROW, SKEL_REC, LANES), f32),
            ),
            in_specs=[smem()] + [in_hbm()] * len(inputs),
            out_specs=[vmem()] * 2,
            scratch_shapes=[pltpu.VMEM(x.shape, x.dtype) for x in inputs]
            + [pltpu.SemaphoreType.DMA((len(inputs),))],
            compiler_params=first_params,
        )(near_count, *inputs)
    skels = lax.all_to_all(skel, "narrow", 0, 0, tiled=True)
    from_down = lax.ppermute(own, "narrow", [(i, i + 1) for i in range(narrow_size - 1)])
    from_up = lax.ppermute(own, "narrow", [(i + 1, i) for i in range(narrow_size - 1)])
    with jax.named_scope("top"):
        top_message = pl.pallas_call(
            top_kernel,
            out_shape=shape((TOP_ROWS * wide_size, LANES), f32),
            in_specs=[vmem()],
            out_specs=vmem(),
            compiler_params=params,
        )(skels)
    tops = lax.all_to_all(top_message, "wide", 0, 0, tiled=True)
    with jax.named_scope("strip"):
        strip = pl.pallas_call(
            strip_kernel,
            out_shape=shape((STRIP_ROWS, LANES), f32),
            in_specs=[vmem()] * 5,
            out_specs=vmem(),
            compiler_params=params,
        )(skels, from_down, own, from_up, top_message)
    before = lax.ppermute(strip, "wide", [(i, i + 1) for i in range(wide_size - 1)])
    after = lax.ppermute(strip, "wide", [(i + 1, i) for i in range(wide_size - 1)])
    def near_scratch(slots):
        return [
            pltpu.VMEM((slots, DEPTH, C), bf16),
            pltpu.VMEM((slots, 8, C), f32),
            pltpu.VMEM((8, LANES), i32),
            pltpu.SMEM((8, LANES), i32),
            pltpu.SemaphoreType.DMA(()),
        ] + [pltpu.VMEM((CLUSTERS, C, LANES), f32)] * SUMS

    with jax.named_scope("inner"):
        lhs, inner = pl.pallas_call(
            inner_kernel,
            out_shape=(shape((CLUSTERS, C, DEPTH), bf16), shape((ROWS, LANES), f32)),
            in_specs=[smem(), vmem()],
            out_specs=[vmem()] * 2,
            scratch_shapes=near_scratch(SELF + CLUSTERS)
            + [pltpu.VMEM((CLUSTERS, DEPTH, C), bf16)],
            compiler_params=params,
        )(place, strip)
    with jax.named_scope("outer"):
        near = pl.pallas_call(
            outer_kernel,
            out_shape=shape((ROWS, LANES), f32),
            in_specs=[smem()] + [vmem()] * 5,
            out_specs=vmem(),
            scratch_shapes=near_scratch(OUTER + 1),
            compiler_params=params,
        )(place, before, strip, after, lhs, inner)
    with jax.named_scope("far"):
        potential = pl.pallas_call(
            far_kernel,
            out_shape=shape((ROWS, LANES), f32),
            in_specs=[smem(), smem()] + [vmem()] * 8,
            out_specs=vmem(),
            scratch_shapes=[pltpu.VMEM((ROWS, LANES), f32)],
            compiler_params=params,
        )(place, far_count, before, strip, after, tops, far_pairs, near, order, target_basis)
    return potential.reshape(-1)


def solution(mesh):
    both = ("wide", "narrow")
    split = P(None, both)
    return jax.shard_map(
        local,
        mesh=mesh,
        in_specs=(
            split,
            P(both),
            P(both),
            split,
            split,
            split,
            split,
            P(None, "wide"),
            split,
            P(both),
            split,
            P(both),
        ),
        out_specs=P(both),
        check_vma=False,
    )
```

```python
import jax
import jax.numpy as jnp
from jax import lax
from jax.experimental import pallas as pl
from jax.experimental.pallas import tpu as pltpu
from jax.sharding import PartitionSpec as P

C = 256
R = 32
LANES = 128
CLUSTERS = 16
ROWS = 32
NARROW = 8
GROUP = 128
WIDTH = 8
STRIP_CLUSTERS = 32
PAIR_ROW = 8 * STRIP_CLUSTERS
SKEL_ROW = PAIR_ROW + 24
STRIP_ROWS = SKEL_ROW + GROUP
SKEL_REC = 24
TOP_ROWS = 2
OUTER = 2 * STRIP_CLUSTERS
SELF = STRIP_CLUSTERS + 1
DEPTH = 48
UNROLL = 8
SUMS = 2
CHUNK = 64

soft_square = 0.01
kernel_scale = 0.07957747154594767
f32 = jnp.float32
bf16 = jnp.bfloat16
i32 = jnp.int32


def iota(shape, dim):
    return lax.broadcasted_iota(i32, shape, dim)


def split3(x):
    high = x.astype(bf16)
    rest = x - high.astype(f32)
    mid = rest.astype(bf16)
    low = (rest - mid.astype(f32)).astype(bf16)
    return high, mid, low


def parts_dot(x, ones, dims):
    dots = [
        lax.dot_general(part, ones, (dims, ((), ())), preferred_element_type=f32)
        for part in split3(x)
    ]
    return dots[0] + dots[1] + dots[2]


def as_bf16(mask):
    return mask.astype(f32).astype(bf16)


def slots_kernel(near_count, *refs):
    count = 8
    own, skel_out = refs[count : count + 2]
    held = refs[count + 2 : 2 * count + 2]
    semaphores = refs[2 * count + 2]
    copies = [
        pltpu.make_async_copy(refs[i], held[i], semaphores.at[i]) for i in range(count)
    ]
    for copy in copies:
        copy.start()
    order, points, charges, near_pairs = held[:4]
    source_basis, transfer, skeleton_points, top_points = held[4:]
    for copy in copies[:4]:
        copy.wait()
    low = order[...] & (LANES - 1)
    high = order[...] >> 7
    sub = iota((8, LANES), 0)
    tables = []
    for row in range(ROWS):
        xyz = points[:, row * LANES : (row + 1) * LANES]
        charge = charges[row : row + 1, :]
        tables.append(jnp.concatenate([xyz, charge, xyz, charge], axis=0))
    tiles = []
    for tile in range(CLUSTERS):
        first = 4 * (tile // 2) + tile % 2
        low_tile = jnp.where(sub < 4, low[first : first + 1], low[first + 2 : first + 3])
        high_tile = jnp.where(sub < 4, high[first : first + 1], high[first + 2 : first + 3])
        values = jnp.zeros((8, LANES), f32)
        for row in range(ROWS):
            found = jnp.take_along_axis(tables[row], low_tile, axis=1)
            values = jnp.where(high_tile == row, found, values)
        own[8 * tile : 8 * tile + 8, :] = values
        tiles.append(values)

    pairs = jnp.where(iota((2, 64), 1) < near_count[0], near_pairs[...] + 1, 0).astype(f32)
    own[128:136, :] = jnp.zeros((8, LANES), f32)
    own[128:130, 0:64] = pairs
    for copy in copies[4:]:
        copy.wait()

    lane = iota((R, LANES), 1)
    skel = jnp.zeros((R, LANES), f32)
    for cluster in range(CLUSTERS):
        block, place = cluster // 2, 4 * (cluster % 2) + 3
        basis = source_basis[:, cluster * C : (cluster + 1) * C]
        product = (
            basis[:, :LANES] * tiles[2 * block][place : place + 1]
            + basis[:, LANES:] * tiles[2 * block + 1][place : place + 1]
        )
        skel = jnp.where(lane == cluster, jnp.sum(product, axis=1, keepdims=True), skel)
    skel_rows = skel.T[:CLUSTERS, :]
    long_lane = iota((R, CLUSTERS * R), 1)
    repeat = as_bf16(long_lane % R == iota((R, CLUSTERS * R), 0))
    tiled = parts_dot(skel_rows, repeat, ((1,), (0,)))
    mine = iota((CLUSTERS, CLUSTERS * R), 1) // R == iota((CLUSTERS, CLUSTERS * R), 0)
    flat = jnp.sum(jnp.where(mine, tiled, 0.0), axis=0, keepdims=True)
    partial = jnp.sum(transfer[...] * flat, axis=1, keepdims=True)
    skel = jnp.where(lane == CLUSTERS, partial, skel)
    to_charge = as_bf16(lane == iota((R, LANES), 0) + 3 * R)
    record = parts_dot(skel.T[:SKEL_REC, :], to_charge, ((1,), (0,)))
    fold = as_bf16(iota((CLUSTERS * R, LANES), 1) % R == iota((CLUSTERS * R, LANES), 0) % R)
    short_lane = iota((CLUSTERS, LANES), 1) // R
    geometry = jnp.zeros((CLUSTERS, LANES), f32)
    for axis in range(3):
        masked = jnp.where(mine, skeleton_points[axis : axis + 1, :], 0.0)
        folded = parts_dot(masked, fold, ((1,), (0,)))
        geometry = jnp.where(short_lane == axis, folded, geometry)
    spread = as_bf16(lane % R == iota((R, LANES), 0))
    top = parts_dot(top_points[...], spread, ((1,), (0,)))
    top_mine = iota((3, LANES), 1) // R == iota((3, LANES), 0)
    top_row = jnp.sum(jnp.where(top_mine, top, 0.0), axis=0, keepdims=True)
    last = jnp.where(iota((8, LANES), 0) == 1, top_row, 0.0)
    record = record + jnp.concatenate([geometry, last], axis=0)
    for device in range(NARROW):
        skel_out[device] = record


def top_kernel(skels, top_message):
    last = skels[0, CLUSTERS:SKEL_REC, :]
    row = last[0:1] + last[1:2]
    for device in range(1, NARROW):
        row = row + skels[device, CLUSTERS:SKEL_REC, :][0:1]
    top_message[...] = jnp.broadcast_to(row, top_message.shape)


def strip_kernel(skels, from_down, own, from_up, top_message, strip):
    del top_message
    strip[0:64, :] = from_down[64:128, :]
    strip[64:192, :] = own[0:128, :]
    strip[192:256, :] = from_up[0:64, :]
    strip[PAIR_ROW : PAIR_ROW + 8, :] = from_down[128:136, :]
    strip[PAIR_ROW + 8 : PAIR_ROW + 16, :] = own[128:136, :]
    strip[PAIR_ROW + 16 : PAIR_ROW + 24, :] = from_up[128:136, :]
    for device in range(NARROW):
        start = SKEL_ROW + device * CLUSTERS
        strip[start : start + CLUSTERS, :] = skels[device, :CLUSTERS, :]


def with_norms(halves, origin):
    out = []
    for half in halves:
        sub = iota((8, LANES), 0)
        shifted = jnp.where(sub < 3, half - origin, 0.0)
        norms = jnp.sum(shifted * shifted, axis=0, keepdims=True)
        out.append((shifted, norms))
    return out


def source_features(halves, origin):
    sub = iota((8, LANES), 0)
    columns = []
    for shifted, norms in with_norms(halves, origin):
        rows = jnp.where(sub < 3, shifted, jnp.where(sub == 4, norms, 0.0))
        rows = jnp.where(sub == 5, 1.0, rows)
        high, mid, low = [part.astype(f32) for part in split3(rows)]
        columns.append(jnp.concatenate([high, mid, high, mid, low, high], axis=0).astype(bf16))
    return jnp.concatenate(columns, axis=1)


def target_features(halves, origin):
    sub = iota((8, LANES), 0)
    columns = []
    for shifted, norms in with_norms(halves, origin):
        rows = jnp.where(sub < 3, -2.0 * shifted, jnp.where(sub == 5, norms + soft_square, 0.0))
        rows = jnp.where(sub == 4, 1.0, rows)
        high, mid, low = [part.astype(f32) for part in split3(rows)]
        columns.append(jnp.concatenate([high, high, mid, mid, high, low], axis=0))
    return columns


def cluster_halves(ref, block, odd):
    halves = []
    for half in range(2):
        tile = ref[pl.ds(pl.multiple_of(16 * block + 8 * half, 8), 8), :]
        halves.append(pltpu.roll(tile, 4, 0) if odd else tile)
    return halves


def own_origin(ref, start):
    whole = jnp.zeros((8, LANES), f32)
    for tile in range(CLUSTERS):
        whole = whole + ref[start + 8 * tile : start + 8 * tile + 8, :]
    mean = jnp.sum(whole, axis=1, keepdims=True) * (1.0 / (CLUSTERS * C))
    mean = jnp.broadcast_to(mean, (8, LANES))
    return jnp.where(iota((8, LANES), 0) < 3, mean + pltpu.roll(mean, 4, 0), 0.0)


def kernel_sums(square, charge_low, charge_high):
    inverse = lax.rsqrt(jnp.maximum(square, soft_square))
    return inverse[:, :LANES] * charge_low + inverse[:, LANES:] * charge_high


def put_source(features, charge, slot, halves, origin):
    features[slot] = source_features(halves, origin)
    for half in range(2):
        row = halves[half][3:4]
        charge[slot, :, half * LANES : (half + 1) * LANES] = jnp.broadcast_to(row, (8, LANES))


def pair_rows(refs):
    targets, sources = [], []
    for ref in refs:
        for block in range(3):
            start = PAIR_ROW + 8 * block
            targets.append(ref[start : start + 1, :])
            sources.append(ref[start + 1 : start + 2, :])
    return targets, sources


def list_entries(place, own_rows, other_rows, inner, out):
    wide_index = place[0:1, 0:1].astype(f32)
    narrow_index = place[0:1, 1:2].astype(f32)
    count_rows = len(own_rows)
    base = wide_index * GROUP + narrow_index * CLUSTERS + 1.0
    nothing = [jnp.zeros((16 - count_rows, LANES), f32)]
    own_ids = jnp.concatenate(own_rows + nothing, axis=0)
    other_ids = jnp.concatenate(other_rows + nothing, axis=0)
    local = own_ids - base
    other = other_ids - 1.0
    group = jnp.floor(other * (1.0 / GROUP))
    rest = other - GROUP * group
    depth = jnp.floor(rest * (1.0 / WIDTH))
    column = rest - WIDTH * depth
    group_step = group - (wide_index - 1.0)
    depth_step = depth - (2.0 * narrow_index - 1.0)
    slot = depth_step * WIDTH + column
    if inner:
        wanted = group_step == 1.0
    else:
        wanted = group_step != 1.0
        odd = wide_index - 2.0 * jnp.floor(0.5 * wide_index)
        second = jnp.where(group_step > 1.0, 1.0 - odd, odd)
        slot = slot + STRIP_CLUSTERS * second
    used = wanted & (local >= 0.0) & (local < CLUSTERS) & (own_ids > 0.0)
    count = used.astype(f32)
    upto = as_bf16(iota((LANES, LANES), 0) <= iota((LANES, LANES), 1))
    inclusive = jnp.dot(count.astype(bf16), upto, preferred_element_type=f32)
    totals = jnp.sum(count, axis=1, keepdims=True)
    row_of = iota((16, LANES), 0)
    offset = jnp.zeros((16, LANES), f32)
    for row in range(count_rows):
        offset = jnp.where(row_of > row, offset + totals[row : row + 1], offset)
    spot = jnp.where(used, inclusive - count + offset, -1.0)
    slot = jnp.where(used, slot, 0.0)
    local = jnp.where(used, local, 0.0)
    spot_high = jnp.floor(spot * (1.0 / LANES))
    spot_low = spot - LANES * spot_high
    listed = jnp.zeros((16, LANES), f32)
    eight = iota((8, LANES), 0).astype(f32)
    tall = iota((LANES, LANES), 0).astype(f32)
    for row in range(count_rows):
        here = eight == spot_high[row : row + 1]
        values = jnp.concatenate(
            [
                jnp.where(here, local[row : row + 1], 0.0),
                jnp.where(here, slot[row : row + 1], 0.0),
            ],
            axis=0,
        ).astype(bf16)
        hot = as_bf16(tall == spot_low[row : row + 1])
        listed = listed + lax.dot_general(
            values, hot, (((1,), (1,)), ((), ())), preferred_element_type=f32
        )
    coded = listed[:8] * float(GROUP) + listed[8:]
    out[...] = jnp.where(eight == 7.0, jnp.sum(totals), coded).astype(i32)


def add_pairs(entries, lhs, features, charge, dummy, sums):
    pair_total = entries[7, 0]

    def pair_steps(first, turns, carry):
        for turn in range(turns):
            index = first + turn
            code = entries[index >> 7, index & (LANES - 1)]
            live = index < pair_total
            cluster = jnp.where(live, code >> 7, 0)
            slot = jnp.where(live, code & (LANES - 1), dummy)
            right = features[slot]
            charge_low = charge[slot, 0:1, 0:LANES]
            charge_high = charge[slot, 0:1, LANES:C]
            for start in range(0, C, CHUNK):
                square = jnp.dot(
                    lhs[cluster, start : start + CHUNK, :], right, preferred_element_type=f32
                )
                sums[turn % SUMS][cluster, start : start + CHUNK, :] += kernel_sums(
                    square, charge_low, charge_high
                )
        return carry

    steps = (pair_total + UNROLL - 1) // UNROLL
    lax.fori_loop(
        0, steps // 2, lambda step, carry: pair_steps(2 * UNROLL * step, 2 * UNROLL, carry), 0
    )
    lax.fori_loop(
        2 * (steps // 2), steps, lambda step, carry: pair_steps(UNROLL * step, UNROLL, carry), 0
    )


def summed_row(sums, cluster, half):
    rows = slice(half * LANES, (half + 1) * LANES)
    total = sums[0][cluster, rows, :] + sums[1][cluster, rows, :]
    return kernel_scale * jnp.sum(total.T, axis=0, keepdims=True)


def inner_kernel(
    place, strip, lhs, near, features, charge, listed, entries, semaphore, *rest
):
    first_sum, second_sum, own_lhs = rest
    targets, sources = pair_rows((strip,))
    list_entries(place, sources + [targets[1]], targets + [sources[1]], True, listed)
    copy = pltpu.make_async_copy(listed, entries, semaphore)
    copy.start()
    origin = own_origin(strip, 64)

    def own_step(block, carry):
        for odd in range(2):
            cluster = 2 * block + odd
            halves = cluster_halves(strip, block + 4, odd)
            for half, column in enumerate(target_features(halves, origin)):
                lhs[cluster, half * LANES : (half + 1) * LANES, :] = column.T.astype(bf16)
            centre = jnp.sum(halves[0] + halves[1], axis=1, keepdims=True) * (1.0 / C)
            for half, column in enumerate(target_features(halves, centre)):
                own_lhs[cluster, :, half * LANES : (half + 1) * LANES] = column.astype(bf16)
            put_source(features, charge, SELF + cluster, halves, centre)
        return carry

    lax.fori_loop(0, CLUSTERS // 2, own_step, 0, unroll=4)

    def strip_step(block, carry):
        for odd in range(2):
            put_source(features, charge, 2 * block + odd, cluster_halves(strip, block, odd), origin)
        return carry

    lax.fori_loop(0, STRIP_CLUSTERS // 2, strip_step, 0, unroll=2)
    features[STRIP_CLUSTERS] = jnp.zeros((DEPTH, C), bf16)
    charge[STRIP_CLUSTERS] = jnp.zeros((8, C), f32)

    def self_step(step, carry):
        for turn in range(UNROLL):
            cluster = step * UNROLL + turn
            square = lax.dot_general(
                own_lhs[cluster],
                features[SELF + cluster],
                (((0,), (0,)), ((), ())),
                preferred_element_type=f32,
            )
            first_sum[cluster] = kernel_sums(
                square,
                charge[SELF + cluster, 0:1, 0:LANES],
                charge[SELF + cluster, 0:1, LANES:C],
            )
            second_sum[cluster] = jnp.zeros((C, LANES), f32)
        return carry

    lax.fori_loop(0, CLUSTERS // UNROLL, self_step, 0)
    copy.wait()
    add_pairs(entries, lhs, features, charge, STRIP_CLUSTERS, (first_sum, second_sum))
    for cluster in range(CLUSTERS):
        for half in range(2):
            row = 2 * cluster + half
            near[row : row + 1, :] = summed_row((first_sum, second_sum), cluster, half)


def outer_kernel(
    place,
    first_strip,
    strip,
    second_strip,
    lhs,
    inner,
    near,
    features,
    charge,
    listed,
    entries,
    semaphore,
    *sums,
):
    targets, sources = pair_rows((first_strip, second_strip))
    own_targets, own_sources = pair_rows((strip,))
    list_entries(
        place, sources + [own_targets[1]], targets + [own_sources[1]], False, listed
    )
    copy = pltpu.make_async_copy(listed, entries, semaphore)
    copy.start()
    for total in sums:
        total[...] = jnp.zeros(total.shape, f32)
    origin = own_origin(strip, 64)

    def window_step(block, carry):
        for part, ref in enumerate((first_strip, second_strip)):
            for odd in range(2):
                slot = part * STRIP_CLUSTERS + 2 * block + odd
                put_source(features, charge, slot, cluster_halves(ref, block, odd), origin)
        return carry

    lax.fori_loop(0, STRIP_CLUSTERS // 2, window_step, 0, unroll=2)
    features[OUTER] = jnp.zeros((DEPTH, C), bf16)
    charge[OUTER] = jnp.zeros((8, C), f32)
    copy.wait()
    add_pairs(entries, lhs, features, charge, OUTER, sums)
    for cluster in range(CLUSTERS):
        for half in range(2):
            row = 2 * cluster + half
            near[row : row + 1, :] = inner[row : row + 1, :] + summed_row(sums, cluster, half)


def far_kernel(
    far_count,
    place,
    first_strip,
    strip,
    second_strip,
    top,
    far_pairs,
    near,
    order,
    target_basis,
    potential,
    total,
):
    group_first = place[0:1, 0:1] * GROUP
    target = far_pairs[0:1, :] - group_first
    source = far_pairs[1:2, :]
    is_leaf = far_pairs[2:3, :] == 0
    live = iota((1, LANES), 1) < far_count[0]
    sign = 1 - 2 * (place[0:1, 0:1] & 1)
    offset = source - group_first
    leaf = (1 + sign * (offset >> 7)) * GROUP + (offset & (GROUP - 1))
    index = jnp.where(is_leaf, leaf, source + 3 * GROUP)
    skel = slice(SKEL_ROW, SKEL_ROW + GROUP)
    tops = top[pl.ds(0, top.shape[0] // TOP_ROWS, stride=TOP_ROWS), :]
    table = jnp.concatenate([first_strip[skel, :], strip[skel, :], second_strip[skel, :], tops], axis=0)
    chosen = as_bf16(iota((table.shape[0], LANES), 0) == index)
    over_rows = ((0,), (0,))
    sources = parts_dot(table, chosen, over_rows)
    own_chosen = as_bf16(iota((GROUP, LANES), 0) == target)
    targets = parts_dot(strip[skel, :], own_chosen, over_rows)
    target = target - place[0:1, 1:2] * CLUSTERS
    rows = []
    for a in range(R):
        square = soft_square
        for axis in range(3):
            offset = sources[axis * R : (axis + 1) * R] - targets[axis * R + a : axis * R + a + 1]
            square = square + offset * offset
        product = lax.rsqrt(square) * sources[3 * R :]
        rows.append(jnp.sum(product, axis=0, keepdims=True))
    middle = jnp.where(live, jnp.concatenate(rows, axis=0) * kernel_scale, 0.0)
    for cluster in range(CLUSTERS):
        column = jnp.sum(jnp.where(target == cluster, middle, 0.0), axis=1, keepdims=True)
        spread = jnp.sum(
            target_basis[:, cluster * C : (cluster + 1) * C] * column, axis=0, keepdims=True
        )
        for half in range(2):
            row = 2 * cluster + half
            total[row : row + 1, :] = (
                near[row : row + 1, :] + spread[:, half * LANES : (half + 1) * LANES]
            )
    low = order[...] & (LANES - 1)
    high = order[...] >> 7
    tall = iota((LANES, LANES), 0)
    wide = iota((ROWS, LANES), 0)
    whole = [part.astype(f32) for part in split3(total[...])]
    values, places = [], []
    for row in range(ROWS):
        here = wide == high[row : row + 1]
        parts = [jnp.where(here, part[row : row + 1, :], 0.0) for part in whole]
        values.append(jnp.concatenate(parts, axis=0).astype(bf16))
        places.append(as_bf16(tall == low[row : row + 1]))
    placed = lax.dot_general(
        jnp.concatenate(values, axis=1),
        jnp.concatenate(places, axis=1),
        (((1,), (1,)), ((), ())),
        preferred_element_type=f32,
    )
    out = placed[:ROWS] + placed[ROWS : 2 * ROWS] + placed[2 * ROWS :]
    potential[...] = out


def smem():
    return pl.BlockSpec(memory_space=pltpu.SMEM)


def in_hbm():
    return pl.BlockSpec(memory_space=pltpu.HBM)


def vmem():
    return pl.BlockSpec(memory_space=pltpu.VMEM)


params = pltpu.CompilerParams(vmem_limit_bytes=50 * 1024 * 1024)
first_params = pltpu.CompilerParams(vmem_limit_bytes=127 * 512 * 1024)


def local(
    points,
    charges,
    order,
    source_basis,
    target_basis,
    skeleton_points,
    transfer,
    top_points,
    near_pairs,
    near_count,
    far_pairs,
    far_count,
):
    wide_size = lax.axis_size("wide")
    narrow_size = lax.axis_size("narrow")
    place = jnp.stack([lax.axis_index("wide"), lax.axis_index("narrow")]).astype(i32).reshape(1, 2)
    order = order.reshape(ROWS, LANES)
    shape = jax.ShapeDtypeStruct
    inputs = (
        order,
        points,
        charges.reshape(ROWS, LANES),
        near_pairs,
        source_basis,
        transfer,
        skeleton_points,
        top_points,
    )
    with jax.named_scope("slots"):
        own, skel = pl.pallas_call(
            slots_kernel,
            out_shape=(
                shape((136, LANES), f32),
                shape((NARROW, SKEL_REC, LANES), f32),
            ),
            in_specs=[smem()] + [in_hbm()] * len(inputs),
            out_specs=[vmem()] * 2,
            scratch_shapes=[pltpu.VMEM(x.shape, x.dtype) for x in inputs]
            + [pltpu.SemaphoreType.DMA((len(inputs),))],
            compiler_params=first_params,
        )(near_count, *inputs)
    skels = lax.all_to_all(skel, "narrow", 0, 0, tiled=True)
    from_down = lax.ppermute(own, "narrow", [(i, i + 1) for i in range(narrow_size - 1)])
    from_up = lax.ppermute(own, "narrow", [(i + 1, i) for i in range(narrow_size - 1)])
    with jax.named_scope("top"):
        top_message = pl.pallas_call(
            top_kernel,
            out_shape=shape((TOP_ROWS * wide_size, LANES), f32),
            in_specs=[vmem()],
            out_specs=vmem(),
            compiler_params=params,
        )(skels)
    tops = lax.all_to_all(top_message, "wide", 0, 0, tiled=True)
    with jax.named_scope("strip"):
        strip = pl.pallas_call(
            strip_kernel,
            out_shape=shape((STRIP_ROWS, LANES), f32),
            in_specs=[vmem()] * 5,
            out_specs=vmem(),
            compiler_params=params,
        )(skels, from_down, own, from_up, top_message)
    odd_even = [(i, i + 1) for i in range(1, wide_size - 1, 2)]
    even_odd = [(i, i + 1) for i in range(0, wide_size - 1, 2)]
    first_strip = lax.ppermute(strip, "wide", odd_even + [(j, i) for i, j in odd_even])
    second_strip = lax.ppermute(strip, "wide", even_odd + [(j, i) for i, j in even_odd])
    def near_scratch(slots):
        return [
            pltpu.VMEM((slots, DEPTH, C), bf16),
            pltpu.VMEM((slots, 8, C), f32),
            pltpu.VMEM((8, LANES), i32),
            pltpu.SMEM((8, LANES), i32),
            pltpu.SemaphoreType.DMA(()),
        ] + [pltpu.VMEM((CLUSTERS, C, LANES), f32)] * SUMS

    with jax.named_scope("inner"):
        lhs, inner = pl.pallas_call(
            inner_kernel,
            out_shape=(shape((CLUSTERS, C, DEPTH), bf16), shape((ROWS, LANES), f32)),
            in_specs=[vmem()] * 2,
            out_specs=[vmem()] * 2,
            scratch_shapes=near_scratch(SELF + CLUSTERS)
            + [pltpu.VMEM((CLUSTERS, DEPTH, C), bf16)],
            compiler_params=params,
        )(place, strip)
    with jax.named_scope("outer"):
        near = pl.pallas_call(
            outer_kernel,
            out_shape=shape((ROWS, LANES), f32),
            in_specs=[vmem()] * 6,
            out_specs=vmem(),
            scratch_shapes=near_scratch(OUTER + 1),
            compiler_params=params,
        )(place, first_strip, strip, second_strip, lhs, inner)
    with jax.named_scope("far"):
        potential = pl.pallas_call(
            far_kernel,
            out_shape=shape((ROWS, LANES), f32),
            in_specs=[smem()] + [vmem()] * 9,
            out_specs=vmem(),
            scratch_shapes=[pltpu.VMEM((ROWS, LANES), f32)],
            compiler_params=params,
        )(far_count, place, first_strip, strip, second_strip, tops, far_pairs, near, order, target_basis)
    return potential.reshape(-1)


def solution(mesh):
    both = ("wide", "narrow")
    split = P(None, both)
    return jax.shard_map(
        local,
        mesh=mesh,
        in_specs=(
            split,
            P(both),
            P(both),
            split,
            split,
            split,
            split,
            P(None, "wide"),
            split,
            P(both),
            split,
            P(both),
        ),
        out_specs=P(both),
        check_vma=False,
    )
```

```python
import jax
import jax.numpy as jnp
from jax import lax
from jax.experimental import pallas as pl
from jax.experimental.pallas import tpu as pltpu
from jax.sharding import PartitionSpec as P

C = 256
R = 32
LANES = 128
CLUSTERS = 16
ROWS = 32
NARROW = 8
GROUP = 128
WIDTH = 8
STRIP_CLUSTERS = 32
PAIR_ROW = 8 * STRIP_CLUSTERS
SKEL_ROW = PAIR_ROW + 24
STRIP_ROWS = SKEL_ROW + GROUP
SKEL_REC = 24
TOP_ROWS = 2
OUTER = 2 * STRIP_CLUSTERS
SELF = STRIP_CLUSTERS + 1
DEPTH = 48
UNROLL = 8
SUMS = 2
CHUNK = 64

soft_square = 0.01
kernel_scale = 0.07957747154594767
f32 = jnp.float32
bf16 = jnp.bfloat16
i32 = jnp.int32


def iota(shape, dim):
    return lax.broadcasted_iota(i32, shape, dim)


def split3(x):
    high = x.astype(bf16)
    rest = x - high.astype(f32)
    mid = rest.astype(bf16)
    low = (rest - mid.astype(f32)).astype(bf16)
    return high, mid, low


def parts_dot(x, ones, dims):
    dots = [
        lax.dot_general(part, ones, (dims, ((), ())), preferred_element_type=f32)
        for part in split3(x)
    ]
    return dots[0] + dots[1] + dots[2]


def as_bf16(mask):
    return mask.astype(f32).astype(bf16)


def slots_kernel(near_count, *refs):
    count = 8
    own, skel_out = refs[count : count + 2]
    held = refs[count + 2 : 2 * count + 2]
    semaphores = refs[2 * count + 2]
    copies = [
        pltpu.make_async_copy(refs[i], held[i], semaphores.at[i]) for i in range(count)
    ]
    for copy in copies:
        copy.start()
    order, points, charges, near_pairs = held[:4]
    source_basis, transfer, skeleton_points, top_points = held[4:]
    for copy in copies[:4]:
        copy.wait()
    low = order[...] & (LANES - 1)
    high = order[...] >> 7
    sub = iota((8, LANES), 0)
    tables = []
    for row in range(ROWS):
        xyz = points[:, row * LANES : (row + 1) * LANES]
        charge = charges[row : row + 1, :]
        tables.append(jnp.concatenate([xyz, charge, xyz, charge], axis=0))
    tiles = []
    for tile in range(CLUSTERS):
        first = 4 * (tile // 2) + tile % 2
        low_tile = jnp.where(sub < 4, low[first : first + 1], low[first + 2 : first + 3])
        high_tile = jnp.where(sub < 4, high[first : first + 1], high[first + 2 : first + 3])
        values = jnp.zeros((8, LANES), f32)
        for row in range(ROWS):
            found = jnp.take_along_axis(tables[row], low_tile, axis=1)
            values = jnp.where(high_tile == row, found, values)
        own[8 * tile : 8 * tile + 8, :] = values
        tiles.append(values)

    pairs = jnp.where(iota((2, 64), 1) < near_count[0], near_pairs[...] + 1, 0).astype(f32)
    own[128:136, :] = jnp.zeros((8, LANES), f32)
    own[128:130, 0:64] = pairs
    for copy in copies[4:]:
        copy.wait()

    lane = iota((R, LANES), 1)
    skel = jnp.zeros((R, LANES), f32)
    for cluster in range(CLUSTERS):
        block, place = cluster // 2, 4 * (cluster % 2) + 3
        basis = source_basis[:, cluster * C : (cluster + 1) * C]
        product = (
            basis[:, :LANES] * tiles[2 * block][place : place + 1]
            + basis[:, LANES:] * tiles[2 * block + 1][place : place + 1]
        )
        skel = jnp.where(lane == cluster, jnp.sum(product, axis=1, keepdims=True), skel)
    skel_rows = skel.T[:CLUSTERS, :]
    long_lane = iota((R, CLUSTERS * R), 1)
    repeat = as_bf16(long_lane % R == iota((R, CLUSTERS * R), 0))
    tiled = parts_dot(skel_rows, repeat, ((1,), (0,)))
    mine = iota((CLUSTERS, CLUSTERS * R), 1) // R == iota((CLUSTERS, CLUSTERS * R), 0)
    flat = jnp.sum(jnp.where(mine, tiled, 0.0), axis=0, keepdims=True)
    partial = jnp.sum(transfer[...] * flat, axis=1, keepdims=True)
    skel = jnp.where(lane == CLUSTERS, partial, skel)
    to_charge = as_bf16(lane == iota((R, LANES), 0) + 3 * R)
    record = parts_dot(skel.T[:SKEL_REC, :], to_charge, ((1,), (0,)))
    fold = as_bf16(iota((CLUSTERS * R, LANES), 1) % R == iota((CLUSTERS * R, LANES), 0) % R)
    short_lane = iota((CLUSTERS, LANES), 1) // R
    geometry = jnp.zeros((CLUSTERS, LANES), f32)
    for axis in range(3):
        masked = jnp.where(mine, skeleton_points[axis : axis + 1, :], 0.0)
        folded = parts_dot(masked, fold, ((1,), (0,)))
        geometry = jnp.where(short_lane == axis, folded, geometry)
    spread = as_bf16(lane % R == iota((R, LANES), 0))
    top = parts_dot(top_points[...], spread, ((1,), (0,)))
    top_mine = iota((3, LANES), 1) // R == iota((3, LANES), 0)
    top_row = jnp.sum(jnp.where(top_mine, top, 0.0), axis=0, keepdims=True)
    last = jnp.where(iota((8, LANES), 0) == 1, top_row, 0.0)
    record = record + jnp.concatenate([geometry, last], axis=0)
    for device in range(NARROW):
        skel_out[device] = record


def top_kernel(skels, top_message):
    last = skels[0, CLUSTERS:SKEL_REC, :]
    row = last[0:1] + last[1:2]
    for device in range(1, NARROW):
        row = row + skels[device, CLUSTERS:SKEL_REC, :][0:1]
    top_message[...] = jnp.broadcast_to(row, top_message.shape)


def strip_kernel(skels, from_down, own, from_up, top_message, strip):
    del top_message
    strip[0:64, :] = from_down[64:128, :]
    strip[64:192, :] = own[0:128, :]
    strip[192:256, :] = from_up[0:64, :]
    strip[PAIR_ROW : PAIR_ROW + 8, :] = from_down[128:136, :]
    strip[PAIR_ROW + 8 : PAIR_ROW + 16, :] = own[128:136, :]
    strip[PAIR_ROW + 16 : PAIR_ROW + 24, :] = from_up[128:136, :]
    for device in range(NARROW):
        start = SKEL_ROW + device * CLUSTERS
        strip[start : start + CLUSTERS, :] = skels[device, :CLUSTERS, :]


def with_norms(halves, origin):
    out = []
    for half in halves:
        sub = iota((8, LANES), 0)
        shifted = jnp.where(sub < 3, half - origin, 0.0)
        norms = jnp.sum(shifted * shifted, axis=0, keepdims=True)
        out.append((shifted, norms))
    return out


def source_features(halves, origin):
    sub = iota((8, LANES), 0)
    columns = []
    for shifted, norms in with_norms(halves, origin):
        rows = jnp.where(sub < 3, shifted, jnp.where(sub == 4, norms, 0.0))
        rows = jnp.where(sub == 5, 1.0, rows)
        high, mid, low = [part.astype(f32) for part in split3(rows)]
        columns.append(jnp.concatenate([high, mid, high, mid, low, high], axis=0).astype(bf16))
    return jnp.concatenate(columns, axis=1)


def target_features(halves, origin):
    sub = iota((8, LANES), 0)
    columns = []
    for shifted, norms in with_norms(halves, origin):
        rows = jnp.where(sub < 3, -2.0 * shifted, jnp.where(sub == 5, norms + soft_square, 0.0))
        rows = jnp.where(sub == 4, 1.0, rows)
        high, mid, low = [part.astype(f32) for part in split3(rows)]
        columns.append(jnp.concatenate([high, high, mid, mid, high, low], axis=0))
    return columns


def cluster_halves(ref, block, odd):
    halves = []
    for half in range(2):
        tile = ref[pl.ds(pl.multiple_of(16 * block + 8 * half, 8), 8), :]
        halves.append(pltpu.roll(tile, 4, 0) if odd else tile)
    return halves


def own_origin(ref, start):
    whole = jnp.zeros((8, LANES), f32)
    for tile in range(CLUSTERS):
        whole = whole + ref[start + 8 * tile : start + 8 * tile + 8, :]
    mean = jnp.sum(whole, axis=1, keepdims=True) * (1.0 / (CLUSTERS * C))
    mean = jnp.broadcast_to(mean, (8, LANES))
    return jnp.where(iota((8, LANES), 0) < 3, mean + pltpu.roll(mean, 4, 0), 0.0)


def kernel_sums(square, charge_low, charge_high):
    inverse = lax.rsqrt(jnp.maximum(square, soft_square))
    return inverse[:, :LANES] * charge_low + inverse[:, LANES:] * charge_high


def put_source(features, charge, slot, halves, origin):
    features[slot] = source_features(halves, origin)
    for half in range(2):
        row = halves[half][3:4]
        charge[slot, :, half * LANES : (half + 1) * LANES] = jnp.broadcast_to(row, (8, LANES))


def pair_rows(refs):
    targets, sources = [], []
    for ref in refs:
        for block in range(3):
            start = PAIR_ROW + 8 * block
            targets.append(ref[start : start + 1, :])
            sources.append(ref[start + 1 : start + 2, :])
    return targets, sources


def list_entries(place, own_rows, other_rows, inner, out):
    wide_index = place[0:1, 0:1].astype(f32)
    narrow_index = place[0:1, 1:2].astype(f32)
    count_rows = len(own_rows)
    base = wide_index * GROUP + narrow_index * CLUSTERS + 1.0
    nothing = [jnp.zeros((16 - count_rows, LANES), f32)]
    own_ids = jnp.concatenate(own_rows + nothing, axis=0)
    other_ids = jnp.concatenate(other_rows + nothing, axis=0)
    local = own_ids - base
    other = other_ids - 1.0
    group = jnp.floor(other * (1.0 / GROUP))
    rest = other - GROUP * group
    depth = jnp.floor(rest * (1.0 / WIDTH))
    column = rest - WIDTH * depth
    group_step = group - (wide_index - 1.0)
    depth_step = depth - (2.0 * narrow_index - 1.0)
    slot = depth_step * WIDTH + column
    if inner:
        wanted = group_step == 1.0
    else:
        wanted = group_step != 1.0
        odd = wide_index - 2.0 * jnp.floor(0.5 * wide_index)
        second = jnp.where(group_step > 1.0, 1.0 - odd, odd)
        slot = slot + STRIP_CLUSTERS * second
    used = wanted & (local >= 0.0) & (local < CLUSTERS) & (own_ids > 0.0)
    count = used.astype(f32)
    upto = as_bf16(iota((LANES, LANES), 0) <= iota((LANES, LANES), 1))
    inclusive = jnp.dot(count.astype(bf16), upto, preferred_element_type=f32)
    totals = jnp.sum(count, axis=1, keepdims=True)
    row_of = iota((16, LANES), 0)
    offset = jnp.zeros((16, LANES), f32)
    for row in range(count_rows):
        offset = jnp.where(row_of > row, offset + totals[row : row + 1], offset)
    spot = jnp.where(used, inclusive - count + offset, -1.0)
    slot = jnp.where(used, slot, 0.0)
    local = jnp.where(used, local, 0.0)
    spot_high = jnp.floor(spot * (1.0 / LANES))
    spot_low = spot - LANES * spot_high
    listed = jnp.zeros((16, LANES), f32)
    eight = iota((8, LANES), 0).astype(f32)
    tall = iota((LANES, LANES), 0).astype(f32)
    for row in range(count_rows):
        here = eight == spot_high[row : row + 1]
        values = jnp.concatenate(
            [
                jnp.where(here, local[row : row + 1], 0.0),
                jnp.where(here, slot[row : row + 1], 0.0),
            ],
            axis=0,
        ).astype(bf16)
        hot = as_bf16(tall == spot_low[row : row + 1])
        listed = listed + lax.dot_general(
            values, hot, (((1,), (1,)), ((), ())), preferred_element_type=f32
        )
    coded = listed[:8] * float(GROUP) + listed[8:]
    out[...] = jnp.where(eight == 7.0, jnp.sum(totals), coded).astype(i32)


def add_pairs(entries, lhs, features, charge, dummy, sums):
    pair_total = entries[7, 0]

    def pair_steps(first, turns, carry):
        for turn in range(turns):
            index = first + turn
            code = entries[index >> 7, index & (LANES - 1)]
            live = index < pair_total
            cluster = jnp.where(live, code >> 7, 0)
            slot = jnp.where(live, code & (LANES - 1), dummy)
            right = features[slot]
            charge_low = charge[slot, 0:1, 0:LANES]
            charge_high = charge[slot, 0:1, LANES:C]
            for start in range(0, C, CHUNK):
                square = jnp.dot(
                    lhs[cluster, start : start + CHUNK, :], right, preferred_element_type=f32
                )
                sums[turn % SUMS][cluster, start : start + CHUNK, :] += kernel_sums(
                    square, charge_low, charge_high
                )
        return carry

    steps = (pair_total + UNROLL - 1) // UNROLL
    lax.fori_loop(
        0, steps // 2, lambda step, carry: pair_steps(2 * UNROLL * step, 2 * UNROLL, carry), 0
    )
    lax.fori_loop(
        2 * (steps // 2), steps, lambda step, carry: pair_steps(UNROLL * step, UNROLL, carry), 0
    )


def summed_row(sums, cluster, half):
    rows = slice(half * LANES, (half + 1) * LANES)
    total = sums[0][cluster, rows, :] + sums[1][cluster, rows, :]
    return kernel_scale * jnp.sum(total.T, axis=0, keepdims=True)


def inner_kernel(
    place, strip, lhs, near, features, charge, listed, entries, semaphore, *rest
):
    first_sum, second_sum, own_lhs = rest
    targets, sources = pair_rows((strip,))
    list_entries(place, sources + [targets[1]], targets + [sources[1]], True, listed)
    copy = pltpu.make_async_copy(listed, entries, semaphore)
    copy.start()
    origin = own_origin(strip, 64)

    def own_step(block, carry):
        for odd in range(2):
            cluster = 2 * block + odd
            halves = cluster_halves(strip, block + 4, odd)
            for half, column in enumerate(target_features(halves, origin)):
                lhs[cluster, half * LANES : (half + 1) * LANES, :] = column.T.astype(bf16)
            centre = jnp.sum(halves[0] + halves[1], axis=1, keepdims=True) * (1.0 / C)
            for half, column in enumerate(target_features(halves, centre)):
                own_lhs[cluster, :, half * LANES : (half + 1) * LANES] = column.astype(bf16)
            put_source(features, charge, SELF + cluster, halves, centre)
        return carry

    lax.fori_loop(0, CLUSTERS // 2, own_step, 0, unroll=4)

    def strip_step(block, carry):
        for odd in range(2):
            put_source(features, charge, 2 * block + odd, cluster_halves(strip, block, odd), origin)
        return carry

    lax.fori_loop(0, STRIP_CLUSTERS // 2, strip_step, 0, unroll=2)
    features[STRIP_CLUSTERS] = jnp.zeros((DEPTH, C), bf16)
    charge[STRIP_CLUSTERS] = jnp.zeros((8, C), f32)

    def self_step(step, carry):
        for turn in range(UNROLL):
            cluster = step * UNROLL + turn
            square = lax.dot_general(
                own_lhs[cluster],
                features[SELF + cluster],
                (((0,), (0,)), ((), ())),
                preferred_element_type=f32,
            )
            first_sum[cluster] = kernel_sums(
                square,
                charge[SELF + cluster, 0:1, 0:LANES],
                charge[SELF + cluster, 0:1, LANES:C],
            )
            second_sum[cluster] = jnp.zeros((C, LANES), f32)
        return carry

    lax.fori_loop(0, CLUSTERS // UNROLL, self_step, 0)
    copy.wait()
    add_pairs(entries, lhs, features, charge, STRIP_CLUSTERS, (first_sum, second_sum))
    for cluster in range(CLUSTERS):
        for half in range(2):
            row = 2 * cluster + half
            near[row : row + 1, :] = summed_row((first_sum, second_sum), cluster, half)


def far_rows(far_count, place, strips, top, far_pairs, target_basis, inner, total):
    first_strip, strip, second_strip = strips
    tops = top[pl.ds(0, top.shape[0] // TOP_ROWS, stride=TOP_ROWS), :]
    group_first = place[0:1, 0:1] * GROUP
    target = far_pairs[0:1, :] - group_first
    source = far_pairs[1:2, :]
    is_leaf = far_pairs[2:3, :] == 0
    live = iota((1, LANES), 1) < far_count[0]
    sign = 1 - 2 * (place[0:1, 0:1] & 1)
    offset = source - group_first
    leaf = (1 + sign * (offset >> 7)) * GROUP + (offset & (GROUP - 1))
    groups = tops.shape[0]
    index = jnp.where(is_leaf, leaf, ((source + groups // 2) & (groups - 1)) + 3 * GROUP)
    skel = slice(SKEL_ROW, SKEL_ROW + GROUP)
    table = jnp.concatenate([first_strip[skel, :], strip[skel, :], second_strip[skel, :], tops], axis=0)
    chosen = as_bf16(iota((table.shape[0], LANES), 0) == index)
    over_rows = ((0,), (0,))
    sources = parts_dot(table, chosen, over_rows)
    own_chosen = as_bf16(iota((GROUP, LANES), 0) == target)
    targets = parts_dot(strip[skel, :], own_chosen, over_rows)
    target = target - place[0:1, 1:2] * CLUSTERS
    rows = []
    for a in range(R):
        square = soft_square
        for axis in range(3):
            offset = sources[axis * R : (axis + 1) * R] - targets[axis * R + a : axis * R + a + 1]
            square = square + offset * offset
        product = lax.rsqrt(square) * sources[3 * R :]
        rows.append(jnp.sum(product, axis=0, keepdims=True))
    middle = jnp.where(live, jnp.concatenate(rows, axis=0) * kernel_scale, 0.0)
    for cluster in range(CLUSTERS):
        column = jnp.sum(jnp.where(target == cluster, middle, 0.0), axis=1, keepdims=True)
        spread = jnp.sum(
            target_basis[:, cluster * C : (cluster + 1) * C] * column, axis=0, keepdims=True
        )
        for half in range(2):
            row = 2 * cluster + half
            total[row : row + 1, :] = (
                inner[row : row + 1, :] + spread[:, half * LANES : (half + 1) * LANES]
            )


def arrival_order(total, order):
    low = order[...] & (LANES - 1)
    high = order[...] >> 7
    tall = iota((LANES, LANES), 0)
    wide = iota((ROWS, LANES), 0)
    whole = [part.astype(f32) for part in split3(total[...])]
    values, places = [], []
    for row in range(ROWS):
        here = wide == high[row : row + 1]
        parts = [jnp.where(here, part[row : row + 1, :], 0.0) for part in whole]
        values.append(jnp.concatenate(parts, axis=0).astype(bf16))
        places.append(as_bf16(tall == low[row : row + 1]))
    placed = lax.dot_general(
        jnp.concatenate(values, axis=1),
        jnp.concatenate(places, axis=1),
        (((1,), (1,)), ((), ())),
        preferred_element_type=f32,
    )
    out = placed[:ROWS] + placed[ROWS : 2 * ROWS] + placed[2 * ROWS :]
    return out


def outer_kernel(
    far_count,
    place,
    second_strip,
    strip,
    first_strip,
    lhs,
    inner,
    top,
    far_pairs,
    order,
    target_basis,
    potential,
    features,
    charge,
    listed,
    entries,
    semaphore,
    *rest,
):
    *sums, total = rest
    targets, sources = pair_rows((first_strip, second_strip))
    own_targets, own_sources = pair_rows((strip,))
    list_entries(
        place, sources + [own_targets[1]], targets + [own_sources[1]], False, listed
    )
    copy = pltpu.make_async_copy(listed, entries, semaphore)
    copy.start()
    for part in sums:
        part[...] = jnp.zeros(part.shape, f32)
    strips = (first_strip, strip, second_strip)
    far_rows(far_count, place, strips, top, far_pairs, target_basis, inner, total)
    origin = own_origin(strip, 64)

    def window_step(block, carry):
        for part, ref in enumerate((first_strip, second_strip)):
            for odd in range(2):
                slot = part * STRIP_CLUSTERS + 2 * block + odd
                put_source(features, charge, slot, cluster_halves(ref, block, odd), origin)
        return carry

    lax.fori_loop(0, STRIP_CLUSTERS // 2, window_step, 0, unroll=2)
    features[OUTER] = jnp.zeros((DEPTH, C), bf16)
    charge[OUTER] = jnp.zeros((8, C), f32)
    copy.wait()
    add_pairs(entries, lhs, features, charge, OUTER, sums)
    for cluster in range(CLUSTERS):
        for half in range(2):
            row = 2 * cluster + half
            total[row : row + 1, :] += summed_row(sums, cluster, half)
    potential[...] = arrival_order(total, order)


def smem():
    return pl.BlockSpec(memory_space=pltpu.SMEM)


def in_hbm():
    return pl.BlockSpec(memory_space=pltpu.HBM)


def vmem():
    return pl.BlockSpec(memory_space=pltpu.VMEM)


params = pltpu.CompilerParams(vmem_limit_bytes=50 * 1024 * 1024)
first_params = pltpu.CompilerParams(vmem_limit_bytes=127 * 512 * 1024)


def local(
    points,
    charges,
    order,
    source_basis,
    target_basis,
    skeleton_points,
    transfer,
    top_points,
    near_pairs,
    near_count,
    far_pairs,
    far_count,
):
    wide_size = lax.axis_size("wide")
    narrow_size = lax.axis_size("narrow")
    place = jnp.stack([lax.axis_index("wide"), lax.axis_index("narrow")]).astype(i32).reshape(1, 2)
    order = order.reshape(ROWS, LANES)
    shape = jax.ShapeDtypeStruct
    inputs = (
        order,
        points,
        charges.reshape(ROWS, LANES),
        near_pairs,
        source_basis,
        transfer,
        skeleton_points,
        top_points,
    )
    with jax.named_scope("slots"):
        own, skel = pl.pallas_call(
            slots_kernel,
            out_shape=(
                shape((136, LANES), f32),
                shape((NARROW, SKEL_REC, LANES), f32),
            ),
            in_specs=[smem()] + [in_hbm()] * len(inputs),
            out_specs=[vmem()] * 2,
            scratch_shapes=[pltpu.VMEM(x.shape, x.dtype) for x in inputs]
            + [pltpu.SemaphoreType.DMA((len(inputs),))],
            compiler_params=first_params,
        )(near_count, *inputs)
    skels = lax.all_to_all(skel, "narrow", 0, 0, tiled=True)
    from_down = lax.ppermute(own, "narrow", [(i, i + 1) for i in range(narrow_size - 1)])
    from_up = lax.ppermute(own, "narrow", [(i + 1, i) for i in range(narrow_size - 1)])
    with jax.named_scope("top"):
        top_message = pl.pallas_call(
            top_kernel,
            out_shape=shape((TOP_ROWS * wide_size, LANES), f32),
            in_specs=[vmem()],
            out_specs=vmem(),
            compiler_params=params,
        )(skels)
    members = [(i + wide_size // 2) % wide_size for i in range(wide_size)]
    tops = lax.all_to_all(
        top_message, "wide", 0, 0, tiled=True, axis_index_groups=[members]
    )
    with jax.named_scope("strip"):
        strip = pl.pallas_call(
            strip_kernel,
            out_shape=shape((STRIP_ROWS, LANES), f32),
            in_specs=[vmem()] * 5,
            out_specs=vmem(),
            compiler_params=params,
        )(skels, from_down, own, from_up, top_message)
    odd_even = [(i, i + 1) for i in range(1, wide_size - 1, 2)]
    even_odd = [(i, i + 1) for i in range(0, wide_size - 1, 2)]
    first_strip = lax.ppermute(strip, "wide", odd_even + [(j, i) for i, j in odd_even])
    second_strip = lax.ppermute(strip, "wide", even_odd + [(j, i) for i, j in even_odd])
    def near_scratch(slots):
        return [
            pltpu.VMEM((slots, DEPTH, C), bf16),
            pltpu.VMEM((slots, 8, C), f32),
            pltpu.VMEM((8, LANES), i32),
            pltpu.SMEM((8, LANES), i32),
            pltpu.SemaphoreType.DMA(()),
        ] + [pltpu.VMEM((CLUSTERS, C, LANES), f32)] * SUMS

    with jax.named_scope("inner"):
        lhs, inner = pl.pallas_call(
            inner_kernel,
            out_shape=(shape((CLUSTERS, C, DEPTH), bf16), shape((ROWS, LANES), f32)),
            in_specs=[vmem()] * 2,
            out_specs=[vmem()] * 2,
            scratch_shapes=near_scratch(SELF + CLUSTERS)
            + [pltpu.VMEM((CLUSTERS, DEPTH, C), bf16)],
            compiler_params=params,
        )(place, strip)
    with jax.named_scope("outer"):
        potential = pl.pallas_call(
            outer_kernel,
            out_shape=shape((ROWS, LANES), f32),
            in_specs=[smem()] + [vmem()] * 10,
            out_specs=vmem(),
            scratch_shapes=near_scratch(OUTER + 1) + [pltpu.VMEM((ROWS, LANES), f32)],
            compiler_params=params,
        )(
            far_count,
            place,
            second_strip,
            strip,
            first_strip,
            lhs,
            inner,
            tops,
            far_pairs,
            order,
            target_basis,
        )
    return potential.reshape(-1)


def solution(mesh):
    both = ("wide", "narrow")
    split = P(None, both)
    return jax.shard_map(
        local,
        mesh=mesh,
        in_specs=(
            split,
            P(both),
            P(both),
            split,
            split,
            split,
            split,
            P(None, "wide"),
            split,
            P(both),
            split,
            P(both),
        ),
        out_specs=P(both),
        check_vma=False,
    )
```

```python
import jax
import jax.numpy as jnp
from jax import lax
from jax.experimental import pallas as pl
from jax.experimental.pallas import tpu as pltpu
from jax.sharding import PartitionSpec as P

C = 256
R = 32
LANES = 128
CLUSTERS = 16
ROWS = 32
NARROW = 8
GROUP = 128
WIDTH = 8
STRIP_CLUSTERS = 32
PAIR_ROW = 8 * STRIP_CLUSTERS
SKEL_ROW = PAIR_ROW + 24
STRIP_ROWS = SKEL_ROW + GROUP
SKEL_REC = 24
TOP_ROWS = 2
OUTER = 2 * STRIP_CLUSTERS
SELF = STRIP_CLUSTERS + 1
DEPTH = 48
UNROLL = 8
SUMS = 2
CHUNK = 64

soft_square = 0.01
kernel_scale = 0.07957747154594767
f32 = jnp.float32
bf16 = jnp.bfloat16
i32 = jnp.int32


def iota(shape, dim):
    return lax.broadcasted_iota(i32, shape, dim)


def split3(x):
    high = x.astype(bf16)
    rest = x - high.astype(f32)
    mid = rest.astype(bf16)
    low = (rest - mid.astype(f32)).astype(bf16)
    return high, mid, low


def parts_dot(x, ones, dims):
    dots = [
        lax.dot_general(part, ones, (dims, ((), ())), preferred_element_type=f32)
        for part in split3(x)
    ]
    return dots[0] + dots[1] + dots[2]


def as_bf16(mask):
    return mask.astype(f32).astype(bf16)


def slots_kernel(near_count, *refs):
    count = 9
    own, skel_out = refs[count : count + 2]
    held = refs[count + 2 : 2 * count + 2]
    semaphores = refs[2 * count + 2]
    copies = [
        pltpu.make_async_copy(refs[i], held[i], semaphores.at[i]) for i in range(count)
    ]
    for copy in copies:
        copy.start()
    order, points, charges, near_pairs, far_pairs = held[:5]
    source_basis, transfer, skeleton_points, top_points = held[5:]
    for copy in copies[:5]:
        copy.wait()
    low = order[...] & (LANES - 1)
    high = order[...] >> 7
    sub = iota((8, LANES), 0)
    tables = []
    for row in range(ROWS):
        xyz = points[:, row * LANES : (row + 1) * LANES]
        charge = charges[row : row + 1, :]
        tables.append(jnp.concatenate([xyz, charge, xyz, charge], axis=0))
    tiles = []
    for tile in range(CLUSTERS):
        first = 4 * (tile // 2) + tile % 2
        low_tile = jnp.where(sub < 4, low[first : first + 1], low[first + 2 : first + 3])
        high_tile = jnp.where(sub < 4, high[first : first + 1], high[first + 2 : first + 3])
        values = jnp.zeros((8, LANES), f32)
        for row in range(ROWS):
            found = jnp.take_along_axis(tables[row], low_tile, axis=1)
            values = jnp.where(high_tile == row, found, values)
        own[8 * tile : 8 * tile + 8, :] = values
        tiles.append(values)

    pairs = jnp.where(iota((2, 64), 1) < near_count[0], near_pairs[...] + 1, 0).astype(f32)
    own[128:144, :] = jnp.zeros((16, LANES), f32)
    own[128:130, 0:64] = pairs
    own[136:139, :] = far_pairs[...].astype(f32)
    for copy in copies[5:]:
        copy.wait()

    lane = iota((R, LANES), 1)
    skel = jnp.zeros((R, LANES), f32)
    for cluster in range(CLUSTERS):
        block, place = cluster // 2, 4 * (cluster % 2) + 3
        basis = source_basis[:, cluster * C : (cluster + 1) * C]
        product = (
            basis[:, :LANES] * tiles[2 * block][place : place + 1]
            + basis[:, LANES:] * tiles[2 * block + 1][place : place + 1]
        )
        skel = jnp.where(lane == cluster, jnp.sum(product, axis=1, keepdims=True), skel)
    skel_rows = skel.T[:CLUSTERS, :]
    long_lane = iota((R, CLUSTERS * R), 1)
    repeat = as_bf16(long_lane % R == iota((R, CLUSTERS * R), 0))
    tiled = parts_dot(skel_rows, repeat, ((1,), (0,)))
    mine = iota((CLUSTERS, CLUSTERS * R), 1) // R == iota((CLUSTERS, CLUSTERS * R), 0)
    flat = jnp.sum(jnp.where(mine, tiled, 0.0), axis=0, keepdims=True)
    partial = jnp.sum(transfer[...] * flat, axis=1, keepdims=True)
    skel = jnp.where(lane == CLUSTERS, partial, skel)
    to_charge = as_bf16(lane == iota((R, LANES), 0) + 3 * R)
    record = parts_dot(skel.T[:SKEL_REC, :], to_charge, ((1,), (0,)))
    fold = as_bf16(iota((CLUSTERS * R, LANES), 1) % R == iota((CLUSTERS * R, LANES), 0) % R)
    short_lane = iota((CLUSTERS, LANES), 1) // R
    geometry = jnp.zeros((CLUSTERS, LANES), f32)
    for axis in range(3):
        masked = jnp.where(mine, skeleton_points[axis : axis + 1, :], 0.0)
        folded = parts_dot(masked, fold, ((1,), (0,)))
        geometry = jnp.where(short_lane == axis, folded, geometry)
    spread = as_bf16(lane % R == iota((R, LANES), 0))
    top = parts_dot(top_points[...], spread, ((1,), (0,)))
    top_mine = iota((3, LANES), 1) // R == iota((3, LANES), 0)
    top_row = jnp.sum(jnp.where(top_mine, top, 0.0), axis=0, keepdims=True)
    last = jnp.where(iota((8, LANES), 0) == 1, top_row, 0.0)
    record = record + jnp.concatenate([geometry, last], axis=0)
    for device in range(NARROW):
        skel_out[device] = record


def top_kernel(skels, top_message):
    last = skels[0, CLUSTERS:SKEL_REC, :]
    row = last[0:1] + last[1:2]
    for device in range(1, NARROW):
        row = row + skels[device, CLUSTERS:SKEL_REC, :][0:1]
    top_message[...] = jnp.broadcast_to(row, top_message.shape)


def strip_kernel(skels, from_down, own, from_up, top_message, strip):
    del top_message
    strip[0:64, :] = from_down[64:128, :]
    strip[64:192, :] = own[0:128, :]
    strip[192:256, :] = from_up[0:64, :]
    strip[PAIR_ROW : PAIR_ROW + 8, :] = from_down[128:136, :]
    strip[PAIR_ROW + 8 : PAIR_ROW + 16, :] = own[128:136, :]
    strip[PAIR_ROW + 16 : PAIR_ROW + 24, :] = from_up[128:136, :]
    for device in range(NARROW):
        start = SKEL_ROW + device * CLUSTERS
        strip[start : start + CLUSTERS, :] = skels[device, :CLUSTERS, :]


def with_norms(halves, origin):
    out = []
    for half in halves:
        sub = iota((8, LANES), 0)
        shifted = jnp.where(sub < 3, half - origin, 0.0)
        norms = jnp.sum(shifted * shifted, axis=0, keepdims=True)
        out.append((shifted, norms))
    return out


def source_features(halves, origin):
    sub = iota((8, LANES), 0)
    columns = []
    for shifted, norms in with_norms(halves, origin):
        rows = jnp.where(sub < 3, shifted, jnp.where(sub == 4, norms, 0.0))
        rows = jnp.where(sub == 5, 1.0, rows)
        high, mid, low = [part.astype(f32) for part in split3(rows)]
        columns.append(jnp.concatenate([high, mid, high, mid, low, high], axis=0).astype(bf16))
    return jnp.concatenate(columns, axis=1)


def target_features(halves, origin):
    sub = iota((8, LANES), 0)
    columns = []
    for shifted, norms in with_norms(halves, origin):
        rows = jnp.where(sub < 3, -2.0 * shifted, jnp.where(sub == 5, norms + soft_square, 0.0))
        rows = jnp.where(sub == 4, 1.0, rows)
        high, mid, low = [part.astype(f32) for part in split3(rows)]
        columns.append(jnp.concatenate([high, high, mid, mid, high, low], axis=0))
    return columns


def cluster_halves(ref, block, odd):
    halves = []
    for half in range(2):
        tile = ref[pl.ds(pl.multiple_of(16 * block + 8 * half, 8), 8), :]
        halves.append(pltpu.roll(tile, 4, 0) if odd else tile)
    return halves


def own_origin(ref, start):
    whole = jnp.zeros((8, LANES), f32)
    for tile in range(CLUSTERS):
        whole = whole + ref[start + 8 * tile : start + 8 * tile + 8, :]
    mean = jnp.sum(whole, axis=1, keepdims=True) * (1.0 / (CLUSTERS * C))
    mean = jnp.broadcast_to(mean, (8, LANES))
    return jnp.where(iota((8, LANES), 0) < 3, mean + pltpu.roll(mean, 4, 0), 0.0)


def kernel_sums(square, charge_low, charge_high):
    inverse = lax.rsqrt(jnp.maximum(square, soft_square))
    return inverse[:, :LANES] * charge_low + inverse[:, LANES:] * charge_high


def put_source(features, charge, slot, halves, origin):
    features[slot] = source_features(halves, origin)
    for half in range(2):
        row = halves[half][3:4]
        charge[slot, :, half * LANES : (half + 1) * LANES] = jnp.broadcast_to(row, (8, LANES))


def pair_rows(refs):
    targets, sources = [], []
    for ref in refs:
        for block in range(3):
            start = PAIR_ROW + 8 * block
            targets.append(ref[start : start + 1, :])
            sources.append(ref[start + 1 : start + 2, :])
    return targets, sources


def list_entries(place, own_rows, other_rows, inner, out):
    wide_index = place[0:1, 0:1].astype(f32)
    narrow_index = place[0:1, 1:2].astype(f32)
    count_rows = len(own_rows)
    base = wide_index * GROUP + narrow_index * CLUSTERS + 1.0
    nothing = [jnp.zeros((16 - count_rows, LANES), f32)]
    own_ids = jnp.concatenate(own_rows + nothing, axis=0)
    other_ids = jnp.concatenate(other_rows + nothing, axis=0)
    local = own_ids - base
    other = other_ids - 1.0
    group = jnp.floor(other * (1.0 / GROUP))
    rest = other - GROUP * group
    depth = jnp.floor(rest * (1.0 / WIDTH))
    column = rest - WIDTH * depth
    group_step = group - (wide_index - 1.0)
    depth_step = depth - (2.0 * narrow_index - 1.0)
    slot = depth_step * WIDTH + column
    if inner:
        wanted = group_step == 1.0
    else:
        wanted = group_step != 1.0
        odd = wide_index - 2.0 * jnp.floor(0.5 * wide_index)
        second = jnp.where(group_step > 1.0, 1.0 - odd, odd)
        slot = slot + STRIP_CLUSTERS * second
    used = wanted & (local >= 0.0) & (local < CLUSTERS) & (own_ids > 0.0)
    count = used.astype(f32)
    upto = as_bf16(iota((LANES, LANES), 0) <= iota((LANES, LANES), 1))
    inclusive = jnp.dot(count.astype(bf16), upto, preferred_element_type=f32)
    totals = jnp.sum(count, axis=1, keepdims=True)
    row_of = iota((16, LANES), 0)
    offset = jnp.zeros((16, LANES), f32)
    for row in range(count_rows):
        offset = jnp.where(row_of > row, offset + totals[row : row + 1], offset)
    spot = jnp.where(used, inclusive - count + offset, -1.0)
    slot = jnp.where(used, slot, 0.0)
    local = jnp.where(used, local, 0.0)
    spot_high = jnp.floor(spot * (1.0 / LANES))
    spot_low = spot - LANES * spot_high
    listed = jnp.zeros((16, LANES), f32)
    eight = iota((8, LANES), 0).astype(f32)
    tall = iota((LANES, LANES), 0).astype(f32)
    for row in range(count_rows):
        here = eight == spot_high[row : row + 1]
        values = jnp.concatenate(
            [
                jnp.where(here, local[row : row + 1], 0.0),
                jnp.where(here, slot[row : row + 1], 0.0),
            ],
            axis=0,
        ).astype(bf16)
        hot = as_bf16(tall == spot_low[row : row + 1])
        listed = listed + lax.dot_general(
            values, hot, (((1,), (1,)), ((), ())), preferred_element_type=f32
        )
    coded = listed[:8] * float(GROUP) + listed[8:]
    out[...] = jnp.where(eight == 7.0, jnp.sum(totals), coded).astype(i32)


def add_pairs(entries, lhs, features, charge, dummy, sums):
    pair_total = entries[7, 0]

    def pair_steps(first, turns, carry):
        for turn in range(turns):
            index = first + turn
            code = entries[index >> 7, index & (LANES - 1)]
            live = index < pair_total
            cluster = jnp.where(live, code >> 7, 0)
            slot = jnp.where(live, code & (LANES - 1), dummy)
            right = features[slot]
            charge_low = charge[slot, 0:1, 0:LANES]
            charge_high = charge[slot, 0:1, LANES:C]
            for start in range(0, C, CHUNK):
                square = jnp.dot(
                    lhs[cluster, start : start + CHUNK, :], right, preferred_element_type=f32
                )
                sums[turn % SUMS][cluster, start : start + CHUNK, :] += kernel_sums(
                    square, charge_low, charge_high
                )
        return carry

    steps = (pair_total + UNROLL - 1) // UNROLL
    lax.fori_loop(
        0, steps // 2, lambda step, carry: pair_steps(2 * UNROLL * step, 2 * UNROLL, carry), 0
    )
    lax.fori_loop(
        2 * (steps // 2), steps, lambda step, carry: pair_steps(UNROLL * step, UNROLL, carry), 0
    )


def summed_row(sums, cluster, half):
    rows = slice(half * LANES, (half + 1) * LANES)
    total = sums[0][cluster, rows, :] + sums[1][cluster, rows, :]
    return kernel_scale * jnp.sum(total.T, axis=0, keepdims=True)


def inner_kernel(
    place, strip, lhs, near, features, charge, listed, entries, semaphore, *rest
):
    first_sum, second_sum, own_lhs = rest
    targets, sources = pair_rows((strip,))
    list_entries(place, sources + [targets[1]], targets + [sources[1]], True, listed)
    copy = pltpu.make_async_copy(listed, entries, semaphore)
    copy.start()
    origin = own_origin(strip, 64)

    def own_step(block, carry):
        for odd in range(2):
            cluster = 2 * block + odd
            halves = cluster_halves(strip, block + 4, odd)
            for half, column in enumerate(target_features(halves, origin)):
                lhs[cluster, half * LANES : (half + 1) * LANES, :] = column.T.astype(bf16)
            centre = jnp.sum(halves[0] + halves[1], axis=1, keepdims=True) * (1.0 / C)
            for half, column in enumerate(target_features(halves, centre)):
                own_lhs[cluster, :, half * LANES : (half + 1) * LANES] = column.astype(bf16)
            put_source(features, charge, SELF + cluster, halves, centre)
        return carry

    lax.fori_loop(0, CLUSTERS // 2, own_step, 0, unroll=4)

    def strip_step(block, carry):
        for odd in range(2):
            put_source(features, charge, 2 * block + odd, cluster_halves(strip, block, odd), origin)
        return carry

    lax.fori_loop(0, STRIP_CLUSTERS // 2, strip_step, 0, unroll=2)
    features[STRIP_CLUSTERS] = jnp.zeros((DEPTH, C), bf16)
    charge[STRIP_CLUSTERS] = jnp.zeros((8, C), f32)

    def self_step(step, carry):
        for turn in range(UNROLL):
            cluster = step * UNROLL + turn
            square = lax.dot_general(
                own_lhs[cluster],
                features[SELF + cluster],
                (((0,), (0,)), ((), ())),
                preferred_element_type=f32,
            )
            first_sum[cluster] = kernel_sums(
                square,
                charge[SELF + cluster, 0:1, 0:LANES],
                charge[SELF + cluster, 0:1, LANES:C],
            )
            second_sum[cluster] = jnp.zeros((C, LANES), f32)
        return carry

    lax.fori_loop(0, CLUSTERS // UNROLL, self_step, 0)
    copy.wait()
    add_pairs(entries, lhs, features, charge, STRIP_CLUSTERS, (first_sum, second_sum))
    for cluster in range(CLUSTERS):
        for half in range(2):
            row = 2 * cluster + half
            near[row : row + 1, :] = summed_row((first_sum, second_sum), cluster, half)


def far_rows(far_count, place, strips, top, far_pairs, target_basis, inner, total):
    first_strip, strip, second_strip = strips
    tops = top[pl.ds(0, top.shape[0] // TOP_ROWS, stride=TOP_ROWS), :]
    group_first = place[0:1, 0:1] * GROUP
    far_pairs = far_pairs.astype(i32)
    target = far_pairs[0:1, :] - group_first
    source = far_pairs[1:2, :]
    is_leaf = far_pairs[2:3, :] == 0
    live = iota((1, LANES), 1) < far_count[0]
    sign = 1 - 2 * (place[0:1, 0:1] & 1)
    offset = source - group_first
    leaf = (1 + sign * (offset >> 7)) * GROUP + (offset & (GROUP - 1))
    index = jnp.where(is_leaf, leaf, source + 3 * GROUP)
    skel = slice(SKEL_ROW, SKEL_ROW + GROUP)
    table = jnp.concatenate([first_strip[skel, :], strip[skel, :], second_strip[skel, :], tops], axis=0)
    chosen = as_bf16(iota((table.shape[0], LANES), 0) == index)
    over_rows = ((0,), (0,))
    sources = parts_dot(table, chosen, over_rows)
    own_chosen = as_bf16(iota((GROUP, LANES), 0) == target)
    targets = parts_dot(strip[skel, :], own_chosen, over_rows)
    target = target - place[0:1, 1:2] * CLUSTERS
    rows = []
    for a in range(R):
        square = soft_square
        for axis in range(3):
            offset = sources[axis * R : (axis + 1) * R] - targets[axis * R + a : axis * R + a + 1]
            square = square + offset * offset
        product = lax.rsqrt(square) * sources[3 * R :]
        rows.append(jnp.sum(product, axis=0, keepdims=True))
    middle = jnp.where(live, jnp.concatenate(rows, axis=0) * kernel_scale, 0.0)
    for cluster in range(CLUSTERS):
        column = jnp.sum(jnp.where(target == cluster, middle, 0.0), axis=1, keepdims=True)
        spread = jnp.sum(
            target_basis[:, cluster * C : (cluster + 1) * C] * column, axis=0, keepdims=True
        )
        for half in range(2):
            row = 2 * cluster + half
            total[row : row + 1, :] = (
                inner[row : row + 1, :] + spread[:, half * LANES : (half + 1) * LANES]
            )


def arrival_order(total, order):
    low = order[...] & (LANES - 1)
    high = order[...] >> 7
    tall = iota((LANES, LANES), 0)
    wide = iota((ROWS, LANES), 0)
    whole = [part.astype(f32) for part in split3(total[...])]
    values, places = [], []
    for row in range(ROWS):
        here = wide == high[row : row + 1]
        parts = [jnp.where(here, part[row : row + 1, :], 0.0) for part in whole]
        values.append(jnp.concatenate(parts, axis=0).astype(bf16))
        places.append(as_bf16(tall == low[row : row + 1]))
    placed = lax.dot_general(
        jnp.concatenate(values, axis=1),
        jnp.concatenate(places, axis=1),
        (((1,), (1,)), ((), ())),
        preferred_element_type=f32,
    )
    out = placed[:ROWS] + placed[ROWS : 2 * ROWS] + placed[2 * ROWS :]
    return out


def outer_kernel(
    far_count,
    place,
    second_strip,
    strip,
    first_strip,
    lhs,
    inner,
    top,
    own,
    order,
    target_basis,
    potential,
    features,
    charge,
    listed,
    entries,
    semaphore,
    *rest,
):
    *sums, total = rest
    targets, sources = pair_rows((first_strip, second_strip))
    own_targets, own_sources = pair_rows((strip,))
    list_entries(
        place, sources + [own_targets[1]], targets + [own_sources[1]], False, listed
    )
    copy = pltpu.make_async_copy(listed, entries, semaphore)
    copy.start()
    for part in sums:
        part[...] = jnp.zeros(part.shape, f32)
    strips = (first_strip, strip, second_strip)
    far_rows(far_count, place, strips, top, own[136:139, :], target_basis, inner, total)
    origin = own_origin(strip, 64)

    def window_step(block, carry):
        for part, ref in enumerate((first_strip, second_strip)):
            for odd in range(2):
                slot = part * STRIP_CLUSTERS + 2 * block + odd
                put_source(features, charge, slot, cluster_halves(ref, block, odd), origin)
        return carry

    lax.fori_loop(0, STRIP_CLUSTERS // 2, window_step, 0, unroll=2)
    features[OUTER] = jnp.zeros((DEPTH, C), bf16)
    charge[OUTER] = jnp.zeros((8, C), f32)
    copy.wait()
    add_pairs(entries, lhs, features, charge, OUTER, sums)
    for cluster in range(CLUSTERS):
        for half in range(2):
            row = 2 * cluster + half
            total[row : row + 1, :] += summed_row(sums, cluster, half)
    potential[...] = arrival_order(total, order)


def smem():
    return pl.BlockSpec(memory_space=pltpu.SMEM)


def in_hbm():
    return pl.BlockSpec(memory_space=pltpu.HBM)


def vmem():
    return pl.BlockSpec(memory_space=pltpu.VMEM)


params = pltpu.CompilerParams(vmem_limit_bytes=50 * 1024 * 1024)
first_params = pltpu.CompilerParams(vmem_limit_bytes=127 * 512 * 1024)


def local(
    points,
    charges,
    order,
    source_basis,
    target_basis,
    skeleton_points,
    transfer,
    top_points,
    near_pairs,
    near_count,
    far_pairs,
    far_count,
):
    wide_size = lax.axis_size("wide")
    narrow_size = lax.axis_size("narrow")
    place = jnp.stack([lax.axis_index("wide"), lax.axis_index("narrow")]).astype(i32).reshape(1, 2)
    order = order.reshape(ROWS, LANES)
    shape = jax.ShapeDtypeStruct
    inputs = (
        order,
        points,
        charges.reshape(ROWS, LANES),
        near_pairs,
        far_pairs,
        source_basis,
        transfer,
        skeleton_points,
        top_points,
    )
    with jax.named_scope("slots"):
        own, skel = pl.pallas_call(
            slots_kernel,
            out_shape=(
                shape((144, LANES), f32),
                shape((NARROW, SKEL_REC, LANES), f32),
            ),
            in_specs=[smem()] + [in_hbm()] * len(inputs),
            out_specs=[vmem()] * 2,
            scratch_shapes=[pltpu.VMEM(x.shape, x.dtype) for x in inputs]
            + [pltpu.SemaphoreType.DMA((len(inputs),))],
            compiler_params=first_params,
        )(near_count, *inputs)
    skels = lax.all_to_all(skel, "narrow", 0, 0, tiled=True)
    from_down = lax.ppermute(own, "narrow", [(i, i + 1) for i in range(narrow_size - 1)])
    from_up = lax.ppermute(own, "narrow", [(i + 1, i) for i in range(narrow_size - 1)])
    with jax.named_scope("top"):
        top_message = pl.pallas_call(
            top_kernel,
            out_shape=shape((TOP_ROWS * wide_size, LANES), f32),
            in_specs=[vmem()],
            out_specs=vmem(),
            compiler_params=params,
        )(skels)
    tops = lax.all_to_all(top_message, "wide", 0, 0, tiled=True)
    with jax.named_scope("strip"):
        strip = pl.pallas_call(
            strip_kernel,
            out_shape=shape((STRIP_ROWS, LANES), f32),
            in_specs=[vmem()] * 5,
            out_specs=vmem(),
            compiler_params=params,
        )(skels, from_down, own, from_up, top_message)
    odd_even = [(i, i + 1) for i in range(1, wide_size - 1, 2)]
    even_odd = [(i, i + 1) for i in range(0, wide_size - 1, 2)]
    first_strip = lax.ppermute(strip, "wide", odd_even + [(j, i) for i, j in odd_even])
    second_strip = lax.ppermute(strip, "wide", even_odd + [(j, i) for i, j in even_odd])
    def near_scratch(slots):
        return [
            pltpu.VMEM((slots, DEPTH, C), bf16),
            pltpu.VMEM((slots, 8, C), f32),
            pltpu.VMEM((8, LANES), i32),
            pltpu.SMEM((8, LANES), i32),
            pltpu.SemaphoreType.DMA(()),
        ] + [pltpu.VMEM((CLUSTERS, C, LANES), f32)] * SUMS

    with jax.named_scope("inner"):
        lhs, inner = pl.pallas_call(
            inner_kernel,
            out_shape=(shape((CLUSTERS, C, DEPTH), bf16), shape((ROWS, LANES), f32)),
            in_specs=[vmem()] * 2,
            out_specs=[vmem()] * 2,
            scratch_shapes=near_scratch(SELF + CLUSTERS)
            + [pltpu.VMEM((CLUSTERS, DEPTH, C), bf16)],
            compiler_params=params,
        )(place, strip)
    with jax.named_scope("outer"):
        potential = pl.pallas_call(
            outer_kernel,
            out_shape=shape((ROWS, LANES), f32),
            in_specs=[smem()] + [vmem()] * 10,
            out_specs=vmem(),
            scratch_shapes=near_scratch(OUTER + 1) + [pltpu.VMEM((ROWS, LANES), f32)],
            compiler_params=params,
        )(
            far_count,
            place,
            second_strip,
            strip,
            first_strip,
            lhs,
            inner,
            tops,
            own,
            order,
            target_basis,
        )
    return potential.reshape(-1)


def solution(mesh):
    both = ("wide", "narrow")
    split = P(None, both)
    return jax.shard_map(
        local,
        mesh=mesh,
        in_specs=(
            split,
            P(both),
            P(both),
            split,
            split,
            split,
            split,
            P(None, "wide"),
            split,
            P(both),
            split,
            P(both),
        ),
        out_specs=P(both),
        check_vma=False,
    )
```

```python
import jax
import jax.numpy as jnp
from jax import lax
from jax.experimental import pallas as pl
from jax.experimental.pallas import tpu as pltpu
from jax.sharding import PartitionSpec as P

C = 256
R = 32
LANES = 128
CLUSTERS = 16
ROWS = 32
NARROW = 8
GROUP = 128
WIDTH = 8
STRIP_CLUSTERS = 32
PAIR_ROW = 8 * STRIP_CLUSTERS
SKEL_ROW = PAIR_ROW + 8
STRIP_ROWS = SKEL_ROW + GROUP
SKEL_REC = 24
TOP_ROWS = 2
OUTER = 2 * STRIP_CLUSTERS
SELF = STRIP_CLUSTERS + 1
DEPTH = 48
UNROLL = 8
SUMS = 2
CHUNK = 64

soft_square = 0.01
kernel_scale = 0.07957747154594767
f32 = jnp.float32
bf16 = jnp.bfloat16
i32 = jnp.int32


def iota(shape, dim):
    return lax.broadcasted_iota(i32, shape, dim)


def split3(x):
    high = x.astype(bf16)
    rest = x - high.astype(f32)
    mid = rest.astype(bf16)
    low = (rest - mid.astype(f32)).astype(bf16)
    return high, mid, low


def parts_dot(x, ones, dims):
    dots = [
        lax.dot_general(part, ones, (dims, ((), ())), preferred_element_type=f32)
        for part in split3(x)
    ]
    return dots[0] + dots[1] + dots[2]


def as_bf16(mask):
    return mask.astype(f32).astype(bf16)


def slots_kernel(near_count, *refs):
    count = 8
    own, skel_out = refs[count : count + 2]
    held = refs[count + 2 : 2 * count + 2]
    semaphores = refs[2 * count + 2]
    copies = [
        pltpu.make_async_copy(refs[i], held[i], semaphores.at[i]) for i in range(count)
    ]
    for copy in copies:
        copy.start()
    order, points, charges, near_pairs = held[:4]
    source_basis, transfer, skeleton_points, top_points = held[4:]
    for copy in copies[:4]:
        copy.wait()
    low = order[...] & (LANES - 1)
    high = order[...] >> 7
    sub = iota((8, LANES), 0)
    tables = []
    for row in range(ROWS):
        xyz = points[:, row * LANES : (row + 1) * LANES]
        charge = charges[row : row + 1, :]
        tables.append(jnp.concatenate([xyz, charge, xyz, charge], axis=0))
    tiles = []
    for tile in range(CLUSTERS):
        first = 4 * (tile // 2) + tile % 2
        low_tile = jnp.where(sub < 4, low[first : first + 1], low[first + 2 : first + 3])
        high_tile = jnp.where(sub < 4, high[first : first + 1], high[first + 2 : first + 3])
        values = jnp.zeros((8, LANES), f32)
        for row in range(ROWS):
            found = jnp.take_along_axis(tables[row], low_tile, axis=1)
            values = jnp.where(high_tile == row, found, values)
        own[8 * tile : 8 * tile + 8, :] = values
        tiles.append(values)

    pairs = jnp.where(iota((2, 64), 1) < near_count[0], near_pairs[...] + 1, 0).astype(f32)
    own[128:136, :] = jnp.zeros((8, LANES), f32)
    own[128:130, 0:64] = pairs
    for copy in copies[4:]:
        copy.wait()

    lane = iota((R, LANES), 1)
    skel = jnp.zeros((R, LANES), f32)
    for cluster in range(CLUSTERS):
        block, place = cluster // 2, 4 * (cluster % 2) + 3
        basis = source_basis[:, cluster * C : (cluster + 1) * C]
        product = (
            basis[:, :LANES] * tiles[2 * block][place : place + 1]
            + basis[:, LANES:] * tiles[2 * block + 1][place : place + 1]
        )
        skel = jnp.where(lane == cluster, jnp.sum(product, axis=1, keepdims=True), skel)
    skel_rows = skel.T[:CLUSTERS, :]
    long_lane = iota((R, CLUSTERS * R), 1)
    repeat = as_bf16(long_lane % R == iota((R, CLUSTERS * R), 0))
    tiled = parts_dot(skel_rows, repeat, ((1,), (0,)))
    mine = iota((CLUSTERS, CLUSTERS * R), 1) // R == iota((CLUSTERS, CLUSTERS * R), 0)
    flat = jnp.sum(jnp.where(mine, tiled, 0.0), axis=0, keepdims=True)
    partial = jnp.sum(transfer[...] * flat, axis=1, keepdims=True)
    skel = jnp.where(lane == CLUSTERS, partial, skel)
    to_charge = as_bf16(lane == iota((R, LANES), 0) + 3 * R)
    record = parts_dot(skel.T[:SKEL_REC, :], to_charge, ((1,), (0,)))
    fold = as_bf16(iota((CLUSTERS * R, LANES), 1) % R == iota((CLUSTERS * R, LANES), 0) % R)
    short_lane = iota((CLUSTERS, LANES), 1) // R
    geometry = jnp.zeros((CLUSTERS, LANES), f32)
    for axis in range(3):
        masked = jnp.where(mine, skeleton_points[axis : axis + 1, :], 0.0)
        folded = parts_dot(masked, fold, ((1,), (0,)))
        geometry = jnp.where(short_lane == axis, folded, geometry)
    spread = as_bf16(lane % R == iota((R, LANES), 0))
    top = parts_dot(top_points[...], spread, ((1,), (0,)))
    top_mine = iota((3, LANES), 1) // R == iota((3, LANES), 0)
    top_row = jnp.sum(jnp.where(top_mine, top, 0.0), axis=0, keepdims=True)
    last = jnp.where(iota((8, LANES), 0) == 1, top_row, 0.0)
    record = record + jnp.concatenate([geometry, last], axis=0)
    for device in range(NARROW):
        skel_out[device] = record


def top_kernel(skels, top_message):
    last = skels[0, CLUSTERS:SKEL_REC, :]
    row = last[0:1] + last[1:2]
    for device in range(1, NARROW):
        row = row + skels[device, CLUSTERS:SKEL_REC, :][0:1]
    top_message[...] = jnp.broadcast_to(row, top_message.shape)


def strip_kernel(place, skels, chip_own, own, next_own, top_message, strip):
    del top_message
    odd = (place[0:1, 1:2] & 1) == 1
    strip[0:64, :] = jnp.where(odd, chip_own[64:128, :], next_own[64:128, :])
    strip[64:192, :] = own[0:128, :]
    strip[192:256, :] = jnp.where(odd, next_own[0:64, :], chip_own[0:64, :])
    pairs = [ref[128:130, :] for ref in (chip_own, own, next_own)]
    pairs.append(jnp.zeros((2, LANES), f32))
    strip[PAIR_ROW : PAIR_ROW + 8, :] = jnp.concatenate(pairs, axis=0)
    for device in range(NARROW):
        start = SKEL_ROW + device * CLUSTERS
        strip[start : start + CLUSTERS, :] = skels[device, :CLUSTERS, :]


def with_norms(halves, origin):
    out = []
    for half in halves:
        sub = iota((8, LANES), 0)
        shifted = jnp.where(sub < 3, half - origin, 0.0)
        norms = jnp.sum(shifted * shifted, axis=0, keepdims=True)
        out.append((shifted, norms))
    return out


def source_features(halves, origin):
    sub = iota((8, LANES), 0)
    columns = []
    for shifted, norms in with_norms(halves, origin):
        rows = jnp.where(sub < 3, shifted, jnp.where(sub == 4, norms, 0.0))
        rows = jnp.where(sub == 5, 1.0, rows)
        high, mid, low = [part.astype(f32) for part in split3(rows)]
        columns.append(jnp.concatenate([high, mid, high, mid, low, high], axis=0).astype(bf16))
    return jnp.concatenate(columns, axis=1)


def target_features(halves, origin):
    sub = iota((8, LANES), 0)
    columns = []
    for shifted, norms in with_norms(halves, origin):
        rows = jnp.where(sub < 3, -2.0 * shifted, jnp.where(sub == 5, norms + soft_square, 0.0))
        rows = jnp.where(sub == 4, 1.0, rows)
        high, mid, low = [part.astype(f32) for part in split3(rows)]
        columns.append(jnp.concatenate([high, high, mid, mid, high, low], axis=0))
    return columns


def cluster_halves(ref, block, odd):
    halves = []
    for half in range(2):
        tile = ref[pl.ds(pl.multiple_of(16 * block + 8 * half, 8), 8), :]
        halves.append(pltpu.roll(tile, 4, 0) if odd else tile)
    return halves


def own_origin(ref, start):
    whole = jnp.zeros((8, LANES), f32)
    for tile in range(CLUSTERS):
        whole = whole + ref[start + 8 * tile : start + 8 * tile + 8, :]
    mean = jnp.sum(whole, axis=1, keepdims=True) * (1.0 / (CLUSTERS * C))
    mean = jnp.broadcast_to(mean, (8, LANES))
    return jnp.where(iota((8, LANES), 0) < 3, mean + pltpu.roll(mean, 4, 0), 0.0)


def kernel_sums(square, charge_low, charge_high):
    inverse = lax.rsqrt(jnp.maximum(square, soft_square))
    return inverse[:, :LANES] * charge_low + inverse[:, LANES:] * charge_high


def put_source(features, charge, slot, halves, origin):
    features[slot] = source_features(halves, origin)
    for half in range(2):
        row = halves[half][3:4]
        charge[slot, :, half * LANES : (half + 1) * LANES] = jnp.broadcast_to(row, (8, LANES))


def pair_rows(refs):
    targets, sources = [], []
    for ref in refs:
        for block in range(3):
            start = PAIR_ROW + 2 * block
            targets.append(ref[start : start + 1, :])
            sources.append(ref[start + 1 : start + 2, :])
    return targets, sources


def list_entries(place, own_rows, other_rows, inner, out):
    wide_index = place[0:1, 0:1].astype(f32)
    narrow_index = place[0:1, 1:2].astype(f32)
    count_rows = len(own_rows)
    base = wide_index * GROUP + narrow_index * CLUSTERS + 1.0
    nothing = [jnp.zeros((16 - count_rows, LANES), f32)]
    own_ids = jnp.concatenate(own_rows + nothing, axis=0)
    other_ids = jnp.concatenate(other_rows + nothing, axis=0)
    local = own_ids - base
    other = other_ids - 1.0
    group = jnp.floor(other * (1.0 / GROUP))
    rest = other - GROUP * group
    depth = jnp.floor(rest * (1.0 / WIDTH))
    column = rest - WIDTH * depth
    group_step = group - (wide_index - 1.0)
    depth_step = depth - (2.0 * narrow_index - 1.0)
    slot = depth_step * WIDTH + column
    if inner:
        wanted = group_step == 1.0
    else:
        wanted = group_step != 1.0
        odd = wide_index - 2.0 * jnp.floor(0.5 * wide_index)
        second = jnp.where(group_step > 1.0, 1.0 - odd, odd)
        slot = slot + STRIP_CLUSTERS * second
    used = wanted & (local >= 0.0) & (local < CLUSTERS) & (own_ids > 0.0)
    count = used.astype(f32)
    upto = as_bf16(iota((LANES, LANES), 0) <= iota((LANES, LANES), 1))
    inclusive = jnp.dot(count.astype(bf16), upto, preferred_element_type=f32)
    totals = jnp.sum(count, axis=1, keepdims=True)
    row_of = iota((16, LANES), 0)
    offset = jnp.zeros((16, LANES), f32)
    for row in range(count_rows):
        offset = jnp.where(row_of > row, offset + totals[row : row + 1], offset)
    spot = jnp.where(used, inclusive - count + offset, -1.0)
    slot = jnp.where(used, slot, 0.0)
    local = jnp.where(used, local, 0.0)
    spot_high = jnp.floor(spot * (1.0 / LANES))
    spot_low = spot - LANES * spot_high
    listed = jnp.zeros((16, LANES), f32)
    eight = iota((8, LANES), 0).astype(f32)
    tall = iota((LANES, LANES), 0).astype(f32)
    for row in range(count_rows):
        here = eight == spot_high[row : row + 1]
        values = jnp.concatenate(
            [
                jnp.where(here, local[row : row + 1], 0.0),
                jnp.where(here, slot[row : row + 1], 0.0),
            ],
            axis=0,
        ).astype(bf16)
        hot = as_bf16(tall == spot_low[row : row + 1])
        listed = listed + lax.dot_general(
            values, hot, (((1,), (1,)), ((), ())), preferred_element_type=f32
        )
    coded = listed[:8] * float(GROUP) + listed[8:]
    out[...] = jnp.where(eight == 7.0, jnp.sum(totals), coded).astype(i32)


def add_pairs(entries, lhs, features, charge, dummy, sums):
    pair_total = entries[7, 0]

    def pair_steps(first, turns, carry):
        for turn in range(turns):
            index = first + turn
            code = entries[index >> 7, index & (LANES - 1)]
            live = index < pair_total
            cluster = jnp.where(live, code >> 7, 0)
            slot = jnp.where(live, code & (LANES - 1), dummy)
            right = features[slot]
            charge_low = charge[slot, 0:1, 0:LANES]
            charge_high = charge[slot, 0:1, LANES:C]
            for start in range(0, C, CHUNK):
                square = jnp.dot(
                    lhs[cluster, start : start + CHUNK, :], right, preferred_element_type=f32
                )
                sums[turn % SUMS][cluster, start : start + CHUNK, :] += kernel_sums(
                    square, charge_low, charge_high
                )
        return carry

    steps = (pair_total + UNROLL - 1) // UNROLL
    lax.fori_loop(
        0, steps // 2, lambda step, carry: pair_steps(2 * UNROLL * step, 2 * UNROLL, carry), 0
    )
    lax.fori_loop(
        2 * (steps // 2), steps, lambda step, carry: pair_steps(UNROLL * step, UNROLL, carry), 0
    )


def summed_row(sums, cluster, half):
    rows = slice(half * LANES, (half + 1) * LANES)
    total = sums[0][cluster, rows, :] + sums[1][cluster, rows, :]
    return kernel_scale * jnp.sum(total.T, axis=0, keepdims=True)


def inner_kernel(
    place, strip, lhs, near, features, charge, listed, entries, semaphore, *rest
):
    first_sum, second_sum, own_lhs = rest
    targets, sources = pair_rows((strip,))
    list_entries(place, sources + [targets[1]], targets + [sources[1]], True, listed)
    copy = pltpu.make_async_copy(listed, entries, semaphore)
    copy.start()
    origin = own_origin(strip, 64)

    def own_step(block, carry):
        for odd in range(2):
            cluster = 2 * block + odd
            halves = cluster_halves(strip, block + 4, odd)
            for half, column in enumerate(target_features(halves, origin)):
                lhs[cluster, half * LANES : (half + 1) * LANES, :] = column.T.astype(bf16)
            centre = jnp.sum(halves[0] + halves[1], axis=1, keepdims=True) * (1.0 / C)
            for half, column in enumerate(target_features(halves, centre)):
                own_lhs[cluster, :, half * LANES : (half + 1) * LANES] = column.astype(bf16)
            put_source(features, charge, SELF + cluster, halves, centre)
        return carry

    lax.fori_loop(0, CLUSTERS // 2, own_step, 0, unroll=4)

    def strip_step(block, carry):
        for odd in range(2):
            put_source(features, charge, 2 * block + odd, cluster_halves(strip, block, odd), origin)
        return carry

    lax.fori_loop(0, STRIP_CLUSTERS // 2, strip_step, 0, unroll=2)
    features[STRIP_CLUSTERS] = jnp.zeros((DEPTH, C), bf16)
    charge[STRIP_CLUSTERS] = jnp.zeros((8, C), f32)

    def self_step(step, carry):
        for turn in range(UNROLL):
            cluster = step * UNROLL + turn
            square = lax.dot_general(
                own_lhs[cluster],
                features[SELF + cluster],
                (((0,), (0,)), ((), ())),
                preferred_element_type=f32,
            )
            first_sum[cluster] = kernel_sums(
                square,
                charge[SELF + cluster, 0:1, 0:LANES],
                charge[SELF + cluster, 0:1, LANES:C],
            )
            second_sum[cluster] = jnp.zeros((C, LANES), f32)
        return carry

    lax.fori_loop(0, CLUSTERS // UNROLL, self_step, 0)
    copy.wait()
    add_pairs(entries, lhs, features, charge, STRIP_CLUSTERS, (first_sum, second_sum))
    for cluster in range(CLUSTERS):
        for half in range(2):
            row = 2 * cluster + half
            near[row : row + 1, :] = summed_row((first_sum, second_sum), cluster, half)


def outer_kernel(
    place,
    first_strip,
    strip,
    second_strip,
    lhs,
    inner,
    near,
    features,
    charge,
    listed,
    entries,
    semaphore,
    *sums,
):
    targets, sources = pair_rows((first_strip, second_strip))
    own_targets, own_sources = pair_rows((strip,))
    list_entries(
        place, sources + [own_targets[1]], targets + [own_sources[1]], False, listed
    )
    copy = pltpu.make_async_copy(listed, entries, semaphore)
    copy.start()
    for total in sums:
        total[...] = jnp.zeros(total.shape, f32)
    origin = own_origin(strip, 64)

    def window_step(block, carry):
        for part, ref in enumerate((first_strip, second_strip)):
            for odd in range(2):
                slot = part * STRIP_CLUSTERS + 2 * block + odd
                put_source(features, charge, slot, cluster_halves(ref, block, odd), origin)
        return carry

    lax.fori_loop(0, STRIP_CLUSTERS // 2, window_step, 0, unroll=2)
    features[OUTER] = jnp.zeros((DEPTH, C), bf16)
    charge[OUTER] = jnp.zeros((8, C), f32)
    copy.wait()
    add_pairs(entries, lhs, features, charge, OUTER, sums)
    for cluster in range(CLUSTERS):
        for half in range(2):
            row = 2 * cluster + half
            near[row : row + 1, :] = inner[row : row + 1, :] + summed_row(sums, cluster, half)


def far_kernel(
    far_count,
    place,
    first_strip,
    strip,
    second_strip,
    top,
    far_pairs,
    near,
    order,
    target_basis,
    potential,
    total,
):
    group_first = place[0:1, 0:1] * GROUP
    target = far_pairs[0:1, :] - group_first
    source = far_pairs[1:2, :]
    is_leaf = far_pairs[2:3, :] == 0
    live = iota((1, LANES), 1) < far_count[0]
    sign = 1 - 2 * (place[0:1, 0:1] & 1)
    offset = source - group_first
    leaf = (1 + sign * (offset >> 7)) * GROUP + (offset & (GROUP - 1))
    index = jnp.where(is_leaf, leaf, source + 3 * GROUP)
    skel = slice(SKEL_ROW, SKEL_ROW + GROUP)
    tops = top[pl.ds(0, top.shape[0] // TOP_ROWS, stride=TOP_ROWS), :]
    table = jnp.concatenate([first_strip[skel, :], strip[skel, :], second_strip[skel, :], tops], axis=0)
    chosen = as_bf16(iota((table.shape[0], LANES), 0) == index)
    over_rows = ((0,), (0,))
    sources = parts_dot(table, chosen, over_rows)
    own_chosen = as_bf16(iota((GROUP, LANES), 0) == target)
    targets = parts_dot(strip[skel, :], own_chosen, over_rows)
    target = target - place[0:1, 1:2] * CLUSTERS
    rows = []
    for a in range(R):
        square = soft_square
        for axis in range(3):
            offset = sources[axis * R : (axis + 1) * R] - targets[axis * R + a : axis * R + a + 1]
            square = square + offset * offset
        product = lax.rsqrt(square) * sources[3 * R :]
        rows.append(jnp.sum(product, axis=0, keepdims=True))
    middle = jnp.where(live, jnp.concatenate(rows, axis=0) * kernel_scale, 0.0)
    for cluster in range(CLUSTERS):
        column = jnp.sum(jnp.where(target == cluster, middle, 0.0), axis=1, keepdims=True)
        spread = jnp.sum(
            target_basis[:, cluster * C : (cluster + 1) * C] * column, axis=0, keepdims=True
        )
        for half in range(2):
            row = 2 * cluster + half
            total[row : row + 1, :] = (
                near[row : row + 1, :] + spread[:, half * LANES : (half + 1) * LANES]
            )
    low = order[...] & (LANES - 1)
    high = order[...] >> 7
    tall = iota((LANES, LANES), 0)
    wide = iota((ROWS, LANES), 0)
    whole = [part.astype(f32) for part in split3(total[...])]
    values, places = [], []
    for row in range(ROWS):
        here = wide == high[row : row + 1]
        parts = [jnp.where(here, part[row : row + 1, :], 0.0) for part in whole]
        values.append(jnp.concatenate(parts, axis=0).astype(bf16))
        places.append(as_bf16(tall == low[row : row + 1]))
    placed = lax.dot_general(
        jnp.concatenate(values, axis=1),
        jnp.concatenate(places, axis=1),
        (((1,), (1,)), ((), ())),
        preferred_element_type=f32,
    )
    out = placed[:ROWS] + placed[ROWS : 2 * ROWS] + placed[2 * ROWS :]
    potential[...] = out


def smem():
    return pl.BlockSpec(memory_space=pltpu.SMEM)


def in_hbm():
    return pl.BlockSpec(memory_space=pltpu.HBM)


def vmem():
    return pl.BlockSpec(memory_space=pltpu.VMEM)


params = pltpu.CompilerParams(vmem_limit_bytes=50 * 1024 * 1024)
first_params = pltpu.CompilerParams(vmem_limit_bytes=127 * 512 * 1024)


def local(
    points,
    charges,
    order,
    source_basis,
    target_basis,
    skeleton_points,
    transfer,
    top_points,
    near_pairs,
    near_count,
    far_pairs,
    far_count,
):
    wide_size = lax.axis_size("wide")
    narrow_size = lax.axis_size("narrow")
    place = jnp.stack([lax.axis_index("wide"), lax.axis_index("narrow")]).astype(i32).reshape(1, 2)
    order = order.reshape(ROWS, LANES)
    shape = jax.ShapeDtypeStruct
    inputs = (
        order,
        points,
        charges.reshape(ROWS, LANES),
        near_pairs,
        source_basis,
        transfer,
        skeleton_points,
        top_points,
    )
    with jax.named_scope("slots"):
        own, skel = pl.pallas_call(
            slots_kernel,
            out_shape=(
                shape((136, LANES), f32),
                shape((NARROW, SKEL_REC, LANES), f32),
            ),
            in_specs=[smem()] + [in_hbm()] * len(inputs),
            out_specs=[vmem()] * 2,
            scratch_shapes=[pltpu.VMEM(x.shape, x.dtype) for x in inputs]
            + [pltpu.SemaphoreType.DMA((len(inputs),))],
            compiler_params=first_params,
        )(near_count, *inputs)
    skels = lax.all_to_all(skel, "narrow", 0, 0, tiled=True)
    in_chip = [(i, i + 1) for i in range(0, narrow_size - 1, 2)]
    next_chip = [(i, i + 1) for i in range(1, narrow_size - 1, 2)]
    chip_own = lax.ppermute(own, "narrow", in_chip + [(j, i) for i, j in in_chip])
    next_own = lax.ppermute(own, "narrow", next_chip + [(j, i) for i, j in next_chip])
    with jax.named_scope("top"):
        top_message = pl.pallas_call(
            top_kernel,
            out_shape=shape((TOP_ROWS * wide_size, LANES), f32),
            in_specs=[vmem()],
            out_specs=vmem(),
            compiler_params=params,
        )(skels)
    tops = lax.all_to_all(top_message, "wide", 0, 0, tiled=True)
    with jax.named_scope("strip"):
        strip = pl.pallas_call(
            strip_kernel,
            out_shape=shape((STRIP_ROWS, LANES), f32),
            in_specs=[vmem()] * 6,
            out_specs=vmem(),
            compiler_params=params,
        )(place, skels, chip_own, own, next_own, top_message)
    odd_even = [(i, i + 1) for i in range(1, wide_size - 1, 2)]
    even_odd = [(i, i + 1) for i in range(0, wide_size - 1, 2)]
    first_strip = lax.ppermute(strip, "wide", odd_even + [(j, i) for i, j in odd_even])
    second_strip = lax.ppermute(strip, "wide", even_odd + [(j, i) for i, j in even_odd])
    def near_scratch(slots):
        return [
            pltpu.VMEM((slots, DEPTH, C), bf16),
            pltpu.VMEM((slots, 8, C), f32),
            pltpu.VMEM((8, LANES), i32),
            pltpu.SMEM((8, LANES), i32),
            pltpu.SemaphoreType.DMA(()),
        ] + [pltpu.VMEM((CLUSTERS, C, LANES), f32)] * SUMS

    with jax.named_scope("inner"):
        lhs, inner = pl.pallas_call(
            inner_kernel,
            out_shape=(shape((CLUSTERS, C, DEPTH), bf16), shape((ROWS, LANES), f32)),
            in_specs=[vmem()] * 2,
            out_specs=[vmem()] * 2,
            scratch_shapes=near_scratch(SELF + CLUSTERS)
            + [pltpu.VMEM((CLUSTERS, DEPTH, C), bf16)],
            compiler_params=params,
        )(place, strip)
    with jax.named_scope("outer"):
        near = pl.pallas_call(
            outer_kernel,
            out_shape=shape((ROWS, LANES), f32),
            in_specs=[vmem()] * 6,
            out_specs=vmem(),
            scratch_shapes=near_scratch(OUTER + 1),
            compiler_params=params,
        )(place, first_strip, strip, second_strip, lhs, inner)
    with jax.named_scope("far"):
        potential = pl.pallas_call(
            far_kernel,
            out_shape=shape((ROWS, LANES), f32),
            in_specs=[smem()] + [vmem()] * 9,
            out_specs=vmem(),
            scratch_shapes=[pltpu.VMEM((ROWS, LANES), f32)],
            compiler_params=params,
        )(far_count, place, first_strip, strip, second_strip, tops, far_pairs, near, order, target_basis)
    return potential.reshape(-1)


def solution(mesh):
    both = ("wide", "narrow")
    split = P(None, both)
    return jax.shard_map(
        local,
        mesh=mesh,
        in_specs=(
            split,
            P(both),
            P(both),
            split,
            split,
            split,
            split,
            P(None, "wide"),
            split,
            P(both),
            split,
            P(both),
        ),
        out_specs=P(both),
        check_vma=False,
    )
```

```python
import jax
import jax.numpy as jnp
from jax import lax
from jax.experimental import pallas as pl
from jax.experimental.pallas import tpu as pltpu
from jax.sharding import PartitionSpec as P

C = 256
R = 32
LANES = 128
CLUSTERS = 16
ROWS = 32
NARROW = 8
GROUP = 128
WIDTH = 8
STRIP_CLUSTERS = 32
PAIR_ROW = 8 * STRIP_CLUSTERS
SKEL_ROW = PAIR_ROW + 8
STRIP_ROWS = SKEL_ROW + GROUP
SKEL_REC = 24
TOP_ROWS = 2
OUTER = 2 * STRIP_CLUSTERS
SELF = STRIP_CLUSTERS + 1
DEPTH = 48
UNROLL = 8
SUMS = 2
CHUNK = 64

soft_square = 0.01
kernel_scale = 0.07957747154594767
f32 = jnp.float32
bf16 = jnp.bfloat16
i32 = jnp.int32


def iota(shape, dim):
    return lax.broadcasted_iota(i32, shape, dim)


def split3(x):
    high = x.astype(bf16)
    rest = x - high.astype(f32)
    mid = rest.astype(bf16)
    low = (rest - mid.astype(f32)).astype(bf16)
    return high, mid, low


def parts_dot(x, ones, dims):
    dots = [
        lax.dot_general(part, ones, (dims, ((), ())), preferred_element_type=f32)
        for part in split3(x)
    ]
    return dots[0] + dots[1] + dots[2]


def as_bf16(mask):
    return mask.astype(f32).astype(bf16)


def slots_kernel(near_count, *refs):
    count = 8
    own, skel_out = refs[count : count + 2]
    held = refs[count + 2 : 2 * count + 2]
    semaphores = refs[2 * count + 2]
    copies = [
        pltpu.make_async_copy(refs[i], held[i], semaphores.at[i]) for i in range(count)
    ]
    for copy in copies:
        copy.start()
    order, points, charges, near_pairs = held[:4]
    source_basis, transfer, skeleton_points, top_points = held[4:]
    for copy in copies[:4]:
        copy.wait()
    low = order[...] & (LANES - 1)
    high = order[...] >> 7
    sub = iota((8, LANES), 0)
    tables = []
    for row in range(ROWS):
        xyz = points[:, row * LANES : (row + 1) * LANES]
        charge = charges[row : row + 1, :]
        tables.append(jnp.concatenate([xyz, charge, xyz, charge], axis=0))
    tiles = []
    for tile in range(CLUSTERS):
        first = 4 * (tile // 2) + tile % 2
        low_tile = jnp.where(sub < 4, low[first : first + 1], low[first + 2 : first + 3])
        high_tile = jnp.where(sub < 4, high[first : first + 1], high[first + 2 : first + 3])
        values = jnp.zeros((8, LANES), f32)
        for row in range(ROWS):
            found = jnp.take_along_axis(tables[row], low_tile, axis=1)
            values = jnp.where(high_tile == row, found, values)
        own[8 * tile : 8 * tile + 8, :] = values
        tiles.append(values)

    pairs = jnp.where(iota((2, 64), 1) < near_count[0], near_pairs[...] + 1, 0).astype(f32)
    own[128:136, :] = jnp.zeros((8, LANES), f32)
    own[128:130, 0:64] = pairs
    for copy in copies[4:]:
        copy.wait()

    lane = iota((R, LANES), 1)
    skel = jnp.zeros((R, LANES), f32)
    for cluster in range(CLUSTERS):
        block, place = cluster // 2, 4 * (cluster % 2) + 3
        basis = source_basis[:, cluster * C : (cluster + 1) * C]
        product = (
            basis[:, :LANES] * tiles[2 * block][place : place + 1]
            + basis[:, LANES:] * tiles[2 * block + 1][place : place + 1]
        )
        skel = jnp.where(lane == cluster, jnp.sum(product, axis=1, keepdims=True), skel)
    skel_rows = skel.T[:CLUSTERS, :]
    long_lane = iota((R, CLUSTERS * R), 1)
    repeat = as_bf16(long_lane % R == iota((R, CLUSTERS * R), 0))
    tiled = parts_dot(skel_rows, repeat, ((1,), (0,)))
    mine = iota((CLUSTERS, CLUSTERS * R), 1) // R == iota((CLUSTERS, CLUSTERS * R), 0)
    flat = jnp.sum(jnp.where(mine, tiled, 0.0), axis=0, keepdims=True)
    partial = jnp.sum(transfer[...] * flat, axis=1, keepdims=True)
    skel = jnp.where(lane == CLUSTERS, partial, skel)
    to_charge = as_bf16(lane == iota((R, LANES), 0) + 3 * R)
    record = parts_dot(skel.T[:SKEL_REC, :], to_charge, ((1,), (0,)))
    fold = as_bf16(iota((CLUSTERS * R, LANES), 1) % R == iota((CLUSTERS * R, LANES), 0) % R)
    short_lane = iota((CLUSTERS, LANES), 1) // R
    geometry = jnp.zeros((CLUSTERS, LANES), f32)
    for axis in range(3):
        masked = jnp.where(mine, skeleton_points[axis : axis + 1, :], 0.0)
        folded = parts_dot(masked, fold, ((1,), (0,)))
        geometry = jnp.where(short_lane == axis, folded, geometry)
    spread = as_bf16(lane % R == iota((R, LANES), 0))
    top = parts_dot(top_points[...], spread, ((1,), (0,)))
    top_mine = iota((3, LANES), 1) // R == iota((3, LANES), 0)
    top_row = jnp.sum(jnp.where(top_mine, top, 0.0), axis=0, keepdims=True)
    last = jnp.where(iota((8, LANES), 0) == 1, top_row, 0.0)
    record = record + jnp.concatenate([geometry, last], axis=0)
    for device in range(NARROW):
        skel_out[device] = record


def top_kernel(skels, top_message):
    last = skels[0, CLUSTERS:SKEL_REC, :]
    row = last[0:1] + last[1:2]
    for device in range(1, NARROW):
        row = row + skels[device, CLUSTERS:SKEL_REC, :][0:1]
    top_message[...] = jnp.broadcast_to(row, top_message.shape)


def strip_kernel(place, skels, chip_own, own, next_own, top_message, strip):
    del top_message
    odd = (place[0:1, 1:2] & 1) == 1
    strip[0:64, :] = jnp.where(odd, chip_own[64:128, :], next_own[64:128, :])
    strip[64:192, :] = own[0:128, :]
    strip[192:256, :] = jnp.where(odd, next_own[0:64, :], chip_own[0:64, :])
    pairs = [ref[128:130, :] for ref in (chip_own, own, next_own)]
    pairs.append(jnp.zeros((2, LANES), f32))
    strip[PAIR_ROW : PAIR_ROW + 8, :] = jnp.concatenate(pairs, axis=0)
    for device in range(NARROW):
        start = SKEL_ROW + device * CLUSTERS
        strip[start : start + CLUSTERS, :] = skels[device, :CLUSTERS, :]


def with_norms(halves, origin):
    out = []
    for half in halves:
        sub = iota((8, LANES), 0)
        shifted = jnp.where(sub < 3, half - origin, 0.0)
        norms = jnp.sum(shifted * shifted, axis=0, keepdims=True)
        out.append((shifted, norms))
    return out


def source_features(halves, origin):
    sub = iota((8, LANES), 0)
    columns = []
    for shifted, norms in with_norms(halves, origin):
        rows = jnp.where(sub < 3, shifted, jnp.where(sub == 4, norms, 0.0))
        rows = jnp.where(sub == 5, 1.0, rows)
        high, mid, low = [part.astype(f32) for part in split3(rows)]
        columns.append(jnp.concatenate([high, mid, high, mid, low, high], axis=0).astype(bf16))
    return jnp.concatenate(columns, axis=1)


def target_features(halves, origin):
    sub = iota((8, LANES), 0)
    columns = []
    for shifted, norms in with_norms(halves, origin):
        rows = jnp.where(sub < 3, -2.0 * shifted, jnp.where(sub == 5, norms + soft_square, 0.0))
        rows = jnp.where(sub == 4, 1.0, rows)
        high, mid, low = [part.astype(f32) for part in split3(rows)]
        columns.append(jnp.concatenate([high, high, mid, mid, high, low], axis=0))
    return columns


def cluster_halves(ref, block, odd):
    halves = []
    for half in range(2):
        tile = ref[pl.ds(pl.multiple_of(16 * block + 8 * half, 8), 8), :]
        halves.append(pltpu.roll(tile, 4, 0) if odd else tile)
    return halves


def own_origin(ref, start):
    whole = jnp.zeros((8, LANES), f32)
    for tile in range(CLUSTERS):
        whole = whole + ref[start + 8 * tile : start + 8 * tile + 8, :]
    mean = jnp.sum(whole, axis=1, keepdims=True) * (1.0 / (CLUSTERS * C))
    mean = jnp.broadcast_to(mean, (8, LANES))
    return jnp.where(iota((8, LANES), 0) < 3, mean + pltpu.roll(mean, 4, 0), 0.0)


def kernel_sums(square, charge_low, charge_high):
    inverse = lax.rsqrt(jnp.maximum(square, soft_square))
    return inverse[:, :LANES] * charge_low + inverse[:, LANES:] * charge_high


def put_source(features, charge, slot, halves, origin):
    features[slot] = source_features(halves, origin)
    for half in range(2):
        row = halves[half][3:4]
        charge[slot, :, half * LANES : (half + 1) * LANES] = jnp.broadcast_to(row, (8, LANES))


def pair_rows(refs):
    targets, sources = [], []
    for ref in refs:
        for block in range(3):
            start = PAIR_ROW + 2 * block
            targets.append(ref[start : start + 1, :])
            sources.append(ref[start + 1 : start + 2, :])
    return targets, sources


def list_entries(place, own_rows, other_rows, inner, out):
    wide_index = place[0:1, 0:1].astype(f32)
    narrow_index = place[0:1, 1:2].astype(f32)
    count_rows = len(own_rows)
    base = wide_index * GROUP + narrow_index * CLUSTERS + 1.0
    nothing = [jnp.zeros((16 - count_rows, LANES), f32)]
    own_ids = jnp.concatenate(own_rows + nothing, axis=0)
    other_ids = jnp.concatenate(other_rows + nothing, axis=0)
    local = own_ids - base
    other = other_ids - 1.0
    group = jnp.floor(other * (1.0 / GROUP))
    rest = other - GROUP * group
    depth = jnp.floor(rest * (1.0 / WIDTH))
    column = rest - WIDTH * depth
    group_step = group - (wide_index - 1.0)
    depth_step = depth - (2.0 * narrow_index - 1.0)
    slot = depth_step * WIDTH + column
    if inner:
        wanted = group_step == 1.0
    else:
        wanted = group_step != 1.0
        odd = wide_index - 2.0 * jnp.floor(0.5 * wide_index)
        second = jnp.where(group_step > 1.0, 1.0 - odd, odd)
        slot = slot + STRIP_CLUSTERS * second
    used = wanted & (local >= 0.0) & (local < CLUSTERS) & (own_ids > 0.0)
    count = used.astype(f32)
    upto = as_bf16(iota((LANES, LANES), 0) <= iota((LANES, LANES), 1))
    inclusive = jnp.dot(count.astype(bf16), upto, preferred_element_type=f32)
    totals = jnp.sum(count, axis=1, keepdims=True)
    row_of = iota((16, LANES), 0)
    offset = jnp.zeros((16, LANES), f32)
    for row in range(count_rows):
        offset = jnp.where(row_of > row, offset + totals[row : row + 1], offset)
    spot = jnp.where(used, inclusive - count + offset, -1.0)
    slot = jnp.where(used, slot, 0.0)
    local = jnp.where(used, local, 0.0)
    spot_high = jnp.floor(spot * (1.0 / LANES))
    spot_low = spot - LANES * spot_high
    listed = jnp.zeros((16, LANES), f32)
    eight = iota((8, LANES), 0).astype(f32)
    tall = iota((LANES, LANES), 0).astype(f32)
    for row in range(count_rows):
        here = eight == spot_high[row : row + 1]
        values = jnp.concatenate(
            [
                jnp.where(here, local[row : row + 1], 0.0),
                jnp.where(here, slot[row : row + 1], 0.0),
            ],
            axis=0,
        ).astype(bf16)
        hot = as_bf16(tall == spot_low[row : row + 1])
        listed = listed + lax.dot_general(
            values, hot, (((1,), (1,)), ((), ())), preferred_element_type=f32
        )
    coded = listed[:8] * float(GROUP) + listed[8:]
    out[...] = jnp.where(eight == 7.0, jnp.sum(totals), coded).astype(i32)


def add_pairs(entries, lhs, features, charge, dummy, sums):
    pair_total = entries[7, 0]

    def pair_steps(first, turns, carry):
        for turn in range(turns):
            index = first + turn
            code = entries[index >> 7, index & (LANES - 1)]
            live = index < pair_total
            cluster = jnp.where(live, code >> 7, 0)
            slot = jnp.where(live, code & (LANES - 1), dummy)
            right = features[slot]
            charge_low = charge[slot, 0:1, 0:LANES]
            charge_high = charge[slot, 0:1, LANES:C]
            for start in range(0, C, CHUNK):
                square = jnp.dot(
                    lhs[cluster, start : start + CHUNK, :], right, preferred_element_type=f32
                )
                sums[turn % SUMS][cluster, start : start + CHUNK, :] += kernel_sums(
                    square, charge_low, charge_high
                )
        return carry

    steps = (pair_total + UNROLL - 1) // UNROLL
    lax.fori_loop(
        0, steps // 2, lambda step, carry: pair_steps(2 * UNROLL * step, 2 * UNROLL, carry), 0
    )
    lax.fori_loop(
        2 * (steps // 2), steps, lambda step, carry: pair_steps(UNROLL * step, UNROLL, carry), 0
    )


def summed_row(sums, cluster, half):
    rows = slice(half * LANES, (half + 1) * LANES)
    total = sums[0][cluster, rows, :] + sums[1][cluster, rows, :]
    return kernel_scale * jnp.sum(total.T, axis=0, keepdims=True)


def inner_kernel(
    place, strip, lhs, near, features, charge, listed, entries, semaphore, *rest
):
    first_sum, second_sum, own_lhs = rest
    targets, sources = pair_rows((strip,))
    list_entries(place, sources + [targets[1]], targets + [sources[1]], True, listed)
    copy = pltpu.make_async_copy(listed, entries, semaphore)
    copy.start()
    origin = own_origin(strip, 64)

    def own_step(block, carry):
        for odd in range(2):
            cluster = 2 * block + odd
            halves = cluster_halves(strip, block + 4, odd)
            for half, column in enumerate(target_features(halves, origin)):
                lhs[cluster, half * LANES : (half + 1) * LANES, :] = column.T.astype(bf16)
            centre = jnp.sum(halves[0] + halves[1], axis=1, keepdims=True) * (1.0 / C)
            for half, column in enumerate(target_features(halves, centre)):
                own_lhs[cluster, :, half * LANES : (half + 1) * LANES] = column.astype(bf16)
            put_source(features, charge, SELF + cluster, halves, centre)
        return carry

    lax.fori_loop(0, CLUSTERS // 2, own_step, 0, unroll=8)

    def strip_step(block, carry):
        for odd in range(2):
            put_source(features, charge, 2 * block + odd, cluster_halves(strip, block, odd), origin)
        return carry

    lax.fori_loop(0, STRIP_CLUSTERS // 2, strip_step, 0, unroll=8)
    features[STRIP_CLUSTERS] = jnp.zeros((DEPTH, C), bf16)
    charge[STRIP_CLUSTERS] = jnp.zeros((8, C), f32)

    def self_step(step, carry):
        for turn in range(UNROLL):
            cluster = step * UNROLL + turn
            square = lax.dot_general(
                own_lhs[cluster],
                features[SELF + cluster],
                (((0,), (0,)), ((), ())),
                preferred_element_type=f32,
            )
            first_sum[cluster] = kernel_sums(
                square,
                charge[SELF + cluster, 0:1, 0:LANES],
                charge[SELF + cluster, 0:1, LANES:C],
            )
            second_sum[cluster] = jnp.zeros((C, LANES), f32)
        return carry

    lax.fori_loop(0, CLUSTERS // UNROLL, self_step, 0, unroll=2)
    copy.wait()
    add_pairs(entries, lhs, features, charge, STRIP_CLUSTERS, (first_sum, second_sum))
    for cluster in range(CLUSTERS):
        for half in range(2):
            row = 2 * cluster + half
            near[row : row + 1, :] = summed_row((first_sum, second_sum), cluster, half)


def outer_kernel(
    place,
    first_strip,
    strip,
    second_strip,
    lhs,
    inner,
    near,
    features,
    charge,
    listed,
    entries,
    semaphore,
    *sums,
):
    targets, sources = pair_rows((first_strip, second_strip))
    own_targets, own_sources = pair_rows((strip,))
    list_entries(
        place, sources + [own_targets[1]], targets + [own_sources[1]], False, listed
    )
    copy = pltpu.make_async_copy(listed, entries, semaphore)
    copy.start()
    for total in sums:
        total[...] = jnp.zeros(total.shape, f32)
    origin = own_origin(strip, 64)

    def window_step(block, carry):
        for part, ref in enumerate((first_strip, second_strip)):
            for odd in range(2):
                slot = part * STRIP_CLUSTERS + 2 * block + odd
                put_source(features, charge, slot, cluster_halves(ref, block, odd), origin)
        return carry

    lax.fori_loop(0, STRIP_CLUSTERS // 2, window_step, 0, unroll=4)
    features[OUTER] = jnp.zeros((DEPTH, C), bf16)
    charge[OUTER] = jnp.zeros((8, C), f32)
    copy.wait()
    add_pairs(entries, lhs, features, charge, OUTER, sums)
    for cluster in range(CLUSTERS):
        for half in range(2):
            row = 2 * cluster + half
            near[row : row + 1, :] = inner[row : row + 1, :] + summed_row(sums, cluster, half)


def far_kernel(
    far_count,
    place,
    first_strip,
    strip,
    second_strip,
    top,
    far_pairs,
    near,
    order,
    target_basis,
    potential,
    total,
):
    group_first = place[0:1, 0:1] * GROUP
    target = far_pairs[0:1, :] - group_first
    source = far_pairs[1:2, :]
    is_leaf = far_pairs[2:3, :] == 0
    live = iota((1, LANES), 1) < far_count[0]
    sign = 1 - 2 * (place[0:1, 0:1] & 1)
    offset = source - group_first
    leaf = (1 + sign * (offset >> 7)) * GROUP + (offset & (GROUP - 1))
    index = jnp.where(is_leaf, leaf, source + 3 * GROUP)
    skel = slice(SKEL_ROW, SKEL_ROW + GROUP)
    tops = top[pl.ds(0, top.shape[0] // TOP_ROWS, stride=TOP_ROWS), :]
    table = jnp.concatenate([first_strip[skel, :], strip[skel, :], second_strip[skel, :], tops], axis=0)
    chosen = as_bf16(iota((table.shape[0], LANES), 0) == index)
    over_rows = ((0,), (0,))
    sources = parts_dot(table, chosen, over_rows)
    own_chosen = as_bf16(iota((GROUP, LANES), 0) == target)
    targets = parts_dot(strip[skel, :], own_chosen, over_rows)
    target = target - place[0:1, 1:2] * CLUSTERS
    rows = []
    for a in range(R):
        square = soft_square
        for axis in range(3):
            offset = sources[axis * R : (axis + 1) * R] - targets[axis * R + a : axis * R + a + 1]
            square = square + offset * offset
        product = lax.rsqrt(square) * sources[3 * R :]
        rows.append(jnp.sum(product, axis=0, keepdims=True))
    middle = jnp.where(live, jnp.concatenate(rows, axis=0) * kernel_scale, 0.0)
    for cluster in range(CLUSTERS):
        column = jnp.sum(jnp.where(target == cluster, middle, 0.0), axis=1, keepdims=True)
        spread = jnp.sum(
            target_basis[:, cluster * C : (cluster + 1) * C] * column, axis=0, keepdims=True
        )
        for half in range(2):
            row = 2 * cluster + half
            total[row : row + 1, :] = (
                near[row : row + 1, :] + spread[:, half * LANES : (half + 1) * LANES]
            )
    low = order[...] & (LANES - 1)
    high = order[...] >> 7
    tall = iota((LANES, LANES), 0)
    wide = iota((ROWS, LANES), 0)
    whole = [part.astype(f32) for part in split3(total[...])]
    values, places = [], []
    for row in range(ROWS):
        here = wide == high[row : row + 1]
        parts = [jnp.where(here, part[row : row + 1, :], 0.0) for part in whole]
        values.append(jnp.concatenate(parts, axis=0).astype(bf16))
        places.append(as_bf16(tall == low[row : row + 1]))
    placed = lax.dot_general(
        jnp.concatenate(values, axis=1),
        jnp.concatenate(places, axis=1),
        (((1,), (1,)), ((), ())),
        preferred_element_type=f32,
    )
    out = placed[:ROWS] + placed[ROWS : 2 * ROWS] + placed[2 * ROWS :]
    potential[...] = out


def smem():
    return pl.BlockSpec(memory_space=pltpu.SMEM)


def in_hbm():
    return pl.BlockSpec(memory_space=pltpu.HBM)


def vmem():
    return pl.BlockSpec(memory_space=pltpu.VMEM)


params = pltpu.CompilerParams(vmem_limit_bytes=50 * 1024 * 1024)
first_params = pltpu.CompilerParams(vmem_limit_bytes=127 * 512 * 1024)


def local(
    points,
    charges,
    order,
    source_basis,
    target_basis,
    skeleton_points,
    transfer,
    top_points,
    near_pairs,
    near_count,
    far_pairs,
    far_count,
):
    wide_size = lax.axis_size("wide")
    narrow_size = lax.axis_size("narrow")
    place = jnp.stack([lax.axis_index("wide"), lax.axis_index("narrow")]).astype(i32).reshape(1, 2)
    order = order.reshape(ROWS, LANES)
    shape = jax.ShapeDtypeStruct
    inputs = (
        order,
        points,
        charges.reshape(ROWS, LANES),
        near_pairs,
        source_basis,
        transfer,
        skeleton_points,
        top_points,
    )
    with jax.named_scope("slots"):
        own, skel = pl.pallas_call(
            slots_kernel,
            out_shape=(
                shape((136, LANES), f32),
                shape((NARROW, SKEL_REC, LANES), f32),
            ),
            in_specs=[smem()] + [in_hbm()] * len(inputs),
            out_specs=[vmem()] * 2,
            scratch_shapes=[pltpu.VMEM(x.shape, x.dtype) for x in inputs]
            + [pltpu.SemaphoreType.DMA((len(inputs),))],
            compiler_params=first_params,
        )(near_count, *inputs)
    skels = lax.all_to_all(skel, "narrow", 0, 0, tiled=True)
    in_chip = [(i, i + 1) for i in range(0, narrow_size - 1, 2)]
    next_chip = [(i, i + 1) for i in range(1, narrow_size - 1, 2)]
    chip_own = lax.ppermute(own, "narrow", in_chip + [(j, i) for i, j in in_chip])
    next_own = lax.ppermute(own, "narrow", next_chip + [(j, i) for i, j in next_chip])
    with jax.named_scope("top"):
        top_message = pl.pallas_call(
            top_kernel,
            out_shape=shape((TOP_ROWS * wide_size, LANES), f32),
            in_specs=[vmem()],
            out_specs=vmem(),
            compiler_params=params,
        )(skels)
    tops = lax.all_to_all(top_message, "wide", 0, 0, tiled=True)
    with jax.named_scope("strip"):
        strip = pl.pallas_call(
            strip_kernel,
            out_shape=shape((STRIP_ROWS, LANES), f32),
            in_specs=[vmem()] * 6,
            out_specs=vmem(),
            compiler_params=params,
        )(place, skels, chip_own, own, next_own, top_message)
    odd_even = [(i, i + 1) for i in range(1, wide_size - 1, 2)]
    even_odd = [(i, i + 1) for i in range(0, wide_size - 1, 2)]
    first_strip = lax.ppermute(strip, "wide", odd_even + [(j, i) for i, j in odd_even])
    second_strip = lax.ppermute(strip, "wide", even_odd + [(j, i) for i, j in even_odd])
    def near_scratch(slots):
        return [
            pltpu.VMEM((slots, DEPTH, C), bf16),
            pltpu.VMEM((slots, 8, C), f32),
            pltpu.VMEM((8, LANES), i32),
            pltpu.SMEM((8, LANES), i32),
            pltpu.SemaphoreType.DMA(()),
        ] + [pltpu.VMEM((CLUSTERS, C, LANES), f32)] * SUMS

    with jax.named_scope("inner"):
        lhs, inner = pl.pallas_call(
            inner_kernel,
            out_shape=(shape((CLUSTERS, C, DEPTH), bf16), shape((ROWS, LANES), f32)),
            in_specs=[vmem()] * 2,
            out_specs=[vmem()] * 2,
            scratch_shapes=near_scratch(SELF + CLUSTERS)
            + [pltpu.VMEM((CLUSTERS, DEPTH, C), bf16)],
            compiler_params=params,
        )(place, strip)
    with jax.named_scope("outer"):
        near = pl.pallas_call(
            outer_kernel,
            out_shape=shape((ROWS, LANES), f32),
            in_specs=[vmem()] * 6,
            out_specs=vmem(),
            scratch_shapes=near_scratch(OUTER + 1),
            compiler_params=params,
        )(place, first_strip, strip, second_strip, lhs, inner)
    with jax.named_scope("far"):
        potential = pl.pallas_call(
            far_kernel,
            out_shape=shape((ROWS, LANES), f32),
            in_specs=[smem()] + [vmem()] * 9,
            out_specs=vmem(),
            scratch_shapes=[pltpu.VMEM((ROWS, LANES), f32)],
            compiler_params=params,
        )(far_count, place, first_strip, strip, second_strip, tops, far_pairs, near, order, target_basis)
    return potential.reshape(-1)


def solution(mesh):
    both = ("wide", "narrow")
    split = P(None, both)
    return jax.shard_map(
        local,
        mesh=mesh,
        in_specs=(
            split,
            P(both),
            P(both),
            split,
            split,
            split,
            split,
            P(None, "wide"),
            split,
            P(both),
            split,
            P(both),
        ),
        out_specs=P(both),
        check_vma=False,
    )
```

```python
import jax
import jax.numpy as jnp
from jax import lax
from jax.experimental import pallas as pl
from jax.experimental.pallas import tpu as pltpu
from jax.sharding import PartitionSpec as P

C = 256
R = 32
LANES = 128
CLUSTERS = 16
ROWS = 32
NARROW = 8
GROUP = 128
WIDTH = 8
STRIP_CLUSTERS = 32
PAIR_ROW = 8 * STRIP_CLUSTERS
SKEL_ROW = PAIR_ROW + 8
STRIP_ROWS = SKEL_ROW + GROUP
SKEL_REC = 24
TOP_ROWS = 2
OUTER = 2 * STRIP_CLUSTERS
SELF = STRIP_CLUSTERS + 1
DEPTH = 48
UNROLL = 8
SUMS = 2
CHUNK = 64

soft_square = 0.01
kernel_scale = 0.07957747154594767
f32 = jnp.float32
bf16 = jnp.bfloat16
i32 = jnp.int32


def iota(shape, dim):
    return lax.broadcasted_iota(i32, shape, dim)


def split3(x):
    high = x.astype(bf16)
    rest = x - high.astype(f32)
    mid = rest.astype(bf16)
    low = (rest - mid.astype(f32)).astype(bf16)
    return high, mid, low


def parts_dot(x, ones, dims):
    dots = [
        lax.dot_general(part, ones, (dims, ((), ())), preferred_element_type=f32)
        for part in split3(x)
    ]
    return dots[0] + dots[1] + dots[2]


def as_bf16(mask):
    return mask.astype(f32).astype(bf16)


def slots_kernel(near_count, *refs):
    count = 8
    own, skel_out = refs[count : count + 2]
    held = refs[count + 2 : 2 * count + 2]
    semaphores = refs[2 * count + 2]
    copies = [
        pltpu.make_async_copy(refs[i], held[i], semaphores.at[i]) for i in range(count)
    ]
    for copy in copies:
        copy.start()
    order, points, charges, near_pairs = held[:4]
    source_basis, transfer, skeleton_points, top_points = held[4:]
    for copy in copies[:4]:
        copy.wait()
    low = order[...] & (LANES - 1)
    high = order[...] >> 7
    sub = iota((8, LANES), 0)
    tables = []
    for row in range(ROWS):
        xyz = points[:, row * LANES : (row + 1) * LANES]
        charge = charges[row : row + 1, :]
        tables.append(jnp.concatenate([xyz, charge, xyz, charge], axis=0))
    tiles = []
    for tile in range(CLUSTERS):
        first = 4 * (tile // 2) + tile % 2
        low_tile = jnp.where(sub < 4, low[first : first + 1], low[first + 2 : first + 3])
        high_tile = jnp.where(sub < 4, high[first : first + 1], high[first + 2 : first + 3])
        values = jnp.zeros((8, LANES), f32)
        for row in range(ROWS):
            found = jnp.take_along_axis(tables[row], low_tile, axis=1)
            values = jnp.where(high_tile == row, found, values)
        own[8 * tile : 8 * tile + 8, :] = values
        tiles.append(values)

    pairs = jnp.where(iota((2, 64), 1) < near_count[0], near_pairs[...] + 1, 0).astype(f32)
    own[128:136, :] = jnp.zeros((8, LANES), f32)
    own[128:130, 0:64] = pairs
    for copy in copies[4:]:
        copy.wait()

    lane = iota((R, LANES), 1)
    skel = jnp.zeros((R, LANES), f32)
    for cluster in range(CLUSTERS):
        block, place = cluster // 2, 4 * (cluster % 2) + 3
        basis = source_basis[:, cluster * C : (cluster + 1) * C]
        product = (
            basis[:, :LANES] * tiles[2 * block][place : place + 1]
            + basis[:, LANES:] * tiles[2 * block + 1][place : place + 1]
        )
        skel = jnp.where(lane == cluster, jnp.sum(product, axis=1, keepdims=True), skel)
    skel_rows = skel.T[:CLUSTERS, :]
    long_lane = iota((R, CLUSTERS * R), 1)
    repeat = as_bf16(long_lane % R == iota((R, CLUSTERS * R), 0))
    tiled = parts_dot(skel_rows, repeat, ((1,), (0,)))
    mine = iota((CLUSTERS, CLUSTERS * R), 1) // R == iota((CLUSTERS, CLUSTERS * R), 0)
    flat = jnp.sum(jnp.where(mine, tiled, 0.0), axis=0, keepdims=True)
    partial = jnp.sum(transfer[...] * flat, axis=1, keepdims=True)
    skel = jnp.where(lane == CLUSTERS, partial, skel)
    to_charge = as_bf16(lane == iota((R, LANES), 0) + 3 * R)
    record = parts_dot(skel.T[:SKEL_REC, :], to_charge, ((1,), (0,)))
    fold = as_bf16(iota((CLUSTERS * R, LANES), 1) % R == iota((CLUSTERS * R, LANES), 0) % R)
    short_lane = iota((CLUSTERS, LANES), 1) // R
    geometry = jnp.zeros((CLUSTERS, LANES), f32)
    for axis in range(3):
        masked = jnp.where(mine, skeleton_points[axis : axis + 1, :], 0.0)
        folded = parts_dot(masked, fold, ((1,), (0,)))
        geometry = jnp.where(short_lane == axis, folded, geometry)
    spread = as_bf16(lane % R == iota((R, LANES), 0))
    top = parts_dot(top_points[...], spread, ((1,), (0,)))
    top_mine = iota((3, LANES), 1) // R == iota((3, LANES), 0)
    top_row = jnp.sum(jnp.where(top_mine, top, 0.0), axis=0, keepdims=True)
    last = jnp.where(iota((8, LANES), 0) == 1, top_row, 0.0)
    record = record + jnp.concatenate([geometry, last], axis=0)
    for device in range(NARROW):
        skel_out[device] = record


def top_kernel(skels, top_message):
    last = skels[0, CLUSTERS:SKEL_REC, :]
    row = last[0:1] + last[1:2]
    for device in range(1, NARROW):
        row = row + skels[device, CLUSTERS:SKEL_REC, :][0:1]
    top_message[...] = jnp.broadcast_to(row, top_message.shape)


def strip_kernel(place, skels, chip_own, own, next_own, top_message, strip):
    del top_message
    odd = (place[0:1, 1:2] & 1) == 1
    strip[0:64, :] = jnp.where(odd, chip_own[64:128, :], next_own[64:128, :])
    strip[64:192, :] = own[0:128, :]
    strip[192:256, :] = jnp.where(odd, next_own[0:64, :], chip_own[0:64, :])
    pairs = [ref[128:130, :] for ref in (chip_own, own, next_own)]
    pairs.append(jnp.zeros((2, LANES), f32))
    strip[PAIR_ROW : PAIR_ROW + 8, :] = jnp.concatenate(pairs, axis=0)
    for device in range(NARROW):
        start = SKEL_ROW + device * CLUSTERS
        strip[start : start + CLUSTERS, :] = skels[device, :CLUSTERS, :]


def with_norms(halves, origin):
    out = []
    for half in halves:
        sub = iota((8, LANES), 0)
        shifted = jnp.where(sub < 3, half - origin, 0.0)
        norms = jnp.sum(shifted * shifted, axis=0, keepdims=True)
        out.append((shifted, norms))
    return out


def source_features(halves, origin):
    sub = iota((8, LANES), 0)
    columns = []
    for shifted, norms in with_norms(halves, origin):
        rows = jnp.where(sub < 3, shifted, jnp.where(sub == 4, norms, 0.0))
        rows = jnp.where(sub == 5, 1.0, rows)
        high, mid, low = [part.astype(f32) for part in split3(rows)]
        columns.append(jnp.concatenate([high, mid, high, mid, low, high], axis=0).astype(bf16))
    return jnp.concatenate(columns, axis=1)


def target_features(halves, origin):
    sub = iota((8, LANES), 0)
    columns = []
    for shifted, norms in with_norms(halves, origin):
        rows = jnp.where(sub < 3, -2.0 * shifted, jnp.where(sub == 5, norms + soft_square, 0.0))
        rows = jnp.where(sub == 4, 1.0, rows)
        high, mid, low = [part.astype(f32) for part in split3(rows)]
        columns.append(jnp.concatenate([high, high, mid, mid, high, low], axis=0))
    return columns


def cluster_halves(ref, block, odd):
    halves = []
    for half in range(2):
        tile = ref[pl.ds(pl.multiple_of(16 * block + 8 * half, 8), 8), :]
        halves.append(pltpu.roll(tile, 4, 0) if odd else tile)
    return halves


def own_origin(ref, start):
    whole = jnp.zeros((8, LANES), f32)
    for tile in range(CLUSTERS):
        whole = whole + ref[start + 8 * tile : start + 8 * tile + 8, :]
    mean = jnp.sum(whole, axis=1, keepdims=True) * (1.0 / (CLUSTERS * C))
    mean = jnp.broadcast_to(mean, (8, LANES))
    return jnp.where(iota((8, LANES), 0) < 3, mean + pltpu.roll(mean, 4, 0), 0.0)


def kernel_sums(square, charge_low, charge_high):
    inverse = lax.rsqrt(jnp.maximum(square, soft_square))
    return inverse[:, :LANES] * charge_low + inverse[:, LANES:] * charge_high


def put_source(features, charge, slot, halves, origin):
    features[slot] = source_features(halves, origin)
    for half in range(2):
        row = halves[half][3:4]
        charge[slot, :, half * LANES : (half + 1) * LANES] = jnp.broadcast_to(row, (8, LANES))


def pair_rows(refs):
    targets, sources = [], []
    for ref in refs:
        for block in range(3):
            start = PAIR_ROW + 2 * block
            targets.append(ref[start : start + 1, :])
            sources.append(ref[start + 1 : start + 2, :])
    return targets, sources


def list_entries(place, own_rows, other_rows, inner, out):
    wide_index = place[0:1, 0:1].astype(f32)
    narrow_index = place[0:1, 1:2].astype(f32)
    count_rows = len(own_rows)
    base = wide_index * GROUP + narrow_index * CLUSTERS + 1.0
    nothing = [jnp.zeros((16 - count_rows, LANES), f32)]
    own_ids = jnp.concatenate(own_rows + nothing, axis=0)
    other_ids = jnp.concatenate(other_rows + nothing, axis=0)
    local = own_ids - base
    other = other_ids - 1.0
    group = jnp.floor(other * (1.0 / GROUP))
    rest = other - GROUP * group
    depth = jnp.floor(rest * (1.0 / WIDTH))
    column = rest - WIDTH * depth
    group_step = group - (wide_index - 1.0)
    depth_step = depth - (2.0 * narrow_index - 1.0)
    slot = depth_step * WIDTH + column
    if inner:
        wanted = group_step == 1.0
    else:
        wanted = group_step != 1.0
        odd = wide_index - 2.0 * jnp.floor(0.5 * wide_index)
        second = jnp.where(group_step > 1.0, 1.0 - odd, odd)
        slot = slot + STRIP_CLUSTERS * second
    used = wanted & (local >= 0.0) & (local < CLUSTERS) & (own_ids > 0.0)
    count = used.astype(f32)
    upto = as_bf16(iota((LANES, LANES), 0) <= iota((LANES, LANES), 1))
    inclusive = jnp.dot(count.astype(bf16), upto, preferred_element_type=f32)
    totals = jnp.sum(count, axis=1, keepdims=True)
    row_of = iota((16, LANES), 0)
    offset = jnp.zeros((16, LANES), f32)
    for row in range(count_rows):
        offset = jnp.where(row_of > row, offset + totals[row : row + 1], offset)
    spot = jnp.where(used, inclusive - count + offset, -1.0)
    slot = jnp.where(used, slot, 0.0)
    local = jnp.where(used, local, 0.0)
    spot_high = jnp.floor(spot * (1.0 / LANES))
    spot_low = spot - LANES * spot_high
    listed = jnp.zeros((16, LANES), f32)
    eight = iota((8, LANES), 0).astype(f32)
    tall = iota((LANES, LANES), 0).astype(f32)
    for row in range(count_rows):
        here = eight == spot_high[row : row + 1]
        values = jnp.concatenate(
            [
                jnp.where(here, local[row : row + 1], 0.0),
                jnp.where(here, slot[row : row + 1], 0.0),
            ],
            axis=0,
        ).astype(bf16)
        hot = as_bf16(tall == spot_low[row : row + 1])
        listed = listed + lax.dot_general(
            values, hot, (((1,), (1,)), ((), ())), preferred_element_type=f32
        )
    coded = listed[:8] * float(GROUP) + listed[8:]
    out[...] = jnp.where(eight == 7.0, jnp.sum(totals), coded).astype(i32)


def add_pairs(entries, lhs, features, charge, dummy, sums):
    pair_total = entries[7, 0]

    def pair_steps(first, turns, carry):
        for turn in range(turns):
            index = first + turn
            code = entries[index >> 7, index & (LANES - 1)]
            live = index < pair_total
            cluster = jnp.where(live, code >> 7, 0)
            slot = jnp.where(live, code & (LANES - 1), dummy)
            right = features[slot]
            charge_low = charge[slot, 0:1, 0:LANES]
            charge_high = charge[slot, 0:1, LANES:C]
            for start in range(0, C, CHUNK):
                square = jnp.dot(
                    lhs[cluster, start : start + CHUNK, :], right, preferred_element_type=f32
                )
                sums[turn % SUMS][cluster, start : start + CHUNK, :] += kernel_sums(
                    square, charge_low, charge_high
                )
        return carry

    steps = (pair_total + UNROLL - 1) // UNROLL
    lax.fori_loop(
        0, steps // 2, lambda step, carry: pair_steps(2 * UNROLL * step, 2 * UNROLL, carry), 0
    )
    lax.fori_loop(
        2 * (steps // 2), steps, lambda step, carry: pair_steps(UNROLL * step, UNROLL, carry), 0
    )


def summed_row(sums, cluster, half):
    rows = slice(half * LANES, (half + 1) * LANES)
    total = sums[0][cluster, rows, :] + sums[1][cluster, rows, :]
    return kernel_scale * jnp.sum(total.T, axis=0, keepdims=True)


def inner_kernel(
    place, strip, lhs, near, features, charge, listed, entries, semaphore, *rest
):
    first_sum, second_sum, own_lhs = rest
    targets, sources = pair_rows((strip,))
    list_entries(place, sources + [targets[1]], targets + [sources[1]], True, listed)
    copy = pltpu.make_async_copy(listed, entries, semaphore)
    copy.start()
    origin = own_origin(strip, 64)

    def own_step(block, carry):
        for odd in range(2):
            cluster = 2 * block + odd
            halves = cluster_halves(strip, block + 4, odd)
            for half, column in enumerate(target_features(halves, origin)):
                lhs[cluster, half * LANES : (half + 1) * LANES, :] = column.T.astype(bf16)
            centre = jnp.sum(halves[0] + halves[1], axis=1, keepdims=True) * (1.0 / C)
            for half, column in enumerate(target_features(halves, centre)):
                own_lhs[cluster, :, half * LANES : (half + 1) * LANES] = column.astype(bf16)
            put_source(features, charge, SELF + cluster, halves, centre)
        return carry

    lax.fori_loop(0, CLUSTERS // 2, own_step, 0, unroll=8)

    def strip_step(block, carry):
        for odd in range(2):
            put_source(features, charge, 2 * block + odd, cluster_halves(strip, block, odd), origin)
        return carry

    lax.fori_loop(0, STRIP_CLUSTERS // 2, strip_step, 0, unroll=8)
    features[STRIP_CLUSTERS] = jnp.zeros((DEPTH, C), bf16)
    charge[STRIP_CLUSTERS] = jnp.zeros((8, C), f32)

    def self_step(step, carry):
        for turn in range(UNROLL):
            cluster = step * UNROLL + turn
            square = lax.dot_general(
                own_lhs[cluster],
                features[SELF + cluster],
                (((0,), (0,)), ((), ())),
                preferred_element_type=f32,
            )
            first_sum[cluster] = kernel_sums(
                square,
                charge[SELF + cluster, 0:1, 0:LANES],
                charge[SELF + cluster, 0:1, LANES:C],
            )
            second_sum[cluster] = jnp.zeros((C, LANES), f32)
        return carry

    lax.fori_loop(0, CLUSTERS // UNROLL, self_step, 0, unroll=2)
    copy.wait()
    add_pairs(entries, lhs, features, charge, STRIP_CLUSTERS, (first_sum, second_sum))
    for cluster in range(CLUSTERS):
        for half in range(2):
            row = 2 * cluster + half
            near[row : row + 1, :] = summed_row((first_sum, second_sum), cluster, half)


def outer_kernel(
    place,
    second_strip,
    strip,
    first_strip,
    lhs,
    inner,
    near,
    features,
    charge,
    listed,
    entries,
    semaphore,
    *sums,
):
    targets, sources = pair_rows((first_strip, second_strip))
    own_targets, own_sources = pair_rows((strip,))
    list_entries(
        place, sources + [own_targets[1]], targets + [own_sources[1]], False, listed
    )
    copy = pltpu.make_async_copy(listed, entries, semaphore)
    copy.start()
    for total in sums:
        total[...] = jnp.zeros(total.shape, f32)
    origin = own_origin(strip, 64)

    def window_step(block, carry):
        for part, ref in enumerate((first_strip, second_strip)):
            for odd in range(2):
                slot = part * STRIP_CLUSTERS + 2 * block + odd
                put_source(features, charge, slot, cluster_halves(ref, block, odd), origin)
        return carry

    lax.fori_loop(0, STRIP_CLUSTERS // 2, window_step, 0, unroll=4)
    features[OUTER] = jnp.zeros((DEPTH, C), bf16)
    charge[OUTER] = jnp.zeros((8, C), f32)
    copy.wait()
    add_pairs(entries, lhs, features, charge, OUTER, sums)
    for cluster in range(CLUSTERS):
        for half in range(2):
            row = 2 * cluster + half
            near[row : row + 1, :] = inner[row : row + 1, :] + summed_row(sums, cluster, half)


def far_kernel(
    far_count,
    place,
    first_strip,
    strip,
    second_strip,
    top,
    far_pairs,
    near,
    order,
    target_basis,
    potential,
    total,
):
    group_first = place[0:1, 0:1] * GROUP
    target = far_pairs[0:1, :] - group_first
    source = far_pairs[1:2, :]
    is_leaf = far_pairs[2:3, :] == 0
    live = iota((1, LANES), 1) < far_count[0]
    sign = 1 - 2 * (place[0:1, 0:1] & 1)
    offset = source - group_first
    leaf = (1 + sign * (offset >> 7)) * GROUP + (offset & (GROUP - 1))
    index = jnp.where(is_leaf, leaf, source + 3 * GROUP)
    skel = slice(SKEL_ROW, SKEL_ROW + GROUP)
    tops = top[pl.ds(0, top.shape[0] // TOP_ROWS, stride=TOP_ROWS), :]
    table = jnp.concatenate([first_strip[skel, :], strip[skel, :], second_strip[skel, :], tops], axis=0)
    chosen = as_bf16(iota((table.shape[0], LANES), 0) == index)
    over_rows = ((0,), (0,))
    sources = parts_dot(table, chosen, over_rows)
    own_chosen = as_bf16(iota((GROUP, LANES), 0) == target)
    targets = parts_dot(strip[skel, :], own_chosen, over_rows)
    target = target - place[0:1, 1:2] * CLUSTERS
    rows = []
    for a in range(R):
        square = soft_square
        for axis in range(3):
            offset = sources[axis * R : (axis + 1) * R] - targets[axis * R + a : axis * R + a + 1]
            square = square + offset * offset
        product = lax.rsqrt(square) * sources[3 * R :]
        rows.append(jnp.sum(product, axis=0, keepdims=True))
    middle = jnp.where(live, jnp.concatenate(rows, axis=0) * kernel_scale, 0.0)
    for cluster in range(CLUSTERS):
        column = jnp.sum(jnp.where(target == cluster, middle, 0.0), axis=1, keepdims=True)
        spread = jnp.sum(
            target_basis[:, cluster * C : (cluster + 1) * C] * column, axis=0, keepdims=True
        )
        for half in range(2):
            row = 2 * cluster + half
            total[row : row + 1, :] = (
                near[row : row + 1, :] + spread[:, half * LANES : (half + 1) * LANES]
            )
    low = order[...] & (LANES - 1)
    high = order[...] >> 7
    tall = iota((LANES, LANES), 0)
    wide = iota((ROWS, LANES), 0)
    whole = [part.astype(f32) for part in split3(total[...])]
    values, places = [], []
    for row in range(ROWS):
        here = wide == high[row : row + 1]
        parts = [jnp.where(here, part[row : row + 1, :], 0.0) for part in whole]
        values.append(jnp.concatenate(parts, axis=0).astype(bf16))
        places.append(as_bf16(tall == low[row : row + 1]))
    placed = lax.dot_general(
        jnp.concatenate(values, axis=1),
        jnp.concatenate(places, axis=1),
        (((1,), (1,)), ((), ())),
        preferred_element_type=f32,
    )
    out = placed[:ROWS] + placed[ROWS : 2 * ROWS] + placed[2 * ROWS :]
    potential[...] = out


def smem():
    return pl.BlockSpec(memory_space=pltpu.SMEM)


def in_hbm():
    return pl.BlockSpec(memory_space=pltpu.HBM)


def vmem():
    return pl.BlockSpec(memory_space=pltpu.VMEM)


params = pltpu.CompilerParams(vmem_limit_bytes=50 * 1024 * 1024)
first_params = pltpu.CompilerParams(vmem_limit_bytes=127 * 512 * 1024)


def local(
    points,
    charges,
    order,
    source_basis,
    target_basis,
    skeleton_points,
    transfer,
    top_points,
    near_pairs,
    near_count,
    far_pairs,
    far_count,
):
    wide_size = lax.axis_size("wide")
    narrow_size = lax.axis_size("narrow")
    place = jnp.stack([lax.axis_index("wide"), lax.axis_index("narrow")]).astype(i32).reshape(1, 2)
    order = order.reshape(ROWS, LANES)
    shape = jax.ShapeDtypeStruct
    inputs = (
        order,
        points,
        charges.reshape(ROWS, LANES),
        near_pairs,
        source_basis,
        transfer,
        skeleton_points,
        top_points,
    )
    with jax.named_scope("slots"):
        own, skel = pl.pallas_call(
            slots_kernel,
            out_shape=(
                shape((136, LANES), f32),
                shape((NARROW, SKEL_REC, LANES), f32),
            ),
            in_specs=[smem()] + [in_hbm()] * len(inputs),
            out_specs=[vmem()] * 2,
            scratch_shapes=[pltpu.VMEM(x.shape, x.dtype) for x in inputs]
            + [pltpu.SemaphoreType.DMA((len(inputs),))],
            compiler_params=first_params,
        )(near_count, *inputs)
    skels = lax.all_to_all(skel, "narrow", 0, 0, tiled=True)
    in_chip = [(i, i + 1) for i in range(0, narrow_size - 1, 2)]
    next_chip = [(i, i + 1) for i in range(1, narrow_size - 1, 2)]
    chip_own = lax.ppermute(own, "narrow", in_chip + [(j, i) for i, j in in_chip])
    next_own = lax.ppermute(own, "narrow", next_chip + [(j, i) for i, j in next_chip])
    with jax.named_scope("top"):
        top_message = pl.pallas_call(
            top_kernel,
            out_shape=shape((TOP_ROWS * wide_size, LANES), f32),
            in_specs=[vmem()],
            out_specs=vmem(),
            compiler_params=params,
        )(skels)
    tops = lax.all_to_all(top_message, "wide", 0, 0, tiled=True)
    with jax.named_scope("strip"):
        strip = pl.pallas_call(
            strip_kernel,
            out_shape=shape((STRIP_ROWS, LANES), f32),
            in_specs=[vmem()] * 6,
            out_specs=vmem(),
            compiler_params=params,
        )(place, skels, chip_own, own, next_own, top_message)
    odd_even = [(i, i + 1) for i in range(1, wide_size - 1, 2)]
    even_odd = [(i, i + 1) for i in range(0, wide_size - 1, 2)]
    first_strip = lax.ppermute(strip, "wide", odd_even + [(j, i) for i, j in odd_even])
    second_strip = lax.ppermute(strip, "wide", even_odd + [(j, i) for i, j in even_odd])
    def near_scratch(slots):
        return [
            pltpu.VMEM((slots, DEPTH, C), bf16),
            pltpu.VMEM((slots, 8, C), f32),
            pltpu.VMEM((8, LANES), i32),
            pltpu.SMEM((8, LANES), i32),
            pltpu.SemaphoreType.DMA(()),
        ] + [pltpu.VMEM((CLUSTERS, C, LANES), f32)] * SUMS

    with jax.named_scope("inner"):
        lhs, inner = pl.pallas_call(
            inner_kernel,
            out_shape=(shape((CLUSTERS, C, DEPTH), bf16), shape((ROWS, LANES), f32)),
            in_specs=[vmem()] * 2,
            out_specs=[vmem()] * 2,
            scratch_shapes=near_scratch(SELF + CLUSTERS)
            + [pltpu.VMEM((CLUSTERS, DEPTH, C), bf16)],
            compiler_params=params,
        )(place, strip)
    with jax.named_scope("outer"):
        near = pl.pallas_call(
            outer_kernel,
            out_shape=shape((ROWS, LANES), f32),
            in_specs=[vmem()] * 6,
            out_specs=vmem(),
            scratch_shapes=near_scratch(OUTER + 1),
            compiler_params=params,
        )(place, second_strip, strip, first_strip, lhs, inner)
    with jax.named_scope("far"):
        potential = pl.pallas_call(
            far_kernel,
            out_shape=shape((ROWS, LANES), f32),
            in_specs=[smem()] + [vmem()] * 9,
            out_specs=vmem(),
            scratch_shapes=[pltpu.VMEM((ROWS, LANES), f32)],
            compiler_params=params,
        )(far_count, place, first_strip, strip, second_strip, tops, far_pairs, near, order, target_basis)
    return potential.reshape(-1)


def solution(mesh):
    both = ("wide", "narrow")
    split = P(None, both)
    return jax.shard_map(
        local,
        mesh=mesh,
        in_specs=(
            split,
            P(both),
            P(both),
            split,
            split,
            split,
            split,
            P(None, "wide"),
            split,
            P(both),
            split,
            P(both),
        ),
        out_specs=P(both),
        check_vma=False,
    )
```
